32 devices in a mesh: ctx: 8 (over z, x), head: 4 (over y, core).
Axes of the slice: x: 2, y: 2, z: 4, core: 2. Of those that a mesh axis runs over, the one named last changes fastest.
Arguments:
- queries: bfloat16 [8192, 5120], P('ctx', 'head'), may hold values from -60 to 60
- key_rows: bfloat16 [8192, 5120], P('ctx', 'head'), may hold values from -10 to 10
- value_rows: bfloat16 [8192, 5120], P('ctx', 'head'), may hold values from -60 to 60
- norm_gain: float32 [5120], P('head'), may hold values from 0.1 to 1.9
- sort_index: int32 [32], replicated, may hold values from 0 to 31
- grad_normed: bfloat16 [8192, 5120], P('ctx', 'head'), may hold values from -6 to 6
Outputs:
- normed: bfloat16 [8192, 5120], P('ctx', 'head')
- grad_queries: bfloat16 [8192, 5120], P('ctx', 'head')
- grad_keys: bfloat16 [8192, 5120], P('ctx', 'head')
- grad_values: bfloat16 [8192, 5120], P('ctx', 'head')
The draws below stay inside these ranges and needn't reach their ends.
Inputs may be any that keep to these rules, and one draw needn't show every extreme that they name: `sort_index`: several query blocks may name the same block.
All inputs are finite; a program needn't handle non-finite values.
Results may differ from the reference program's by a relative error of at most 0.009.
Values may be sent and summed in bfloat16 or wider, within the bound.
No kernel may reach another device: no remote copies, remote signals or barrier semaphores. Data moves between devices by JAX's collectives and lax.ppermute only.
A program may use at most 128 MiB of HBM per device.

```python
import math
import jax
import jax.numpy as jnp
import numpy as np
from jax import lax

HEADS = 40
HDIM = 128
BLOCK = 256
NBLK = 32
SEQ = 8192
WIDTH = 5120


def drawn_parts(key):
    base = jax.random.normal(jax.random.fold_in(key, 11), (SEQ, WIDTH), jnp.float32)
    return base


def draw_queries(key, part):
    private = jnp.clip(jax.random.normal(jax.random.fold_in(key, 14), (SEQ, WIDTH), jnp.float32), -6.0, 6.0)
    return private.astype(jnp.bfloat16)


def draw_key_rows(key, part):
    base = drawn_parts(key)
    drawn = jnp.clip(base, -6.0, 6.0)
    return drawn.astype(jnp.bfloat16)


def draw_value_rows(key, part):
    column = jnp.arange(WIDTH)[None, :] // HDIM
    share = column.astype(jnp.float32) / max(HEADS - 1, 1)
    level = jax.random.uniform(jax.random.fold_in(key, 22), (SEQ, 1), jnp.float32)
    noise = jax.random.normal(jax.random.fold_in(key, 21), (SEQ, WIDTH), jnp.float32)
    factor = 10.0 ** (0.5 * share) * 10.0 ** (0.5 * level)
    return jnp.clip(noise * factor, -60.0, 60.0).astype(jnp.bfloat16)


def touch_ends(array, stream_key, smallest, high):
    longest = array.shape.index(max(array.shape))
    spots = []
    for shift in (0, 1):
        where = [jax.random.randint(jax.random.fold_in(stream_key, axis), (), 0, length) for axis, length in enumerate(array.shape)]
        where[longest] = (where[longest] + shift) % array.shape[longest]
        spots.append(tuple(where))
    return array.at[spots[0]].set(smallest).at[spots[1]].set(high)


def block_levels(own_key, dims, pieces, low, largest):
    def one(dim, shards_of):
        heights = jax.random.uniform(jax.random.fold_in(jax.random.fold_in(own_key, 6), dim), (shards_of,), jnp.float32, low / len(pieces), largest / len(pieces))
        return jnp.repeat(jnp.exp(heights), dims[dim] // shards_of).reshape((-1,) + (1,) * (len(dims) - dim - 1))

    factor_of = one(*pieces[0])
    for cut in pieces[1:]:
        factor_of = factor_of * one(*cut)
    return factor_of


def cumulative_ranks(number_of, slope):
    weights = [(1 << 20) // math.isqrt(rank ** slope) + 1 for rank in range(1, number_of + 1)]
    deviation = 1 + sum(weights) // (1 << 30)
    return np.cumsum(np.array([max(1, weight // deviation) for weight in weights]))


def ranked_ids(stream_key, shape, count, slope):
    listing = cumulative_ranks(count, slope)
    lot = jax.random.randint(jax.random.fold_in(stream_key, 1), shape, 0, int(listing[count - 1]))
    rank = jnp.searchsorted(jnp.asarray(listing, jnp.int32), lot, side="right")
    return jax.random.permutation(jax.random.fold_in(stream_key, 2), count)[rank].astype(jnp.int32)


def scatter_about(rng, extent, deviation, reach, shards=(), kind=jnp.bfloat16):
    level = block_levels(rng, extent, shards, -0.22, 0.18) if shards else 1.0
    values = jax.random.normal(rng, extent, jnp.float32) * deviation * level
    return jnp.minimum(jnp.maximum(values, -reach), reach).astype(kind)


def setup_inputs(seed: int = 0) -> dict:
    streams_of = jax.random.split(jax.random.key(seed), 7)
    queries = draw_queries(jax.random.fold_in(streams_of[6], 71), 0)
    key_rows = draw_key_rows(jax.random.fold_in(streams_of[6], 71), 0)
    value_rows = draw_value_rows(jax.random.fold_in(streams_of[6], 71), 0)
    norm_gain = jnp.clip(1.0 + 0.18 * jax.random.normal(streams_of[3], (WIDTH,), jnp.float32), 0.1, 1.9)
    sort_index = touch_ends(ranked_ids(streams_of[4], (NBLK,), NBLK, 2), jax.random.fold_in(streams_of[4], 3), 0, NBLK - 1).astype(jnp.int32)
    grad_normed = scatter_about(streams_of[5], (SEQ, WIDTH), 1.0, 6.0, ((0, 8), (1, 4)))
    return dict(queries=queries, key_rows=key_rows, value_rows=value_rows, norm_gain=norm_gain, sort_index=sort_index, grad_normed=grad_normed)


def allowed_keys(block_id):
    query_pos = jnp.arange(BLOCK)[:, None]
    key_pos = jnp.arange(BLOCK)[None, :]
    causal = key_pos <= query_pos
    before = jnp.broadcast_to(block_id > 0, (BLOCK, BLOCK))
    chosen = jnp.ones((BLOCK, BLOCK), dtype=jnp.bool_)
    return jnp.concatenate([causal, before, chosen], axis=1)

def probabilities(query_block, key_set, allowed):
    head_count = query_block.shape[1] // HDIM
    q_split = query_block.reshape(BLOCK, head_count, HDIM).astype(jnp.float32)
    k_split = key_set.reshape(3 * BLOCK, head_count, HDIM).astype(jnp.float32)
    scores = jnp.einsum('qhd,khd->hqk', q_split, k_split) * HDIM ** (-0.5)
    scores = jnp.where(allowed[None], scores, -jnp.inf)
    highest = lax.optimization_barrier(jnp.max(scores, axis=2, keepdims=True))
    weights = jnp.exp(scores - highest)
    return weights / lax.optimization_barrier(jnp.sum(weights, axis=2, keepdims=True))

def reference(queries, key_rows, value_rows, norm_gain, sort_index, grad_normed):
    q_blocks = queries.reshape(NBLK, BLOCK, WIDTH)
    k_blocks = key_rows.reshape(NBLK, BLOCK, WIDTH)
    v_blocks = value_rows.reshape(NBLK, BLOCK, WIDTH)
    block_ids = jnp.arange(NBLK, dtype=jnp.int32)
    before_ids = jnp.maximum(block_ids - 1, 0).astype(jnp.int32)

    def gather_set(blocks, index):
        return jnp.concatenate([blocks[index], blocks[before_ids[index]], blocks[sort_index[index]]], axis=0)

    def forward(index):
        key_set = gather_set(k_blocks, index)
        value_set = gather_set(v_blocks, index)
        probs = probabilities(q_blocks[index], key_set, allowed_keys(index))
        probs_low = probs.astype(jnp.bfloat16).astype(jnp.float32)
        v_split = value_set.reshape(3 * BLOCK, HEADS, HDIM).astype(jnp.float32)
        result = jnp.einsum('hqk,khd->qhd', probs_low, v_split)
        return result.reshape(BLOCK, WIDTH)
    attended = lax.map(forward, block_ids).reshape(SEQ, WIDTH)
    inv_rms = lax.rsqrt(lax.optimization_barrier(jnp.mean(attended * attended, axis=1, keepdims=True)) + 1e-05)
    normed = (attended * inv_rms * norm_gain).astype(jnp.bfloat16)
    lifted = norm_gain * grad_normed.astype(jnp.float32)
    center = lax.optimization_barrier(jnp.sum(lifted * attended, axis=1, keepdims=True))
    grad_attended = (inv_rms * lifted - attended * inv_rms ** 3 * center / WIDTH).astype(jnp.bfloat16)
    g_blocks = grad_attended.reshape(NBLK, BLOCK, WIDTH)

    def backward(index):
        key_set = gather_set(k_blocks, index)
        value_set = gather_set(v_blocks, index)
        probs = probabilities(q_blocks[index], key_set, allowed_keys(index))
        probs_low = probs.astype(jnp.bfloat16).astype(jnp.float32)
        q_split = q_blocks[index].reshape(BLOCK, HEADS, HDIM).astype(jnp.float32)
        k_split = key_set.reshape(3 * BLOCK, HEADS, HDIM).astype(jnp.float32)
        v_split = value_set.reshape(3 * BLOCK, HEADS, HDIM).astype(jnp.float32)
        d_split = g_blocks[index].reshape(BLOCK, HEADS, HDIM).astype(jnp.float32)
        grad_set_v = jnp.einsum('hqk,qhd->khd', probs_low, d_split).reshape(3 * BLOCK, WIDTH)
        grad_probs = jnp.einsum('qhd,khd->hqk', d_split, v_split)
        row_center = lax.optimization_barrier(jnp.sum(probs * grad_probs, axis=2, keepdims=True))
        grad_scores = (probs * (grad_probs - row_center) * HDIM ** (-0.5)).astype(jnp.bfloat16).astype(jnp.float32)
        grad_q = jnp.einsum('hqk,khd->qhd', grad_scores, k_split).reshape(BLOCK, WIDTH).astype(jnp.bfloat16)
        grad_set_k = jnp.einsum('hqk,qhd->khd', grad_scores, q_split).reshape(3 * BLOCK, WIDTH)
        return (grad_q, grad_set_k[:BLOCK], grad_set_k[BLOCK:].astype(jnp.bfloat16), grad_set_v[:BLOCK], grad_set_v[BLOCK:].astype(jnp.bfloat16))
    grad_q, own_k, far_k, own_v, far_v = lax.map(backward, block_ids)

    def settle(own_part, far_part):
        before_part = far_part[:, :BLOCK].astype(jnp.float32)
        chosen_part = far_part[:, BLOCK:].astype(jnp.float32)
        shifted = jnp.concatenate([before_part[1:], jnp.zeros_like(before_part[:1])], axis=0)
        summed = jax.ops.segment_sum(chosen_part, sort_index, num_segments=NBLK)
        return (own_part + shifted + summed).astype(jnp.bfloat16).reshape(SEQ, WIDTH)
    grad_keys = settle(own_k, far_k)
    grad_values = settle(own_v, far_v)
    return (normed, grad_q.reshape(SEQ, WIDTH), grad_keys, grad_values)
```

```python
import functools
import math

import jax
import jax.numpy as jnp
import numpy as np
from jax import lax
from jax.experimental import pallas as pl
from jax.experimental.pallas import tpu as pltpu
from jax.sharding import PartitionSpec as P

HDIM = 128
BLOCK = 256
WIDTH = 5120
LANES = 128
ROW = 8
STATIC_STEPS = 5
SCALE = HDIM ** (-0.5)
ANY = pl.BlockSpec(memory_space=pl.ANY)
SMEM = pl.BlockSpec(memory_space=pltpu.SMEM)
VMEM = pl.BlockSpec(memory_space=pltpu.VMEM)


def max_steps(ctx_size, blocks):
    return blocks * (ctx_size // 2) + ctx_size // 2 + 2 * blocks + 4


def shift_rows(array, count, rows):
    n = array.shape[0]
    if abs(count) >= n:
        return jnp.zeros_like(array)
    rolled = pltpu.roll(array, (-count) % n, 0)
    inside = (rows < n - count) if count > 0 else (rows >= -count)
    return jnp.where(inside, rolled, 0.0)


def table_kernel(picks_ref, owner_ref, slot_ref, out_ref, *, blocks, steps):
    n = picks_ref.shape[0]
    levels = n // 2
    rows = lax.broadcasted_iota(jnp.int32, (n, LANES), 0)
    lanes = lax.broadcasted_iota(jnp.int32, (n, LANES), 1)
    owner = owner_ref[...]
    slot = slot_ref[...]
    picks = picks_ref[...]
    side = rows & 1
    level = rows >> 1
    owner_side = owner & 1
    owner_level = owner >> 1

    def other(array):
        return jnp.where(side == 0, pltpu.roll(array, n - 1, 0), pltpu.roll(array, 1, 0))

    need = jnp.zeros((n, LANES), jnp.float32)
    for j in range(blocks + 1):
        need = jnp.where(picks[:, j : j + 1] == lanes, 1.0, need)
    need = jnp.where(owner == rows, 0.0, need)
    wanted = jnp.maximum(need, other(need))
    far_up = jnp.zeros_like(need)
    far_down = jnp.zeros_like(need)
    for k in range(1, levels):
        far_up = jnp.where(shift_rows(wanted, 2 * k, rows) > 0, float(k), far_up)
        far_down = jnp.where(shift_rows(wanted, -2 * k, rows) > 0, float(k), far_down)
    travels = side == owner_side
    low = (LANES - 1 - lanes).astype(jnp.float32)
    up = jnp.where(travels & (level >= owner_level) & (far_up > 0), 1.0, 0.0)
    down = jnp.where(travels & (level <= owner_level) & (far_down > 0), 1.0, 0.0)
    over = jnp.where(travels, other(need), 0.0)
    have = jnp.where(owner == rows, 1.0, 0.0)
    first_over = float(blocks * levels)

    out_ref[...] = jnp.full(out_ref.shape, -1, jnp.int32)

    def pick(pending, have, rank):
        score = jnp.where(pending * have > 0, rank, -1.0)
        best = jnp.max(score, axis=1, keepdims=True)
        return jnp.where((score == best) & (best >= 0), 1.0, 0.0)

    def place(chosen):
        return jnp.sum(chosen * (slot + 1.0), axis=1, keepdims=True) - 1.0

    def pending(state):
        t, have, up, down, over, over_slot, count = state
        return (t < steps) & (jnp.sum(up + down + over) > 0)

    def step(state):
        t, have, up, down, over, over_slot, count = state
        send_up = pick(up, have, far_up * LANES + low)
        send_down = pick(down, have, far_down * LANES + low)
        send_over = pick(over, have, low)
        got_up = shift_rows(send_up, -2, rows)
        got_down = shift_rows(send_down, 2, rows)
        got_over = other(send_over)
        any_over = jnp.max(got_over, axis=1, keepdims=True)
        columns = (
            place(send_up),
            place(send_down),
            place(send_over),
            place(got_up),
            place(got_down),
            jnp.where(any_over > 0, count + first_over, -1.0),
        )
        row = jnp.full((n, LANES), -1.0, jnp.float32)
        for k, column in enumerate(columns):
            row = jnp.where(lanes == k, column, row)
        out_ref[t] = row.astype(jnp.int32)
        over_slot = jnp.where(got_over > 0, count + first_over, over_slot)
        have = jnp.maximum(have, jnp.maximum(got_up, jnp.maximum(got_down, got_over)))
        return (
            t + 1,
            have,
            up - send_up,
            down - send_down,
            over - send_over,
            over_slot,
            count + any_over,
        )

    state = (
        jnp.int32(0),
        have,
        up,
        down,
        over,
        jnp.zeros_like(need),
        jnp.zeros((n, 1), jnp.float32),
    )
    state = lax.while_loop(pending, step, state)
    over_slot = state[5]
    slots = jnp.where(travels, slot, over_slot)
    row = jnp.zeros((n, LANES), jnp.float32)
    for j in range(blocks + 1):
        where = jnp.sum(
            jnp.where(picks[:, j : j + 1] == lanes, slots, 0.0), axis=1, keepdims=True
        )
        row = jnp.where(lanes == j, where, row)
    row = jnp.where(lanes == blocks + 1, state[0].astype(jnp.float32), row)
    row = jnp.where(lanes == blocks + 2, (level * blocks).astype(jnp.float32), row)
    out_ref[steps] = row.astype(jnp.int32)


def routing_table(sort_index, ctx_size, blocks):
    steps = max_steps(ctx_size, blocks)
    block_ids = np.arange(LANES)
    owner = np.broadcast_to((block_ids // blocks)[None], (ctx_size, LANES)).astype(np.int32)
    slot = (block_ids // (2 * blocks)) * blocks + block_ids % blocks
    slot = np.broadcast_to(slot[None], (ctx_size, LANES)).astype(np.float32)
    before = (np.arange(ctx_size, dtype=np.int32) * blocks - 1)[:, None]
    picks = jnp.concatenate(
        [sort_index.reshape(ctx_size, blocks), jnp.asarray(before)], axis=1
    )
    picks = jnp.pad(picks, ((0, 0), (0, LANES - blocks - 1)), constant_values=-1)
    table = pl.pallas_call(
        functools.partial(table_kernel, blocks=blocks, steps=steps),
        out_shape=jax.ShapeDtypeStruct((steps + 1, ctx_size, LANES), jnp.int32),
        in_specs=[VMEM] * 3,
        out_specs=VMEM,
        name="routing_table",
    )(picks, jnp.asarray(owner), jnp.asarray(slot))
    mine = lax.dynamic_slice(table, (0, lax.axis_index("ctx"), 0), (steps + 1, 1, ROW))
    return mine.reshape((steps + 1) * ROW), steps


def routes(ctx_size):
    up = [(d, d + 2) for d in range(ctx_size - 2)]
    down = [(d + 2, d) for d in range(ctx_size - 2)]
    over = [(d, d ^ 1) for d in range(ctx_size)]
    return up, down, over


def copy_if(slot, source, target, sem):
    copy = pltpu.make_async_copy(source, target, sem)

    @pl.when(slot >= 0)
    def _():
        copy.start()

    def wait():
        @pl.when(slot >= 0)
        def _():
            copy.wait()

    return wait


def open_kernel(tab_ref, own_ref, pool_ref, up_ref, down_ref, over_ref, sems, *, base_at):
    blocks = own_ref.shape[0]
    base = tab_ref[base_at]
    own = pltpu.make_async_copy(own_ref, pool_ref.at[pl.ds(base, blocks)], sems.at[3])
    own.start()
    waits = []
    for k, out in enumerate((up_ref, down_ref, over_ref)):
        slot = tab_ref[k]
        at = jnp.clip(slot - base, 0, blocks - 1)
        waits.append(copy_if(slot, own_ref.at[at], out, sems.at[k]))
    for wait in waits:
        wait()
    own.wait()


def step_kernel(
    t_ref, tab_ref, pool_in, in_up, in_down, in_over, pool_ref, up_ref, down_ref, over_ref, sems
):
    del pool_in
    t = t_ref[0]
    waits = []
    for k, got in enumerate((in_up, in_down, in_over)):
        slot = tab_ref[(t - 1) * ROW + 3 + k]
        waits.append(copy_if(slot, got, pool_ref.at[jnp.maximum(slot, 0)], sems.at[k]))
    for wait in waits:
        wait()
    waits = []
    for k, out in enumerate((up_ref, down_ref, over_ref)):
        slot = tab_ref[t * ROW + k]
        waits.append(copy_if(slot, pool_ref.at[jnp.maximum(slot, 0)], out, sems.at[3 + k]))
    for wait in waits:
        wait()


def close_kernel(t_ref, tab_ref, pool_in, in_up, in_down, in_over, pool_ref, sems):
    del pool_in
    t = t_ref[0]
    waits = []
    for k, got in enumerate((in_up, in_down, in_over)):
        slot = tab_ref[(t - 1) * ROW + 3 + k]
        waits.append(copy_if(slot, got, pool_ref.at[jnp.maximum(slot, 0)], sems.at[k]))
    for wait in waits:
        wait()


def traffic(byte_count):
    return pl.CostEstimate(flops=0, bytes_accessed=byte_count, transcendentals=0)


def send_all(sends, perms):
    return tuple(lax.ppermute(s, "ctx", p) for s, p in zip(sends, perms))


def gather_blocks(streams, tab, steps, ctx_size):
    blocks = streams[0].shape[0]
    slots = blocks * (ctx_size // 2) + blocks + 1
    perms = routes(ctx_size)
    last_row = steps * ROW
    total = tab[last_row + blocks + 1]

    def shapes(stream):
        one = jax.ShapeDtypeStruct(stream.shape[1:], stream.dtype)
        pool = jax.ShapeDtypeStruct((slots,) + stream.shape[1:], stream.dtype)
        return pool, one

    def size(stream):
        return 2 * math.prod(stream.shape[1:])

    def first(stream):
        pool, one = shapes(stream)
        return pl.pallas_call(
            functools.partial(open_kernel, base_at=last_row + blocks + 2),
            out_shape=(pool, one, one, one),
            in_specs=[SMEM, ANY],
            out_specs=(ANY,) * 4,
            scratch_shapes=[pltpu.SemaphoreType.DMA((4,))],
            cost_estimate=traffic(size(stream) * 14),
            name="gather_open",
        )(tab, stream)

    def later(t, pool, got, stream):
        pool_shape, one = shapes(stream)
        return pl.pallas_call(
            step_kernel,
            out_shape=(pool_shape, one, one, one),
            in_specs=[SMEM, SMEM] + [ANY] * 4,
            out_specs=(ANY,) * 4,
            scratch_shapes=[pltpu.SemaphoreType.DMA((6,))],
            input_output_aliases={2: 0},
            cost_estimate=traffic(size(stream) * 12),
            name="gather_step",
        )(t, tab, pool, *got)

    def close(t, pool, got, stream):
        pool_shape, one = shapes(stream)
        return pl.pallas_call(
            close_kernel,
            out_shape=pool_shape,
            in_specs=[SMEM, SMEM] + [ANY] * 4,
            out_specs=ANY,
            scratch_shapes=[pltpu.SemaphoreType.DMA((3,))],
            input_output_aliases={2: 0},
            cost_estimate=traffic(size(stream) * 6),
            name="gather_close",
        )(t, tab, pool, *got)

    held = []
    for stream in streams:
        pool, *sends = first(stream)
        held.append((pool, send_all(sends, perms)))

    def advance(t, held):
        result = []
        for (pool, got), stream in zip(held, streams):
            pool, *sends = later(t.reshape(1), pool, got, stream)
            result.append((pool, send_all(sends, perms)))
        return result

    for t in range(1, STATIC_STEPS):
        held = advance(jnp.full((1,), t, jnp.int32), held)

    def body(state):
        t, held = state
        return t + 1, advance(t, held)

    t, held = lax.while_loop(
        lambda state: state[0] < total, body, (jnp.int32(STATIC_STEPS), held)
    )
    return [
        close(t.reshape(1), pool, got, stream) for (pool, got), stream in zip(held, streams)
    ]


def init_kernel(slots_ref, own_ref, terms_ref, pool_ref, *, blocks, slot_of):
    s = pl.program_id(0)
    base = slots_ref[0]
    at = s - base
    own = (at >= 0) & (at < blocks)
    own_at = jnp.clip(at, 0, blocks - 1)
    pool_ref[0] = jnp.where(own, own_ref[own_at], 0.0).astype(pool_ref.dtype)
    for k in range(2 * blocks):

        @pl.when(slots_ref[1 + k] == s)
        def _(k=k):
            pool_ref[0] = (
                pool_ref[0].astype(jnp.float32) + terms_ref[k].astype(jnp.float32)
            ).astype(pool_ref.dtype)


def back_kernel(
    t_ref, tab_ref, pool_in, in_up, in_down, in_over, pool_ref, up_ref, down_ref, over_ref,
    held_ref, got_ref, sems,
):
    del pool_in
    t = t_ref[0]
    add_back(t, tab_ref, (in_up, in_down, in_over), pool_ref, held_ref, got_ref, sems)
    waits = []
    for k, out in enumerate((up_ref, down_ref, over_ref)):
        slot = tab_ref[t * ROW + 3 + k]
        waits.append(copy_if(slot, pool_ref.at[jnp.maximum(slot, 0)], out, sems.at[k]))
    for wait in waits:
        wait()


def add_back(t, tab_ref, arrived, pool_ref, held_ref, got_ref, sems):
    for k, got in enumerate(arrived):
        slot = tab_ref[(t + 1) * ROW + k]

        @pl.when(slot >= 0)
        def _(k=k, got=got, slot=slot):
            place = pool_ref.at[jnp.maximum(slot, 0)]
            load = pltpu.make_async_copy(place, held_ref, sems.at[0])
            load_got = pltpu.make_async_copy(got, got_ref, sems.at[1])
            load.start()
            load_got.start()
            load.wait()
            load_got.wait()
            held_ref[...] = (
                held_ref[...].astype(jnp.float32) + got_ref[...].astype(jnp.float32)
            ).astype(held_ref.dtype)
            store = pltpu.make_async_copy(held_ref, place, sems.at[2])
            store.start()
            store.wait()


def finish_kernel(
    tab_ref, pool_in, in_up, in_down, in_over, pool_ref, out_ref, held_ref, got_ref, sems,
    *, base_at,
):
    del pool_in
    add_back(-1, tab_ref, (in_up, in_down, in_over), pool_ref, held_ref, got_ref, sems)
    base = tab_ref[base_at]
    blocks = out_ref.shape[0]
    copy = pltpu.make_async_copy(pool_ref.at[pl.ds(base, blocks)], out_ref, sems.at[0])
    copy.start()
    copy.wait()


def return_blocks(streams, slots_list, tab, steps, ctx_size):
    blocks = streams[0][0].shape[0]
    slots = blocks * (ctx_size // 2) + blocks + 1
    up, down, over = routes(ctx_size)
    perms = ([(b, a) for a, b in up], [(b, a) for a, b in down], over)
    last_row = steps * ROW
    total = tab[last_row + blocks + 1]
    dtype = jnp.bfloat16
    held = []
    for own, far in streams:
        shape = own.shape[1:]
        columns = shape[1] // 2
        pool = pl.pallas_call(
            functools.partial(init_kernel, blocks=blocks, slot_of=None),
            out_shape=jax.ShapeDtypeStruct((slots,) + shape, dtype),
            grid_spec=pltpu.PrefetchScalarGridSpec(
                num_scalar_prefetch=1,
                grid=(slots,),
                in_specs=[VMEM, VMEM],
                out_specs=pl.BlockSpec((1,) + shape, lambda s, ref: (s, 0, 0)),
            ),
            compiler_params=pltpu.CompilerParams(vmem_limit_bytes=48 * 1024 * 1024),
            cost_estimate=traffic(2 * math.prod(shape) * (slots + 3 * blocks)),
            name="return_open",
        )(slots_list, own, far)
        held.append((pool, (jnp.zeros(shape, dtype),) * 3))

    def scratch(one):
        return [
            pltpu.VMEM(one.shape, one.dtype),
            pltpu.VMEM(one.shape, one.dtype),
            pltpu.SemaphoreType.DMA((3,)),
        ]

    def back(t, pool, got):
        one = jax.ShapeDtypeStruct(pool.shape[1:], pool.dtype)
        return pl.pallas_call(
            back_kernel,
            out_shape=(jax.ShapeDtypeStruct(pool.shape, pool.dtype), one, one, one),
            in_specs=[SMEM, SMEM] + [ANY] * 4,
            out_specs=(ANY,) * 4,
            scratch_shapes=scratch(one),
            input_output_aliases={2: 0},
            cost_estimate=traffic(2 * math.prod(one.shape) * 16),
            name="return_step",
        )(t, tab, pool, *got)

    def finish(pool, got):
        one = jax.ShapeDtypeStruct(pool.shape[1:], pool.dtype)
        return pl.pallas_call(
            functools.partial(finish_kernel, base_at=last_row + blocks + 2),
            out_shape=(
                jax.ShapeDtypeStruct(pool.shape, pool.dtype),
                jax.ShapeDtypeStruct((blocks,) + one.shape, one.dtype),
            ),
            in_specs=[SMEM] + [ANY] * 4,
            out_specs=(ANY, ANY),
            scratch_shapes=scratch(one),
            input_output_aliases={1: 0},
            cost_estimate=traffic(2 * math.prod(one.shape) * 16),
            name="return_close",
        )(tab, pool, *got)[1]

    def retreat(t, held):
        result = []
        for pool, got in held:
            pool, *sends = back(t.reshape(1), pool, got)
            result.append((pool, send_all(sends, perms)))
        return result

    def body(state):
        t, held = state
        return t - 1, retreat(t, held)

    _, held = lax.while_loop(
        lambda state: state[0] >= STATIC_STEPS, body, (total - 1, held)
    )
    for t in range(STATIC_STEPS - 1, -1, -1):
        held = retreat(jnp.full((1,), t, jnp.int32), held)
    return [finish(pool, got) for pool, got in held]


QK = (((1,), (1,)), ((), ()))
AB = (((1,), (0,)), ((), ()))
TA = (((0,), (0,)), ((), ()))


def dot(a, b, dims):
    return lax.dot_general(a, b, dims, preferred_element_type=jnp.float32)


def forward_kernel(
    meta_ref, q_ref, ko_ref, kb_ref, ks_ref, vo_ref, vb_ref, vs_ref, gain_ref, grad_ref,
    attended_ref, probs_ref, sums_ref, *, blocks, group,
):
    i = pl.program_id(0)
    h = pl.program_id(1)
    block_id = meta_ref[1 + 2 * blocks] + i
    causal = lax.broadcasted_iota(jnp.int32, (BLOCK, BLOCK), 1) <= lax.broadcasted_iota(
        jnp.int32, (BLOCK, BLOCK), 0
    )
    hide = jnp.where(block_id > 0, 0.0, -jnp.inf).astype(jnp.float32)
    squares = jnp.zeros((BLOCK, 1), jnp.float32)
    center = jnp.zeros((BLOCK, 1), jnp.float32)
    for g in range(group):
        cols = slice(g * HDIM, (g + 1) * HDIM)
        q = q_ref[:, cols]
        s_own = jnp.where(causal, dot(q, ko_ref[0, :, cols], QK) * SCALE, -jnp.inf)
        s_before = dot(q, kb_ref[0, :, cols], QK) * SCALE + hide
        s_sorted = dot(q, ks_ref[0, :, cols], QK) * SCALE
        top = jnp.max(
            jnp.maximum(jnp.maximum(s_own, s_before), s_sorted), axis=1, keepdims=True
        )
        w_own = jnp.exp(s_own - top)
        w_before = jnp.exp(s_before - top)
        w_sorted = jnp.exp(s_sorted - top)
        scale = 1.0 / jnp.sum(w_own + w_before + w_sorted, axis=1, keepdims=True)
        p_own = (w_own * scale).astype(jnp.bfloat16)
        p_before = (w_before * scale).astype(jnp.bfloat16)
        p_sorted = (w_sorted * scale).astype(jnp.bfloat16)
        probs_ref[0, g, :, :BLOCK] = p_own
        probs_ref[0, g, :, BLOCK : 2 * BLOCK] = p_before
        probs_ref[0, g, :, 2 * BLOCK :] = p_sorted
        attended = (
            dot(p_own, vo_ref[0, :, cols], AB)
            + dot(p_before, vb_ref[0, :, cols], AB)
            + dot(p_sorted, vs_ref[0, :, cols], AB)
        )
        attended_ref[:, cols] = attended
        lifted = gain_ref[:, cols] * grad_ref[:, cols].astype(jnp.float32)
        squares += jnp.sum(attended * attended, axis=1, keepdims=True)
        center += jnp.sum(lifted * attended, axis=1, keepdims=True)
    lane = lax.broadcasted_iota(jnp.int32, (BLOCK, LANES), 1)
    both = jnp.where(lane == 0, squares, jnp.where(lane == 1, center, 0.0))

    @pl.when(h == 0)
    def _():
        sums_ref[...] = both

    @pl.when(h > 0)
    def _():
        sums_ref[...] += both


def backward_kernel(
    meta_ref, q_ref, ko_ref, kb_ref, ks_ref, vo_ref, vb_ref, vs_ref, gain_ref, grad_ref,
    attended_ref, probs_ref, sums_ref,
    normed_ref, gq_ref, ok_ref, fk_ref, ov_ref, fv_ref, *, group,
):
    del meta_ref
    squares = sums_ref[:, 0:1]
    center = sums_ref[:, 1:2]
    inv_rms = lax.rsqrt(squares / WIDTH + 1e-05)
    factor = inv_rms * inv_rms * inv_rms * center / WIDTH
    for g in range(group):
        cols = slice(g * HDIM, (g + 1) * HDIM)
        q = q_ref[:, cols]
        attended = attended_ref[:, cols]
        gain = gain_ref[:, cols]
        normed_ref[:, cols] = (attended * inv_rms * gain).astype(jnp.bfloat16)
        lifted = gain * grad_ref[:, cols].astype(jnp.float32)
        grad = (inv_rms * lifted - attended * factor).astype(jnp.bfloat16)
        keys = (ko_ref[0, :, cols], kb_ref[0, :, cols], ks_ref[0, :, cols])
        values = (vo_ref[0, :, cols], vb_ref[0, :, cols], vs_ref[0, :, cols])
        probs = [probs_ref[0, g, :, j * BLOCK : (j + 1) * BLOCK] for j in range(3)]
        ov_ref[0, :, cols] = dot(probs[0], grad, TA)
        fv_ref[0, 0, :, cols] = dot(probs[1], grad, TA).astype(jnp.bfloat16)
        fv_ref[0, 1, :, cols] = dot(probs[2], grad, TA).astype(jnp.bfloat16)
        probs = [p.astype(jnp.float32) for p in probs]
        gp = [dot(grad, v, QK) for v in values]
        mix = [p * g_ for p, g_ in zip(probs, gp)]
        row = jnp.sum(mix[0] + mix[1] + mix[2], axis=1, keepdims=True)
        gs = [(p * (g_ - row) * SCALE).astype(jnp.bfloat16) for p, g_ in zip(probs, gp)]
        gq_ref[:, cols] = (
            dot(gs[0], keys[0], AB) + dot(gs[1], keys[1], AB) + dot(gs[2], keys[2], AB)
        ).astype(jnp.bfloat16)
        ok_ref[0, :, cols] = dot(gs[0], q, TA)
        fk_ref[0, 0, :, cols] = dot(gs[1], q, TA).astype(jnp.bfloat16)
        fk_ref[0, 1, :, cols] = dot(gs[2], q, TA).astype(jnp.bfloat16)


def attention_specs(blocks, width):
    rows = pl.BlockSpec((BLOCK, width), lambda i, h, meta: (i, h))
    own = pl.BlockSpec((1, BLOCK, width), lambda i, h, meta: (meta[0] + i, 0, h))
    before = pl.BlockSpec((1, BLOCK, width), lambda i, h, meta: (meta[1 + 2 * i], 0, h))
    chosen = pl.BlockSpec((1, BLOCK, width), lambda i, h, meta: (meta[2 + 2 * i], 0, h))
    gain = pl.BlockSpec((1, width), lambda i, h, meta: (0, h))
    return rows, own, before, chosen, gain


def on_device(queries, key_rows, value_rows, norm_gain, sort_index, grad_normed):
    ctx_size = lax.axis_size("ctx")
    rows, columns = queries.shape
    blocks = rows // BLOCK
    heads = columns // HDIM
    group = 2 if heads % 2 == 0 else 1
    width = group * HDIM
    tab, steps = routing_table(sort_index, ctx_size, blocks)
    gain = norm_gain.reshape(1, columns)

    last = tab[steps * ROW : (steps + 1) * ROW]
    base = last[blocks + 2]
    before = jnp.concatenate(
        [last[blocks : blocks + 1], base + jnp.arange(blocks - 1, dtype=jnp.int32)]
    )
    chosen = last[:blocks]
    slots_list = jnp.concatenate(
        [base[None], jnp.stack([before, chosen], axis=1).reshape(-1)]
    )
    first_block = lax.axis_index("ctx") * blocks
    meta = jnp.concatenate([slots_list, first_block.astype(jnp.int32)[None]])

    shape3 = (blocks, BLOCK, columns)
    keys, values = gather_blocks(
        [key_rows.reshape(shape3), value_rows.reshape(shape3)], tab, steps, ctx_size
    )

    row_spec, own, prev, pick, gain_spec = attention_specs(blocks, width)
    sums_spec = pl.BlockSpec((BLOCK, LANES), lambda i, h, meta: (i, 0))
    probs_spec = pl.BlockSpec((1, group, BLOCK, 3 * BLOCK), lambda i, h, meta: (i, h, 0, 0))
    common = [row_spec, own, prev, pick, own, prev, pick, gain_spec, row_spec]
    attended, probs, sums = pl.pallas_call(
        functools.partial(forward_kernel, blocks=blocks, group=group),
        out_shape=(
            jax.ShapeDtypeStruct((rows, columns), jnp.float32),
            jax.ShapeDtypeStruct((blocks, heads, BLOCK, 3 * BLOCK), jnp.bfloat16),
            jax.ShapeDtypeStruct((rows, LANES), jnp.float32),
        ),
        grid_spec=pltpu.PrefetchScalarGridSpec(
            num_scalar_prefetch=1,
            grid=(blocks, heads // group),
            in_specs=common,
            out_specs=(row_spec, probs_spec, sums_spec),
        ),
        compiler_params=pltpu.CompilerParams(vmem_limit_bytes=48 * 1024 * 1024),
        cost_estimate=pl.CostEstimate(
            flops=4 * rows * 3 * BLOCK * columns,
            bytes_accessed=50_000_000,
            transcendentals=rows * 3 * BLOCK * heads,
        ),
        name="attention_forward",
    )(meta, queries, keys, keys, keys, values, values, values, gain, grad_normed)

    sums = lax.psum(sums[:, :2], "head")

    far_spec = pl.BlockSpec((1, 2, BLOCK, width), lambda i, h, meta: (i, 0, 0, h))
    block_spec = pl.BlockSpec((1, BLOCK, width), lambda i, h, meta: (i, 0, h))
    two_spec = pl.BlockSpec((BLOCK, 2), lambda i, h, meta: (i, 0))
    wide = jax.ShapeDtypeStruct((rows, columns), jnp.bfloat16)
    own_shape = jax.ShapeDtypeStruct(shape3, jnp.float32)
    far_shape = jax.ShapeDtypeStruct((blocks, 2, BLOCK, columns), jnp.bfloat16)
    normed, grad_q, own_k, far_k, own_v, far_v = pl.pallas_call(
        functools.partial(backward_kernel, group=group),
        out_shape=(wide, wide, own_shape, far_shape, own_shape, far_shape),
        grid_spec=pltpu.PrefetchScalarGridSpec(
            num_scalar_prefetch=1,
            grid=(blocks, heads // group),
            in_specs=common + [row_spec, probs_spec, two_spec],
            out_specs=(row_spec, row_spec, block_spec, far_spec, block_spec, far_spec),
        ),
        compiler_params=pltpu.CompilerParams(vmem_limit_bytes=48 * 1024 * 1024),
        cost_estimate=pl.CostEstimate(
            flops=8 * rows * 3 * BLOCK * columns,
            bytes_accessed=70_000_000,
            transcendentals=0,
        ),
        name="attention_backward",
    )(
        meta, queries, keys, keys, keys, values, values, values, gain, grad_normed,
        attended, probs, sums,
    )
    shape_far = (2 * blocks, BLOCK, columns)
    grad_k, grad_v = return_blocks(
        [(own_k, far_k.reshape(shape_far)), (own_v, far_v.reshape(shape_far))],
        slots_list,
        tab,
        steps,
        ctx_size,
    )
    return normed, grad_q, grad_k.reshape(rows, columns), grad_v.reshape(rows, columns)


def solution(mesh):
    in_specs = (
        P("ctx", "head"),
        P("ctx", "head"),
        P("ctx", "head"),
        P("head"),
        P(),
        P("ctx", "head"),
    )
    out_specs = (P("ctx", "head"), P("ctx", "head"), P("ctx", "head"), P("ctx", "head"))
    return jax.shard_map(
        on_device, mesh=mesh, in_specs=in_specs, out_specs=out_specs, check_vma=False
    )
```

```python
import functools
import math

import jax
import jax.numpy as jnp
import numpy as np
from jax import lax
from jax.experimental import pallas as pl
from jax.experimental.pallas import tpu as pltpu
from jax.sharding import PartitionSpec as P

HDIM = 128
BLOCK = 256
WIDTH = 5120
LANES = 128
ROW = 8
STATIC_STEPS = 5
SCALE = HDIM ** (-0.5)
ANY = pl.BlockSpec(memory_space=pl.ANY)
SMEM = pl.BlockSpec(memory_space=pltpu.SMEM)
VMEM = pl.BlockSpec(memory_space=pltpu.VMEM)


def max_steps(ctx_size, blocks):
    return blocks * (ctx_size // 2) + ctx_size // 2 + 2 * blocks + 4


def shift_rows(array, count, rows):
    n = array.shape[0]
    if abs(count) >= n:
        return jnp.zeros_like(array)
    rolled = pltpu.roll(array, (-count) % n, 0)
    inside = (rows < n - count) if count > 0 else (rows >= -count)
    return jnp.where(inside, rolled, 0.0)


def table_kernel(picks_ref, owner_ref, slot_ref, out_ref, *, blocks, steps):
    n = picks_ref.shape[0]
    levels = n // 2
    rows = lax.broadcasted_iota(jnp.int32, (n, LANES), 0)
    lanes = lax.broadcasted_iota(jnp.int32, (n, LANES), 1)
    owner = owner_ref[...]
    slot = slot_ref[...]
    picks = picks_ref[...]
    side = rows & 1
    level = rows >> 1
    owner_side = owner & 1
    owner_level = owner >> 1

    def other(array):
        return jnp.where(side == 0, pltpu.roll(array, n - 1, 0), pltpu.roll(array, 1, 0))

    need = jnp.zeros((n, LANES), jnp.float32)
    for j in range(blocks + 1):
        need = jnp.where(picks[:, j : j + 1] == lanes, 1.0, need)
    need = jnp.where(owner == rows, 0.0, need)
    wanted = jnp.maximum(need, other(need))
    far_up = jnp.zeros_like(need)
    far_down = jnp.zeros_like(need)
    for k in range(1, levels):
        far_up = jnp.where(shift_rows(wanted, 2 * k, rows) > 0, float(k), far_up)
        far_down = jnp.where(shift_rows(wanted, -2 * k, rows) > 0, float(k), far_down)
    travels = side == owner_side
    low = (LANES - 1 - lanes).astype(jnp.float32)
    up = jnp.where(travels & (level >= owner_level) & (far_up > 0), 1.0, 0.0)
    down = jnp.where(travels & (level <= owner_level) & (far_down > 0), 1.0, 0.0)
    over = jnp.where(travels, other(need), 0.0)
    have = jnp.where(owner == rows, 1.0, 0.0)
    first_over = float(blocks * levels)

    out_ref[...] = jnp.full(out_ref.shape, -1, jnp.int32)

    def pick(pending, have, rank):
        score = jnp.where(pending * have > 0, rank, -1.0)
        best = jnp.max(score, axis=1, keepdims=True)
        return jnp.where((score == best) & (best >= 0), 1.0, 0.0)

    def place(chosen):
        return jnp.sum(chosen * (slot + 1.0), axis=1, keepdims=True) - 1.0

    def pending(state):
        t, have, up, down, over, over_slot, count = state
        return (t < steps) & (jnp.sum(up + down + over) > 0)

    def step(state):
        t, have, up, down, over, over_slot, count = state
        send_up = pick(up, have, far_up * LANES + low)
        send_down = pick(down, have, far_down * LANES + low)
        send_over = pick(over, have, low)
        got_up = shift_rows(send_up, -2, rows)
        got_down = shift_rows(send_down, 2, rows)
        got_over = other(send_over)
        any_over = jnp.max(got_over, axis=1, keepdims=True)
        columns = (
            place(send_up),
            place(send_down),
            place(send_over),
            place(got_up),
            place(got_down),
            jnp.where(any_over > 0, count + first_over, -1.0),
        )
        row = jnp.full((n, LANES), -1.0, jnp.float32)
        for k, column in enumerate(columns):
            row = jnp.where(lanes == k, column, row)
        out_ref[t] = row.astype(jnp.int32)
        over_slot = jnp.where(got_over > 0, count + first_over, over_slot)
        have = jnp.maximum(have, jnp.maximum(got_up, jnp.maximum(got_down, got_over)))
        return (
            t + 1,
            have,
            up - send_up,
            down - send_down,
            over - send_over,
            over_slot,
            count + any_over,
        )

    state = (
        jnp.int32(0),
        have,
        up,
        down,
        over,
        jnp.zeros_like(need),
        jnp.zeros((n, 1), jnp.float32),
    )
    state = lax.while_loop(pending, step, state)
    over_slot = state[5]
    slots = jnp.where(travels, slot, over_slot)
    row = jnp.zeros((n, LANES), jnp.float32)
    for j in range(blocks + 1):
        where = jnp.sum(
            jnp.where(picks[:, j : j + 1] == lanes, slots, 0.0), axis=1, keepdims=True
        )
        row = jnp.where(lanes == j, where, row)
    row = jnp.where(lanes == blocks + 1, state[0].astype(jnp.float32), row)
    row = jnp.where(lanes == blocks + 2, (level * blocks).astype(jnp.float32), row)
    out_ref[steps] = row.astype(jnp.int32)


def routing_table(sort_index, ctx_size, blocks):
    steps = max_steps(ctx_size, blocks)
    block_ids = np.arange(LANES)
    owner = np.broadcast_to((block_ids // blocks)[None], (ctx_size, LANES)).astype(np.int32)
    slot = (block_ids // (2 * blocks)) * blocks + block_ids % blocks
    slot = np.broadcast_to(slot[None], (ctx_size, LANES)).astype(np.float32)
    before = (np.arange(ctx_size, dtype=np.int32) * blocks - 1)[:, None]
    picks = jnp.concatenate(
        [sort_index.reshape(ctx_size, blocks), jnp.asarray(before)], axis=1
    )
    picks = jnp.pad(picks, ((0, 0), (0, LANES - blocks - 1)), constant_values=-1)
    table = pl.pallas_call(
        functools.partial(table_kernel, blocks=blocks, steps=steps),
        out_shape=jax.ShapeDtypeStruct((steps + 1, ctx_size, LANES), jnp.int32),
        in_specs=[VMEM] * 3,
        out_specs=VMEM,
        name="routing_table",
    )(picks, jnp.asarray(owner), jnp.asarray(slot))
    mine = lax.dynamic_slice(table, (0, lax.axis_index("ctx"), 0), (steps + 1, 1, ROW))
    return mine.reshape((steps + 1) * ROW), steps


def routes(ctx_size):
    up = [(d, d + 2) for d in range(ctx_size - 2)]
    down = [(d + 2, d) for d in range(ctx_size - 2)]
    over = [(d, d ^ 1) for d in range(ctx_size)]
    return up, down, over


def copies(jobs, sems):
    started = []
    for k, (valid, source, target) in enumerate(jobs):
        copy = pltpu.make_async_copy(source, target, sems.at[k])
        pl.when(valid)(copy.start)
        started.append((valid, copy))
    for valid, copy in started:
        pl.when(valid)(copy.wait)


def open_kernel(
    tab_ref, own_ref, pool_ref, up_ref, down_ref, over_ref, held_ref, sems, *, base_at
):
    blocks = own_ref.shape[0]
    base = tab_ref[base_at]
    load = pltpu.make_async_copy(own_ref, held_ref, sems.at[0])
    load.start()
    load.wait()
    jobs = []
    for k, out in enumerate((up_ref, down_ref, over_ref)):
        slot = tab_ref[k]
        jobs.append((slot >= 0, held_ref.at[jnp.clip(slot - base, 0, blocks - 1)], out))
    jobs.append((base >= 0, held_ref, pool_ref.at[pl.ds(base, blocks)]))
    copies(jobs, sems)


def store_arrived(t, tab_ref, arrived, pool_ref, held_ref, sems):
    slots = [tab_ref[(t - 1) * ROW + 3 + k] for k in range(3)]
    copies([(s >= 0, got, held_ref.at[k]) for k, (s, got) in enumerate(zip(slots, arrived))], sems)
    copies(
        [(s >= 0, held_ref.at[k], pool_ref.at[jnp.maximum(s, 0)]) for k, s in enumerate(slots)],
        sems,
    )


def take_out(slots, outs, pool_ref, held_ref, sems):
    copies(
        [(s >= 0, pool_ref.at[jnp.maximum(s, 0)], held_ref.at[k]) for k, s in enumerate(slots)],
        sems,
    )
    copies([(s >= 0, held_ref.at[k], out) for k, (s, out) in enumerate(zip(slots, outs))], sems)


def step_kernel(
    t_ref, tab_ref, pool_in, in_up, in_down, in_over, pool_ref, up_ref, down_ref, over_ref,
    held_ref, sems,
):
    del pool_in
    t = t_ref[0]
    store_arrived(t, tab_ref, (in_up, in_down, in_over), pool_ref, held_ref, sems)
    slots = [tab_ref[t * ROW + k] for k in range(3)]
    take_out(slots, (up_ref, down_ref, over_ref), pool_ref, held_ref, sems)


def close_kernel(t_ref, tab_ref, pool_in, in_up, in_down, in_over, pool_ref, held_ref, sems):
    del pool_in
    store_arrived(t_ref[0], tab_ref, (in_up, in_down, in_over), pool_ref, held_ref, sems)


BIG = pltpu.CompilerParams(vmem_limit_bytes=56 * 1024 * 1024)


def traffic(byte_count):
    return pl.CostEstimate(flops=0, bytes_accessed=byte_count, transcendentals=0)


def send_all(sends, perms):
    return tuple(lax.ppermute(s, "ctx", p) for s, p in zip(sends, perms))


def gather_blocks(streams, tab, steps, ctx_size):
    blocks = streams[0].shape[0]
    slots = blocks * (ctx_size // 2) + blocks + 1
    perms = routes(ctx_size)
    last_row = steps * ROW
    total = tab[last_row + blocks + 1]

    def shapes(stream):
        one = jax.ShapeDtypeStruct(stream.shape[1:], stream.dtype)
        pool = jax.ShapeDtypeStruct((slots,) + stream.shape[1:], stream.dtype)
        return pool, one

    def three(one):
        return [pltpu.VMEM((3,) + one.shape, one.dtype), pltpu.SemaphoreType.DMA((3,))]

    def size(stream):
        return 2 * math.prod(stream.shape[1:])

    def first(stream):
        pool, one = shapes(stream)
        return pl.pallas_call(
            functools.partial(open_kernel, base_at=last_row + blocks + 2),
            out_shape=(pool, one, one, one),
            in_specs=[SMEM, ANY],
            out_specs=(ANY,) * 4,
            scratch_shapes=[
                pltpu.VMEM(stream.shape, stream.dtype),
                pltpu.SemaphoreType.DMA((4,)),
            ],
            compiler_params=BIG,
            cost_estimate=traffic(size(stream) * 14),
            name="gather_open",
        )(tab, stream)

    def later(t, pool, got, stream):
        pool_shape, one = shapes(stream)
        return pl.pallas_call(
            step_kernel,
            out_shape=(pool_shape, one, one, one),
            in_specs=[SMEM, SMEM] + [ANY] * 4,
            out_specs=(ANY,) * 4,
            scratch_shapes=three(one),
            compiler_params=BIG,
            input_output_aliases={2: 0},
            cost_estimate=traffic(size(stream) * 12),
            name="gather_step",
        )(t, tab, pool, *got)

    def close(t, pool, got, stream):
        pool_shape, one = shapes(stream)
        return pl.pallas_call(
            close_kernel,
            out_shape=pool_shape,
            in_specs=[SMEM, SMEM] + [ANY] * 4,
            out_specs=ANY,
            scratch_shapes=three(one),
            compiler_params=BIG,
            input_output_aliases={2: 0},
            cost_estimate=traffic(size(stream) * 6),
            name="gather_close",
        )(t, tab, pool, *got)

    held = []
    for stream in streams:
        pool, *sends = first(stream)
        held.append((pool, send_all(sends, perms)))

    def advance(t, held):
        result = []
        for (pool, got), stream in zip(held, streams):
            pool, *sends = later(t.reshape(1), pool, got, stream)
            result.append((pool, send_all(sends, perms)))
        return result

    for t in range(1, STATIC_STEPS):
        held = advance(jnp.full((1,), t, jnp.int32), held)

    def body(state):
        t, held = state
        return t + 1, advance(t, held)

    t, held = lax.while_loop(
        lambda state: state[0] < total, body, (jnp.int32(STATIC_STEPS), held)
    )
    return [
        close(t.reshape(1), pool, got, stream) for (pool, got), stream in zip(held, streams)
    ]


def init_kernel(slots_ref, own_ref, terms_ref, pool_in, pool_ref, *, blocks):
    del pool_in
    s = pl.program_id(0)
    base = slots_ref[0]
    at = s - base
    own = (at >= 0) & (at < blocks)
    own_at = jnp.clip(at, 0, blocks - 1)
    pool_ref[0] = jnp.where(own, own_ref[own_at].astype(jnp.float32), 0.0).astype(pool_ref.dtype)
    for k in range(2 * blocks):

        @pl.when(slots_ref[1 + k] == s)
        def _(k=k):
            pool_ref[0] = (
                pool_ref[0].astype(jnp.float32) + terms_ref[k].astype(jnp.float32)
            ).astype(pool_ref.dtype)


def back_kernel(
    t_ref, tab_ref, pool_in, in_up, in_down, in_over, pool_ref, up_ref, down_ref, over_ref,
    held_ref, got_ref, sems,
):
    del pool_in
    t = t_ref[0]
    add_back(t, tab_ref, (in_up, in_down, in_over), pool_ref, held_ref, got_ref, sems)
    slots = [tab_ref[t * ROW + 3 + k] for k in range(3)]
    take_out(slots, (up_ref, down_ref, over_ref), pool_ref, held_ref, sems)


def add_back(t, tab_ref, arrived, pool_ref, held_ref, got_ref, sems):
    slots = [tab_ref[(t + 1) * ROW + k] for k in range(3)]
    same = [False, slots[1] == slots[0], (slots[2] == slots[0]) | (slots[2] == slots[1])]
    jobs = [(s >= 0, got, got_ref.at[k]) for k, (s, got) in enumerate(zip(slots, arrived))]
    jobs += [
        (s >= 0, pool_ref.at[jnp.maximum(s, 0)], held_ref.at[k]) for k, s in enumerate(slots)
    ]
    copies(jobs, sems)
    for k, slot in enumerate(slots):
        targets = [(k, slot >= 0)]
        if k == 1:
            targets = [(1, (slot >= 0) & (slot != slots[0])), (0, (slot >= 0) & (slot == slots[0]))]
        if k == 2:
            first = slot == slots[0]
            second = (slot == slots[1]) & jnp.logical_not(first)
            neither = jnp.logical_not(first | second)
            targets = [(2, (slot >= 0) & neither), (0, (slot >= 0) & first), (1, (slot >= 0) & second)]
        for at, valid in targets:

            @pl.when(valid)
            def _(k=k, at=at):
                held_ref[at] = (
                    held_ref[at].astype(jnp.float32) + got_ref[k].astype(jnp.float32)
                ).astype(held_ref.dtype)

    copies(
        [
            (
                (s >= 0) & jnp.logical_not(dup),
                held_ref.at[k],
                pool_ref.at[jnp.maximum(s, 0)],
            )
            for k, (s, dup) in enumerate(zip(slots, same))
        ],
        sems,
    )


def finish_kernel(
    tab_ref, pool_in, in_up, in_down, in_over, pool_ref, out_ref, held_ref, got_ref, last_ref,
    sems, *, base_at,
):
    del pool_in
    add_back(-1, tab_ref, (in_up, in_down, in_over), pool_ref, held_ref, got_ref, sems)
    base = tab_ref[base_at]
    blocks = out_ref.shape[0]
    load = pltpu.make_async_copy(pool_ref.at[pl.ds(base, blocks)], last_ref, sems.at[0])
    load.start()
    load.wait()
    store = pltpu.make_async_copy(last_ref, out_ref, sems.at[0])
    store.start()
    store.wait()


def return_blocks(streams, slots_list, tab, steps, ctx_size):
    blocks = streams[0][0].shape[0]
    slots = blocks * (ctx_size // 2) + blocks + 1
    up, down, over = routes(ctx_size)
    perms = ([(b, a) for a, b in up], [(b, a) for a, b in down], over)
    last_row = steps * ROW
    total = tab[last_row + blocks + 1]
    dtype = jnp.bfloat16
    held = []
    for own, far, used in streams:
        shape = own.shape[1:]
        pool = pl.pallas_call(
            functools.partial(init_kernel, blocks=blocks),
            out_shape=jax.ShapeDtypeStruct((slots,) + shape, dtype),
            grid_spec=pltpu.PrefetchScalarGridSpec(
                num_scalar_prefetch=1,
                grid=(slots,),
                in_specs=[VMEM, VMEM, ANY],
                out_specs=pl.BlockSpec((1,) + shape, lambda s, ref: (s, 0, 0)),
            ),
            input_output_aliases={3: 0},
            compiler_params=pltpu.CompilerParams(vmem_limit_bytes=48 * 1024 * 1024),
            cost_estimate=traffic(2 * math.prod(shape) * (slots + 3 * blocks)),
            name="return_open",
        )(slots_list, own, far, used)
        held.append((pool, (jnp.zeros(shape, dtype),) * 3))

    def scratch(one):
        return [
            pltpu.VMEM((3,) + one.shape, one.dtype),
            pltpu.VMEM((3,) + one.shape, one.dtype),
            pltpu.SemaphoreType.DMA((6,)),
        ]

    def back(t, pool, got):
        one = jax.ShapeDtypeStruct(pool.shape[1:], pool.dtype)
        return pl.pallas_call(
            back_kernel,
            out_shape=(jax.ShapeDtypeStruct(pool.shape, pool.dtype), one, one, one),
            in_specs=[SMEM, SMEM] + [ANY] * 4,
            out_specs=(ANY,) * 4,
            scratch_shapes=scratch(one),
            input_output_aliases={2: 0},
            compiler_params=BIG,
            cost_estimate=traffic(2 * math.prod(one.shape) * 16),
            name="return_step",
        )(t, tab, pool, *got)

    def finish(pool, got):
        one = jax.ShapeDtypeStruct(pool.shape[1:], pool.dtype)
        return pl.pallas_call(
            functools.partial(finish_kernel, base_at=last_row + blocks + 2),
            out_shape=(
                jax.ShapeDtypeStruct(pool.shape, pool.dtype),
                jax.ShapeDtypeStruct((blocks,) + one.shape, one.dtype),
            ),
            in_specs=[SMEM] + [ANY] * 4,
            out_specs=(ANY, ANY),
            scratch_shapes=scratch(one)[:2]
            + [pltpu.VMEM((blocks,) + one.shape, one.dtype)]
            + scratch(one)[2:],
            input_output_aliases={1: 0},
            compiler_params=BIG,
            cost_estimate=traffic(2 * math.prod(one.shape) * 16),
            name="return_close",
        )(tab, pool, *got)[1]

    def retreat(t, held):
        result = []
        for pool, got in held:
            pool, *sends = back(t.reshape(1), pool, got)
            result.append((pool, send_all(sends, perms)))
        return result

    def body(state):
        t, held = state
        return t - 1, retreat(t, held)

    _, held = lax.while_loop(
        lambda state: state[0] >= STATIC_STEPS, body, (total - 1, held)
    )
    for t in range(STATIC_STEPS - 1, -1, -1):
        held = retreat(jnp.full((1,), t, jnp.int32), held)
    return [finish(pool, got) for pool, got in held]


QK = (((1,), (1,)), ((), ()))
AB = (((1,), (0,)), ((), ()))
TA = (((0,), (0,)), ((), ()))


def dot(a, b, dims):
    return lax.dot_general(a, b, dims, preferred_element_type=jnp.float32)


def forward_kernel(
    meta_ref, q_ref, ko_ref, kb_ref, ks_ref, vo_ref, vb_ref, vs_ref, gain_ref, grad_ref,
    attended_ref, probs_ref, sums_ref, *, blocks, group,
):
    i = pl.program_id(0)
    h = pl.program_id(1)
    block_id = meta_ref[1 + 2 * blocks] + i
    causal = lax.broadcasted_iota(jnp.int32, (BLOCK, BLOCK), 1) <= lax.broadcasted_iota(
        jnp.int32, (BLOCK, BLOCK), 0
    )
    hide = jnp.where(block_id > 0, 0.0, -jnp.inf).astype(jnp.float32)
    squares = jnp.zeros((BLOCK, 1), jnp.float32)
    center = jnp.zeros((BLOCK, 1), jnp.float32)
    for g in range(group):
        cols = slice(g * HDIM, (g + 1) * HDIM)
        q = q_ref[:, cols]
        s_own = jnp.where(causal, dot(q, ko_ref[0, :, cols], QK) * SCALE, -jnp.inf)
        s_before = dot(q, kb_ref[0, :, cols], QK) * SCALE + hide
        s_sorted = dot(q, ks_ref[0, :, cols], QK) * SCALE
        top = jnp.max(
            jnp.maximum(jnp.maximum(s_own, s_before), s_sorted), axis=1, keepdims=True
        )
        w_own = jnp.exp(s_own - top)
        w_before = jnp.exp(s_before - top)
        w_sorted = jnp.exp(s_sorted - top)
        scale = 1.0 / jnp.sum(w_own + w_before + w_sorted, axis=1, keepdims=True)
        p_own = (w_own * scale).astype(jnp.bfloat16)
        p_before = (w_before * scale).astype(jnp.bfloat16)
        p_sorted = (w_sorted * scale).astype(jnp.bfloat16)
        probs_ref[0, g, :, :BLOCK] = p_own
        probs_ref[0, g, :, BLOCK : 2 * BLOCK] = p_before
        probs_ref[0, g, :, 2 * BLOCK :] = p_sorted
        attended = (
            dot(p_own, vo_ref[0, :, cols], AB)
            + dot(p_before, vb_ref[0, :, cols], AB)
            + dot(p_sorted, vs_ref[0, :, cols], AB)
        )
        attended_ref[:, cols] = attended
        lifted = gain_ref[:, cols] * grad_ref[:, cols].astype(jnp.float32)
        squares += jnp.sum(attended * attended, axis=1, keepdims=True)
        center += jnp.sum(lifted * attended, axis=1, keepdims=True)
    lane = lax.broadcasted_iota(jnp.int32, (BLOCK, LANES), 1)
    both = jnp.where(lane == 0, squares, jnp.where(lane == 1, center, 0.0))

    @pl.when(h == 0)
    def _():
        sums_ref[...] = both

    @pl.when(h > 0)
    def _():
        sums_ref[...] += both


def backward_kernel(
    meta_ref, q_ref, ko_ref, kb_ref, ks_ref, vo_ref, vb_ref, vs_ref, gain_ref, grad_ref,
    attended_ref, probs_ref, sums_ref,
    normed_ref, gq_ref, ok_ref, fk_ref, ov_ref, fv_ref, *, group,
):
    del meta_ref
    squares = sums_ref[:, 0:1]
    center = sums_ref[:, 1:2]
    inv_rms = lax.rsqrt(squares / WIDTH + 1e-05)
    factor = inv_rms * inv_rms * inv_rms * center / WIDTH
    for g in range(group):
        cols = slice(g * HDIM, (g + 1) * HDIM)
        q = q_ref[:, cols]
        attended = attended_ref[:, cols]
        gain = gain_ref[:, cols]
        normed_ref[:, cols] = (attended * inv_rms * gain).astype(jnp.bfloat16)
        lifted = gain * grad_ref[:, cols].astype(jnp.float32)
        grad = (inv_rms * lifted - attended * factor).astype(jnp.bfloat16)
        keys = (ko_ref[0, :, cols], kb_ref[0, :, cols], ks_ref[0, :, cols])
        values = (vo_ref[0, :, cols], vb_ref[0, :, cols], vs_ref[0, :, cols])
        probs = [probs_ref[0, g, :, j * BLOCK : (j + 1) * BLOCK] for j in range(3)]
        ov_ref[0, :, cols] = dot(probs[0], grad, TA).astype(jnp.bfloat16)
        fv_ref[0, 0, :, cols] = dot(probs[1], grad, TA).astype(jnp.bfloat16)
        fv_ref[0, 1, :, cols] = dot(probs[2], grad, TA).astype(jnp.bfloat16)
        probs = [p.astype(jnp.float32) for p in probs]
        gp = [dot(grad, v, QK) for v in values]
        mix = [p * g_ for p, g_ in zip(probs, gp)]
        row = jnp.sum(mix[0] + mix[1] + mix[2], axis=1, keepdims=True)
        gs = [(p * (g_ - row) * SCALE).astype(jnp.bfloat16) for p, g_ in zip(probs, gp)]
        gq_ref[:, cols] = (
            dot(gs[0], keys[0], AB) + dot(gs[1], keys[1], AB) + dot(gs[2], keys[2], AB)
        ).astype(jnp.bfloat16)
        ok_ref[0, :, cols] = dot(gs[0], q, TA).astype(jnp.bfloat16)
        fk_ref[0, 0, :, cols] = dot(gs[1], q, TA).astype(jnp.bfloat16)
        fk_ref[0, 1, :, cols] = dot(gs[2], q, TA).astype(jnp.bfloat16)


def attention_specs(blocks, width):
    rows = pl.BlockSpec((BLOCK, width), lambda i, h, meta: (i, h))
    own = pl.BlockSpec((1, BLOCK, width), lambda i, h, meta: (meta[0] + i, 0, h))
    before = pl.BlockSpec((1, BLOCK, width), lambda i, h, meta: (meta[1 + 2 * i], 0, h))
    chosen = pl.BlockSpec((1, BLOCK, width), lambda i, h, meta: (meta[2 + 2 * i], 0, h))
    gain = pl.BlockSpec((1, width), lambda i, h, meta: (0, h))
    return rows, own, before, chosen, gain


def on_device(queries, key_rows, value_rows, norm_gain, sort_index, grad_normed):
    ctx_size = lax.axis_size("ctx")
    rows, columns = queries.shape
    blocks = rows // BLOCK
    heads = columns // HDIM
    group = 2 if heads % 2 == 0 else 1
    width = group * HDIM
    tab, steps = routing_table(sort_index, ctx_size, blocks)
    gain = norm_gain.reshape(1, columns)

    last = tab[steps * ROW : (steps + 1) * ROW]
    base = last[blocks + 2]
    before = jnp.concatenate(
        [last[blocks : blocks + 1], base + jnp.arange(blocks - 1, dtype=jnp.int32)]
    )
    chosen = last[:blocks]
    slots_list = jnp.concatenate(
        [base[None], jnp.stack([before, chosen], axis=1).reshape(-1)]
    )
    first_block = lax.axis_index("ctx") * blocks
    meta = jnp.concatenate([slots_list, first_block.astype(jnp.int32)[None]])

    shape3 = (blocks, BLOCK, columns)
    keys, values = gather_blocks(
        [key_rows.reshape(shape3), value_rows.reshape(shape3)], tab, steps, ctx_size
    )

    row_spec, own, prev, pick, gain_spec = attention_specs(blocks, width)
    sums_spec = pl.BlockSpec((BLOCK, LANES), lambda i, h, meta: (i, 0))
    probs_spec = pl.BlockSpec((1, group, BLOCK, 3 * BLOCK), lambda i, h, meta: (i, h, 0, 0))
    common = [row_spec, own, prev, pick, own, prev, pick, gain_spec, row_spec]
    attended, probs, sums = pl.pallas_call(
        functools.partial(forward_kernel, blocks=blocks, group=group),
        out_shape=(
            jax.ShapeDtypeStruct((rows, columns), jnp.float32),
            jax.ShapeDtypeStruct((blocks, heads, BLOCK, 3 * BLOCK), jnp.bfloat16),
            jax.ShapeDtypeStruct((rows, LANES), jnp.float32),
        ),
        grid_spec=pltpu.PrefetchScalarGridSpec(
            num_scalar_prefetch=1,
            grid=(blocks, heads // group),
            in_specs=common,
            out_specs=(row_spec, probs_spec, sums_spec),
        ),
        compiler_params=pltpu.CompilerParams(vmem_limit_bytes=48 * 1024 * 1024),
        cost_estimate=pl.CostEstimate(
            flops=4 * rows * 3 * BLOCK * columns,
            bytes_accessed=50_000_000,
            transcendentals=rows * 3 * BLOCK * heads,
        ),
        name="attention_forward",
    )(meta, queries, keys, keys, keys, values, values, values, gain, grad_normed)

    sums = lax.psum(sums[:, :2], "head")

    far_spec = pl.BlockSpec((1, 2, BLOCK, width), lambda i, h, meta: (i, 0, 0, h))
    block_spec = pl.BlockSpec((1, BLOCK, width), lambda i, h, meta: (i, 0, h))
    two_spec = pl.BlockSpec((BLOCK, 2), lambda i, h, meta: (i, 0))
    wide = jax.ShapeDtypeStruct((rows, columns), jnp.bfloat16)
    own_shape = jax.ShapeDtypeStruct(shape3, jnp.bfloat16)
    far_shape = jax.ShapeDtypeStruct((blocks, 2, BLOCK, columns), jnp.bfloat16)
    normed, grad_q, own_k, far_k, own_v, far_v = pl.pallas_call(
        functools.partial(backward_kernel, group=group),
        out_shape=(wide, wide, own_shape, far_shape, own_shape, far_shape),
        grid_spec=pltpu.PrefetchScalarGridSpec(
            num_scalar_prefetch=1,
            grid=(blocks, heads // group),
            in_specs=common + [row_spec, probs_spec, two_spec],
            out_specs=(row_spec, row_spec, block_spec, far_spec, block_spec, far_spec),
        ),
        compiler_params=pltpu.CompilerParams(vmem_limit_bytes=48 * 1024 * 1024),
        cost_estimate=pl.CostEstimate(
            flops=8 * rows * 3 * BLOCK * columns,
            bytes_accessed=70_000_000,
            transcendentals=0,
        ),
        name="attention_backward",
    )(
        meta, queries, keys, keys, keys, values, values, values, gain, grad_normed,
        attended, probs, sums,
    )
    shape_far = (2 * blocks, BLOCK, columns)
    grad_k, grad_v = return_blocks(
        [(own_k, far_k.reshape(shape_far), keys), (own_v, far_v.reshape(shape_far), values)],
        slots_list,
        tab,
        steps,
        ctx_size,
    )
    return normed, grad_q, grad_k.reshape(rows, columns), grad_v.reshape(rows, columns)


def solution(mesh):
    in_specs = (
        P("ctx", "head"),
        P("ctx", "head"),
        P("ctx", "head"),
        P("head"),
        P(),
        P("ctx", "head"),
    )
    out_specs = (P("ctx", "head"), P("ctx", "head"), P("ctx", "head"), P("ctx", "head"))
    return jax.shard_map(
        on_device, mesh=mesh, in_specs=in_specs, out_specs=out_specs, check_vma=False
    )
```

```python
import functools
import math

import jax
import jax.numpy as jnp
import numpy as np
from jax import lax
from jax.experimental import pallas as pl
from jax.experimental.pallas import tpu as pltpu
from jax.sharding import PartitionSpec as P

HDIM = 128
BLOCK = 256
WIDTH = 5120
LANES = 128
ROW = 16
LEAD = 2
FIRST = 1024
STATIC_SLOTS = 9
SCALE = HDIM ** (-0.5)
SCALE_LOG2 = SCALE * math.log2(math.e)
ANY = pl.BlockSpec(memory_space=pl.ANY)
SMEM = pl.BlockSpec(memory_space=pltpu.SMEM)
VMEM = pl.BlockSpec(memory_space=pltpu.VMEM)
BIG = pltpu.CompilerParams(vmem_limit_bytes=56 * 1024 * 1024)


class Layout:
    def __init__(self, ctx_size, blocks):
        self.ctx_size = ctx_size
        self.blocks = blocks
        self.levels = ctx_size // 2
        line = self.levels * blocks
        self.value_line = line
        self.value_own = 2 * line
        self.over = 2 * line + blocks
        self.places = self.over + 2 * (blocks + 1)
        self.slots = 2 * (2 * line + 2 * self.levels + 2 * blocks + 4)
        self.rows = self.slots + 2 * LEAD
        self.info = self.rows * ROW
        self.key_picks = self.info
        self.value_picks = self.info + blocks + 1
        self.total = self.info + 2 * blocks + 2
        self.device = self.info + 2 * blocks + 3


def shift_rows(array, count, rows):
    n = array.shape[0]
    if abs(count) >= n:
        return jnp.zeros_like(array)
    rolled = pltpu.roll(array, (-count) % n, 0)
    inside = (rows < n - count) if count > 0 else (rows >= -count)
    return jnp.where(inside, rolled, 0.0)


def table_kernel(picks_ref, owner_ref, block_ref, kind_ref, place_ref, out_ref, *, lay):
    n = lay.ctx_size
    blocks = lay.blocks
    width = owner_ref.shape[1]
    rows = lax.broadcasted_iota(jnp.int32, (n, width), 0)
    lanes = lax.broadcasted_iota(jnp.int32, (n, width), 1)
    out_lanes = lax.broadcasted_iota(jnp.int32, (n, LANES), 1)
    owner = owner_ref[...]
    block = block_ref[...]
    values = kind_ref[...] == 1
    place = place_ref[...]
    picks = picks_ref[...]
    side = rows & 1
    level = rows >> 1
    same_side = side == (owner & 1)
    travels = jnp.logical_xor(same_side, values)
    owned = owner == rows

    def other(array):
        return jnp.where(side == 0, pltpu.roll(array, n - 1, 0), pltpu.roll(array, 1, 0))

    need = jnp.zeros((n, width), jnp.float32)
    for j in range(blocks + 1):
        need = jnp.where(picks[:, j : j + 1] == block, 1.0, need)
    need = jnp.where(owned, 0.0, need)
    across = other(need)
    wanted = jnp.maximum(need, across)
    final = jnp.where(travels, across, 0.0)
    hops = jnp.where(wanted > 0, 1.0 + final, 0.0)
    up_hops = jnp.zeros_like(need)
    down_hops = jnp.zeros_like(need)
    for k in range(1, lay.levels):
        above = shift_rows(hops, 2 * k, rows)
        below = shift_rows(hops, -2 * k, rows)
        up_hops = jnp.maximum(up_hops, jnp.where(above > 0, above + (k - 1), 0.0))
        down_hops = jnp.maximum(down_hops, jnp.where(below > 0, below + (k - 1), 0.0))
    up = jnp.where(travels & (level >= (owner >> 1)) & (up_hops > 0), 1.0, 0.0)
    down = jnp.where(travels & (level <= (owner >> 1)) & (down_hops > 0), 1.0, 0.0)
    source = owned & jnp.logical_not(travels)
    most = jnp.maximum(up_hops, down_hops)
    over = jnp.where(source & ((most > 0) | (across > 0)), 1.0, final)
    spread = jnp.minimum(jnp.sum(need, axis=0, keepdims=True), 3.0)
    low = (width - 1 - lanes).astype(jnp.float32)
    up_rank = (up_hops * 4.0 + spread) * width + low
    down_rank = (down_hops * 4.0 + spread) * width + low
    over_rank = jnp.where(source, most * 4.0 + spread, 2.0) * width + low
    first_over = float(lay.over)

    out_ref[...] = jnp.full(out_ref.shape, -1, jnp.int32)

    def pick(pending, have, rank):
        score = jnp.where(pending * have > 0, rank, -1.0)
        best = jnp.max(score, axis=1, keepdims=True)
        return jnp.where((score == best) & (best >= 0), 1.0, 0.0)

    def where(chosen):
        return jnp.sum(chosen * (place + 1.0), axis=1, keepdims=True) - 1.0

    def pending(state):
        t, have, fresh, up, down, over, over_place, count = state
        return (t < lay.slots) & (jnp.sum(up + down + over) > 0)

    def step(state):
        t, have, fresh, up, down, over, over_place, count = state
        send_up = pick(up, have, up_rank)
        send_down = pick(down, have, down_rank)
        send_over = pick(over, have, over_rank)
        up = up - send_up
        down = down - send_down
        over = over - send_over
        got_up = shift_rows(send_up, -2, rows)
        got_down = shift_rows(send_down, 2, rows)
        got_over = other(send_over)
        got_final = jnp.where(travels, 0.0, got_over)
        any_final = jnp.max(got_final, axis=1, keepdims=True)
        over_at = jnp.where(any_final > 0, count + first_over, where(got_over))
        last = jnp.where((up + down + over + need > 0) | owned, 0.0, float(FIRST))

        def first_back(chosen):
            return jnp.max(chosen * last, axis=1, keepdims=True)

        columns = (
            where(send_up) + first_back(send_up),
            where(send_down) + first_back(send_down * (1.0 - send_up)),
            where(send_over) + first_back(send_over * (1.0 - send_up) * (1.0 - send_down)),
            where(got_up),
            where(got_down),
            over_at,
        )
        row = jnp.full((n, LANES), -1.0, jnp.float32)
        for k, column in enumerate(columns):
            row = jnp.where(out_lanes == k, column, row)
        out_ref[t + LEAD] = row.astype(jnp.int32)
        over_place = jnp.where(got_final > 0, count + first_over, over_place)
        have = jnp.maximum(have, fresh)
        fresh = jnp.maximum(got_up, jnp.maximum(got_down, got_over))
        return (t + 1, have, fresh, up, down, over, over_place, count + any_final)

    zeros = jnp.zeros_like(need)
    have = jnp.where(owned, 1.0, 0.0)
    state = (jnp.int32(0), have, zeros, up, down, over, zeros, jnp.zeros((n, 1), jnp.float32))
    state = lax.while_loop(pending, step, state)
    at = jnp.where(travels | owned, place, state[6])
    own_row = lax.broadcasted_iota(jnp.int32, (n, LANES), 0)
    row = jnp.zeros((n, LANES), jnp.float32)
    for kind in range(2):
        base = (own_row >> 1) * blocks if kind == 0 else jnp.full((n, LANES), lay.value_own)
        for j in range(blocks + 1):
            chosen = (picks[:, j : j + 1] == block) & (values if kind else jnp.logical_not(values))
            found = jnp.sum(jnp.where(chosen, at, 0.0), axis=1, keepdims=True)
            found = jnp.where(picks[:, j : j + 1] < 0, base[:, :1].astype(jnp.float32), found)
            row = jnp.where(out_lanes == kind * (blocks + 1) + j, found, row)
    row = jnp.where(out_lanes == 2 * blocks + 2, state[0].astype(jnp.float32), row)
    row = jnp.where(out_lanes == 2 * blocks + 3, own_row.astype(jnp.float32), row)
    out_ref[lay.rows] = row.astype(jnp.int32)


def routing_table(sort_index, lay):
    n, blocks = lay.ctx_size, lay.blocks
    count = n * blocks
    width = -(-2 * count // LANES) * LANES
    block = np.full(width, -2, np.int32)
    kind = np.zeros(width, np.int32)
    block[:count] = np.arange(count)
    block[count : 2 * count] = np.arange(count)
    kind[count : 2 * count] = 1
    owner = np.where(block >= 0, block // blocks, -2).astype(np.int32)
    device = np.arange(n)[:, None]
    line = np.where(block >= 0, (block // (2 * blocks)) * blocks + block % blocks, 0)[None]
    place = np.where(kind[None] == 1, lay.value_line + line, line)
    mine = (kind[None] == 1) & (owner[None] == device)
    place = np.where(mine, lay.value_own + block[None] % blocks, place).astype(np.float32)

    def whole(array):
        return jnp.asarray(np.broadcast_to(array[None], (n, width)))

    before = (np.arange(n, dtype=np.int32) * blocks - 1)[:, None]
    picks = jnp.concatenate([sort_index.reshape(n, blocks), jnp.asarray(before)], axis=1)
    picks = jnp.pad(picks, ((0, 0), (0, LANES - blocks - 1)), constant_values=-1)
    table = pl.pallas_call(
        functools.partial(table_kernel, lay=lay),
        out_shape=jax.ShapeDtypeStruct((lay.rows + 1, n, LANES), jnp.int32),
        in_specs=[VMEM] * 5,
        out_specs=VMEM,
        name="routing_table",
    )(picks, whole(owner), whole(block), whole(kind), jnp.asarray(place))
    mine = lax.dynamic_slice(table, (0, lax.axis_index("ctx"), 0), (lay.rows + 1, 1, ROW))
    return mine.reshape((lay.rows + 1) * ROW)


def routes(ctx_size):
    up = [(d, d + 2) for d in range(ctx_size - 2)]
    down = [(d + 2, d) for d in range(ctx_size - 2)]
    over = [(d, d ^ 1) for d in range(ctx_size)]
    return up, down, over


def copies(jobs, sems):
    started = []
    for k, (valid, source, target) in enumerate(jobs):
        copy = pltpu.make_async_copy(source, target, sems.at[k])
        pl.when(valid)(copy.start)
        started.append((valid, copy))
    for valid, copy in started:
        pl.when(valid)(copy.wait)


def entry(tab_ref, t, k):
    return tab_ref[(t + LEAD) * ROW + k]


def place_of(code):
    return jnp.maximum(code, 0) & (FIRST - 1)


def fill_kernel(tab_ref, key_ref, value_ref, pool_ref, held_ref, sems, *, lay):
    blocks = lay.blocks
    level = tab_ref[lay.device] >> 1
    loads = [
        pltpu.make_async_copy(key_ref, held_ref.at[pl.ds(0, blocks)], sems.at[0]),
        pltpu.make_async_copy(value_ref, held_ref.at[pl.ds(blocks, blocks)], sems.at[1]),
    ]
    stores = [
        pltpu.make_async_copy(
            held_ref.at[pl.ds(0, blocks)], pool_ref.at[pl.ds(level * blocks, blocks)], sems.at[2]
        ),
        pltpu.make_async_copy(
            held_ref.at[pl.ds(blocks, blocks)],
            pool_ref.at[pl.ds(lay.value_own, blocks)],
            sems.at[3],
        ),
    ]
    for load in loads:
        load.start()
    for load, store in zip(loads, stores):
        load.wait()
        store.start()
    for store in stores:
        store.wait()


def first_kernel(tab_ref, key_ref, value_ref, up_ref, down_ref, over_ref, held_ref, sems, *, lay):
    blocks = lay.blocks
    level = tab_ref[lay.device] >> 1
    loads, stores = [], []
    for k, out in enumerate((up_ref, down_ref, over_ref)):
        code = entry(tab_ref, 0, k)
        at = place_of(code)
        is_value = at >= lay.value_own
        key_at = jnp.clip(at - level * blocks, 0, blocks - 1)
        value_at = jnp.clip(at - lay.value_own, 0, blocks - 1)
        valid = code >= 0
        loads.append((valid & jnp.logical_not(is_value), key_ref.at[key_at], held_ref.at[k]))
        loads.append((valid & is_value, value_ref.at[value_at], held_ref.at[k]))
        stores.append((valid, held_ref.at[k], out))
    copies(loads, sems)
    copies(stores, sems)


def store_arrived(t, tab_ref, arrived, pool_ref, held_ref, sems):
    codes = [entry(tab_ref, t, 3 + k) for k in range(3)]
    copies([(c >= 0, got, held_ref.at[k]) for k, (c, got) in enumerate(zip(codes, arrived))], sems)
    copies(
        [(c >= 0, held_ref.at[k], pool_ref.at[place_of(c)]) for k, c in enumerate(codes)], sems
    )


def take_out(codes, outs, pool_ref, held_ref, sems):
    copies(
        [(c >= 0, pool_ref.at[place_of(c)], held_ref.at[k]) for k, c in enumerate(codes)], sems
    )
    copies([(c >= 0, held_ref.at[k], out) for k, (c, out) in enumerate(zip(codes, outs))], sems)


def step_kernel(
    t_ref, tab_ref, pool_in, in_up, in_down, in_over, pool_ref, up_ref, down_ref, over_ref,
    held_ref, sems,
):
    del pool_in
    t = t_ref[0]
    store_arrived(t - 2, tab_ref, (in_up, in_down, in_over), pool_ref, held_ref, sems)
    codes = [entry(tab_ref, t, k) for k in range(3)]
    take_out(codes, (up_ref, down_ref, over_ref), pool_ref, held_ref, sems)


def close_kernel(t_ref, tab_ref, pool_in, *refs):
    del pool_in
    older, newer, (pool_ref, held_ref, sems) = refs[:3], refs[3:6], refs[6:]
    t = t_ref[0]
    store_arrived(t - 2, tab_ref, older, pool_ref, held_ref, sems)
    store_arrived(t - 1, tab_ref, newer, pool_ref, held_ref, sems)


def traffic(byte_count):
    return pl.CostEstimate(flops=0, bytes_accessed=byte_count, transcendentals=0)


def send_all(sends, perms):
    return tuple(lax.ppermute(s, "ctx", p) for s, p in zip(sends, perms))


def slot_number(t):
    return jnp.full((1,), t, jnp.int32) if isinstance(t, int) else t.reshape(1)


def gather_blocks(keys, values, tab, lay):
    one = jax.ShapeDtypeStruct(keys.shape[1:], keys.dtype)
    pool_shape = jax.ShapeDtypeStruct((lay.places,) + one.shape, one.dtype)
    size = 2 * math.prod(one.shape)
    perms = routes(lay.ctx_size)
    three = [pltpu.VMEM((3,) + one.shape, one.dtype), pltpu.SemaphoreType.DMA((3,))]

    sends = pl.pallas_call(
        functools.partial(first_kernel, lay=lay),
        out_shape=(one,) * 3,
        in_specs=[SMEM, ANY, ANY],
        out_specs=(ANY,) * 3,
        scratch_shapes=[three[0], pltpu.SemaphoreType.DMA((6,))],
        compiler_params=BIG,
        cost_estimate=traffic(size * 6),
        name="gather_first",
    )(tab, keys, values)
    older = send_all(sends, perms)
    pool = pl.pallas_call(
        functools.partial(fill_kernel, lay=lay),
        out_shape=pool_shape,
        in_specs=[SMEM, ANY, ANY],
        out_specs=ANY,
        scratch_shapes=[
            pltpu.VMEM((2 * lay.blocks,) + one.shape, one.dtype),
            pltpu.SemaphoreType.DMA((4,)),
        ],
        compiler_params=BIG,
        cost_estimate=traffic(size * 4 * lay.blocks),
        name="gather_fill",
    )(tab, keys, values)

    def step(t, pool, got):
        pool, *sends = pl.pallas_call(
            step_kernel,
            out_shape=(pool_shape, one, one, one),
            in_specs=[SMEM, SMEM] + [ANY] * 4,
            out_specs=(ANY,) * 4,
            scratch_shapes=three,
            input_output_aliases={2: 0},
            compiler_params=BIG,
            cost_estimate=traffic(size * 12),
            name="gather_step",
        )(slot_number(t), tab, pool, *got)
        return pool, send_all(sends, perms)

    pool, newer = step(1, pool, older)
    for t in range(2, STATIC_SLOTS):
        pool, latest = step(t, pool, older)
        older, newer = newer, latest

    def body(state):
        t, pool, older, newer = state
        pool, latest = step(t, pool, older)
        return t + 1, pool, newer, latest

    t, pool, older, newer = lax.while_loop(
        lambda state: state[0] < tab[lay.total],
        body,
        (jnp.int32(STATIC_SLOTS), pool, older, newer),
    )
    return pl.pallas_call(
        close_kernel,
        out_shape=pool_shape,
        in_specs=[SMEM, SMEM] + [ANY] * 7,
        out_specs=ANY,
        scratch_shapes=three,
        input_output_aliases={2: 0},
        compiler_params=BIG,
        cost_estimate=traffic(size * 12),
        name="gather_close",
    )(slot_number(t), tab, pool, *older, *newer)


def add_back(t, tab_ref, arrived, pool_ref, held_ref, got_ref, sems):
    codes = [entry(tab_ref, t, k) for k in range(3)]
    places = [place_of(c) for c in codes]
    valid = [c >= 0 for c in codes]
    fresh = [c >= FIRST for c in codes]
    jobs = [(v, got, got_ref.at[k]) for k, (v, got) in enumerate(zip(valid, arrived))]
    jobs += [
        (v & jnp.logical_not(f), pool_ref.at[p], held_ref.at[k])
        for k, (v, f, p) in enumerate(zip(valid, fresh, places))
    ]
    copies(jobs, sems)
    as_0 = [False, valid[1] & valid[0] & (places[1] == places[0])]
    as_0.append(valid[2] & valid[0] & (places[2] == places[0]))
    as_1 = valid[2] & valid[1] & (places[2] == places[1]) & jnp.logical_not(as_0[2])
    alone = [
        valid[0],
        valid[1] & jnp.logical_not(as_0[1]),
        valid[2] & jnp.logical_not(as_0[2] | as_1),
    ]
    adds = [(0, 0, alone[0]), (1, 1, alone[1]), (1, 0, as_0[1])]
    adds += [(2, 2, alone[2]), (2, 0, as_0[2]), (2, 1, as_1)]
    for k, at, here in adds:
        if k == at:

            @pl.when(here & fresh[k])
            def _(k=k):
                held_ref[k] = got_ref[k]

            here = here & jnp.logical_not(fresh[k])

        @pl.when(here)
        def _(k=k, at=at):
            held_ref[at] = (
                held_ref[at].astype(jnp.float32) + got_ref[k].astype(jnp.float32)
            ).astype(held_ref.dtype)

    copies(
        [(a, held_ref.at[k], pool_ref.at[p]) for k, (a, p) in enumerate(zip(alone, places))], sems
    )


def back_kernel(
    t_ref, tab_ref, pool_in, in_up, in_down, in_over, pool_ref, up_ref, down_ref, over_ref,
    held_ref, got_ref, sems,
):
    del pool_in
    t = t_ref[0]
    add_back(t + 2, tab_ref, (in_up, in_down, in_over), pool_ref, held_ref, got_ref, sems)
    codes = [entry(tab_ref, t, 3 + k) for k in range(3)]
    take_out(codes, (up_ref, down_ref, over_ref), pool_ref, held_ref, sems)


def home_kernel(tab_ref, pool_in, *refs, lay):
    del pool_in
    older, newer, refs = refs[:3], refs[3:6], refs[6:]
    pool_ref, key_ref, value_ref, held_ref, got_ref, own_ref, sems = refs
    blocks = lay.blocks
    level = tab_ref[lay.device] >> 1
    add_back(1, tab_ref, older, pool_ref, held_ref, got_ref, sems)
    add_back(0, tab_ref, newer, pool_ref, held_ref, got_ref, sems)
    halves = (
        (pool_ref.at[pl.ds(level * blocks, blocks)], key_ref),
        (pool_ref.at[pl.ds(lay.value_own, blocks)], value_ref),
    )
    loads, stores = [], []
    for k, (source, target) in enumerate(halves):
        held = own_ref.at[pl.ds(k * blocks, blocks)]
        loads.append(pltpu.make_async_copy(source, held, sems.at[k]))
        stores.append(pltpu.make_async_copy(held, target, sems.at[2 + k]))
    for load in loads:
        load.start()
    for load, store in zip(loads, stores):
        load.wait()
        store.start()
    for store in stores:
        store.wait()


def return_blocks(pool, tab, lay):
    one = jax.ShapeDtypeStruct(pool.shape[1:], pool.dtype)
    pool_shape = jax.ShapeDtypeStruct(pool.shape, pool.dtype)
    own_shape = jax.ShapeDtypeStruct((lay.blocks,) + one.shape, one.dtype)
    size = 2 * math.prod(one.shape)
    up, down, over = routes(lay.ctx_size)
    perms = ([(b, a) for a, b in up], [(b, a) for a, b in down], over)
    buffers = [pltpu.VMEM((3,) + one.shape, one.dtype)] * 2

    def step(t, pool, got):
        pool, *sends = pl.pallas_call(
            back_kernel,
            out_shape=(pool_shape, one, one, one),
            in_specs=[SMEM, SMEM] + [ANY] * 4,
            out_specs=(ANY,) * 4,
            scratch_shapes=buffers + [pltpu.SemaphoreType.DMA((6,))],
            input_output_aliases={2: 0},
            compiler_params=BIG,
            cost_estimate=traffic(size * 15),
            name="return_step",
        )(slot_number(t), tab, pool, *got)
        return pool, send_all(sends, perms)

    def body(state):
        t, pool, older, newer = state
        pool, latest = step(t, pool, older)
        return t - 1, pool, newer, latest

    nothing = (jnp.zeros(one.shape, one.dtype),) * 3
    _, pool, older, newer = lax.while_loop(
        lambda state: state[0] >= STATIC_SLOTS,
        body,
        (tab[lay.total] - 1, pool, nothing, nothing),
    )
    for t in range(STATIC_SLOTS - 1, -1, -1):
        pool, latest = step(t, pool, older)
        older, newer = newer, latest
    return pl.pallas_call(
        functools.partial(home_kernel, lay=lay),
        out_shape=(pool_shape, own_shape, own_shape),
        in_specs=[SMEM] + [ANY] * 7,
        out_specs=(ANY, ANY, ANY),
        scratch_shapes=buffers
        + [
            pltpu.VMEM((2 * lay.blocks,) + one.shape, one.dtype),
            pltpu.SemaphoreType.DMA((6,)),
        ],
        input_output_aliases={1: 0},
        compiler_params=BIG,
        cost_estimate=traffic(size * 40),
        name="return_home",
    )(tab, pool, *older, *newer)[1:]


QK = (((1,), (1,)), ((), ()))
AB = (((1,), (0,)), ((), ()))
TA = (((0,), (0,)), ((), ()))


def dot(a, b, dims):
    return lax.dot_general(a, b, dims, preferred_element_type=jnp.float32)


def rows_of(i):
    return slice(i * BLOCK, (i + 1) * BLOCK)


def parts_of(i, cols, own_ref, pick_refs):
    blocks = len(pick_refs) - 1
    before = pick_refs[blocks][0, :, cols] if i == 0 else own_ref[i - 1, :, cols]
    return own_ref[i, :, cols], before, pick_refs[i][0, :, cols]


def term_places(tab_ref, lay):
    level = tab_ref[lay.device] >> 1
    result = []
    for base, picks in ((level * lay.blocks, lay.key_picks), (lay.value_own, lay.value_picks)):
        places = [base + o for o in range(lay.blocks)]
        places += [tab_ref[picks + j] for j in range(lay.blocks + 1)]
        result.append(places)
    return result


def forward_kernel(tab_ref, *refs, lay, group):
    blocks = lay.blocks
    count = blocks + 2
    q_ref, key_refs, value_refs = refs[0], refs[1 : 1 + count], refs[1 + count : 1 + 2 * count]
    gain_ref, grad_ref, attended_ref, probs_ref, sums_ref, acc_ref = refs[1 + 2 * count :]
    h = pl.program_id(0)
    causal = lax.broadcasted_iota(jnp.int32, (BLOCK, BLOCK), 1) <= lax.broadcasted_iota(
        jnp.int32, (BLOCK, BLOCK), 0
    )
    hide = jnp.where(tab_ref[lay.device] > 0, 0.0, -jnp.inf).astype(jnp.float32)
    lane = lax.broadcasted_iota(jnp.int32, (BLOCK, LANES), 1)

    @pl.when(h == 0)
    def _():
        acc_ref[...] = jnp.zeros_like(acc_ref)

    for i in range(blocks):
        squares = jnp.zeros((BLOCK, 1), jnp.float32)
        center = jnp.zeros((BLOCK, 1), jnp.float32)
        for g in range(group):
            cols = slice(g * HDIM, (g + 1) * HDIM)
            q = q_ref[rows_of(i), cols]
            scores = [dot(q, k, QK) for k in parts_of(i, cols, key_refs[0], key_refs[1:])]
            scores[0] = jnp.where(causal, scores[0], -jnp.inf)
            if i == 0:
                scores[1] = scores[1] + hide
            top = jnp.max(
                jnp.maximum(jnp.maximum(scores[0], scores[1]), scores[2]), axis=1, keepdims=True
            )
            weights = [jnp.exp2((s - top) * SCALE_LOG2) for s in scores]
            scale = 1.0 / jnp.sum(weights[0] + weights[1] + weights[2], axis=1, keepdims=True)
            attended = 0.0
            values = parts_of(i, cols, value_refs[0], value_refs[1:])
            for j, (w, v) in enumerate(zip(weights, values)):
                low = (w * scale).astype(jnp.bfloat16)
                probs_ref[i, g, :, j * BLOCK : (j + 1) * BLOCK] = low
                attended += dot(low, v, AB)
            attended_ref[rows_of(i), cols] = attended
            lifted = gain_ref[:, cols] * grad_ref[rows_of(i), cols].astype(jnp.float32)
            squares += jnp.sum(attended * attended, axis=1, keepdims=True)
            center += jnp.sum(lifted * attended, axis=1, keepdims=True)
        acc_ref[i] += jnp.where(lane == 0, squares, jnp.where(lane == 1, center, 0.0))

    @pl.when(h == pl.num_programs(0) - 1)
    def _():
        for i in range(blocks):
            sums_ref[:, rows_of(i)] = jnp.transpose(acc_ref[i])[:8]


def backward_kernel(
    tab_ref, q_ref, pool_in, gain_ref, grad_ref, attended_ref, probs_ref, sums_ref,
    normed_ref, gq_ref, pool_ref, rms_ref, acc_ref, out_ref, kv_ref, sems, load_sems,
    *, lay, group,
):
    del pool_in
    blocks = lay.blocks
    h = pl.program_id(0)
    steps = pl.num_programs(0)
    width = group * HDIM
    terms = 2 * blocks + 1
    places = term_places(tab_ref, lay)
    buffer = lax.rem(h, 2)

    def columns(at):
        return pl.ds(pl.multiple_of(at * width, width), width)

    def loads(at, buffer):
        return [
            pltpu.make_async_copy(
                pool_ref.at[places[kind][n], :, columns(at)],
                kv_ref.at[buffer, kind, n],
                load_sems.at[buffer, kind * terms + n],
            )
            for kind in range(2)
            for n in range(terms)
        ]

    @pl.when(h == 0)
    def _():
        for load in loads(0, 0):
            load.start()

    for load in loads(h, buffer):
        load.wait()

    @pl.when(h + 1 < steps)
    def _():
        for load in loads(h + 1, 1 - buffer):
            load.start()

    @pl.when(h == 0)
    def _():
        squares = sums_ref[0:1]
        center = sums_ref[1:2]
        inv = lax.rsqrt(squares / WIDTH + 1e-05)
        factor = inv * inv * inv * center / WIDTH
        both = jnp.concatenate([inv, factor, jnp.zeros((6,) + inv.shape[1:], jnp.float32)], axis=0)
        for i in range(blocks):
            wide = jnp.concatenate([both[:, rows_of(i)]] * (LANES // 8), axis=0)
            rms_ref[i] = jnp.transpose(wide)

    for i in range(blocks):
        inv_rms = rms_ref[i, :, 0:1]
        factor = rms_ref[i, :, 1:2]
        for g in range(group):
            cols = slice(g * HDIM, (g + 1) * HDIM)
            q = q_ref[rows_of(i), cols]
            attended = attended_ref[rows_of(i), cols]
            gain = gain_ref[:, cols]
            normed_ref[rows_of(i), cols] = (attended * inv_rms * gain).astype(jnp.bfloat16)
            lifted = gain * grad_ref[rows_of(i), cols].astype(jnp.float32)
            grad = (inv_rms * lifted - attended * factor).astype(jnp.bfloat16)
            row = jnp.sum(grad.astype(jnp.float32) * attended, axis=1, keepdims=True)
            at = (i, 2 * blocks if i == 0 else i - 1, blocks + i)
            keys = [kv_ref[buffer, 0, n, :, cols] for n in at]
            values = [kv_ref[buffer, 1, n, :, cols] for n in at]
            gq = 0.0
            for j in range(3):
                low = probs_ref[i, g, :, j * BLOCK : (j + 1) * BLOCK]
                gv = dot(low, grad, TA)
                gp = dot(grad, values[j], QK)
                gs = (low.astype(jnp.float32) * (gp - row)).astype(jnp.bfloat16)
                gq += dot(gs, keys[j], AB)
                gk = dot(gs, q, TA) * SCALE
                if j == 1 and i > 0:
                    acc_ref[0, at[j], :, cols] += gk
                    acc_ref[1, at[j], :, cols] += gv
                else:
                    acc_ref[0, at[j], :, cols] = gk
                    acc_ref[1, at[j], :, cols] = gv
            gq_ref[rows_of(i), cols] = (gq * SCALE).astype(jnp.bfloat16)

    jobs = []
    for kind in range(2):
        writes = [steps > 0] * blocks
        for at in range(terms - 1, blocks - 1, -1):
            taken = False
            for to in list(range(blocks)) + list(range(at - 1, blocks - 1, -1)):
                here = (places[kind][at] == places[kind][to]) & jnp.logical_not(taken)
                taken = taken | here

                @pl.when(here)
                def _(kind=kind, at=at, to=to):
                    acc_ref[kind, to] += acc_ref[kind, at]

            writes.insert(blocks, jnp.logical_not(taken))
        for at in range(terms):
            jobs.append((kind, at, places[kind][at], writes[at]))

    def store(n, job, slot_h):
        kind, at, place, valid = job
        return valid, pltpu.make_async_copy(
            out_ref.at[kind, at],
            pool_ref.at[place, :, columns(slot_h)],
            sems.at[n],
        )

    for n, job in enumerate(jobs):
        valid, copy = store(n, job, jnp.maximum(h - 1, 0))
        pl.when(valid & (h > 0))(copy.wait)
    out_ref[...] = acc_ref[...].astype(out_ref.dtype)
    for n, job in enumerate(jobs):
        valid, copy = store(n, job, h)
        pl.when(valid)(copy.start)

    @pl.when(h == steps - 1)
    def _():
        for n, job in enumerate(jobs):
            valid, copy = store(n, job, h)
            pl.when(valid)(copy.wait)


def on_device(queries, key_rows, value_rows, norm_gain, sort_index, grad_normed):
    rows, columns = queries.shape
    blocks = rows // BLOCK
    lay = Layout(lax.axis_size("ctx"), blocks)
    heads = columns // HDIM
    group = 2 if heads % 2 == 0 else 1
    width = group * HDIM
    tab = routing_table(sort_index, lay)
    gain = norm_gain.reshape(1, columns)

    shape3 = (blocks, BLOCK, columns)
    pool = gather_blocks(key_rows.reshape(shape3), value_rows.reshape(shape3), tab, lay)

    row_spec = pl.BlockSpec((rows, width), lambda h, tab: (0, h))
    gain_spec = pl.BlockSpec((1, width), lambda h, tab: (0, h))
    probs_spec = pl.BlockSpec((blocks, group, BLOCK, 3 * BLOCK), lambda h, tab: (0, h, 0, 0))
    sums_spec = pl.BlockSpec((8, rows), lambda h, tab: (0, 0))

    def pick_specs(own, picks):
        specs = [pl.BlockSpec((blocks, BLOCK, width), own)]
        for j in range(blocks + 1):
            specs.append(
                pl.BlockSpec((1, BLOCK, width), lambda h, tab, j=j: (tab[picks + j], 0, h))
            )
        return specs

    pool_specs = pick_specs(lambda h, tab: (tab[lay.device] >> 1, 0, h), lay.key_picks)
    pool_specs += pick_specs(lambda h, tab: (lay.value_own // blocks, 0, h), lay.value_picks)
    common = [row_spec] + pool_specs + [gain_spec, row_spec]
    operands = (queries,) + (pool,) * len(pool_specs) + (gain, grad_normed)

    attended, probs, sums = pl.pallas_call(
        functools.partial(forward_kernel, lay=lay, group=group),
        out_shape=(
            jax.ShapeDtypeStruct((rows, columns), jnp.float32),
            jax.ShapeDtypeStruct((blocks, heads, BLOCK, 3 * BLOCK), jnp.bfloat16),
            jax.ShapeDtypeStruct((8, rows), jnp.float32),
        ),
        grid_spec=pltpu.PrefetchScalarGridSpec(
            num_scalar_prefetch=1,
            grid=(heads // group,),
            in_specs=common,
            out_specs=(row_spec, probs_spec, sums_spec),
            scratch_shapes=[pltpu.VMEM((blocks, BLOCK, LANES), jnp.float32)],
        ),
        compiler_params=BIG,
        cost_estimate=pl.CostEstimate(
            flops=4 * rows * 3 * BLOCK * columns,
            bytes_accessed=50_000_000,
            transcendentals=rows * 3 * BLOCK * heads,
        ),
        name="attention_forward",
    )(tab, *operands)

    sums = lax.psum(sums, "head")

    wide = jax.ShapeDtypeStruct((rows, columns), jnp.bfloat16)
    terms = (2, 2 * blocks + 1, BLOCK, width)
    normed, grad_q, pool = pl.pallas_call(
        functools.partial(backward_kernel, lay=lay, group=group),
        out_shape=(wide, wide, jax.ShapeDtypeStruct(pool.shape, pool.dtype)),
        grid_spec=pltpu.PrefetchScalarGridSpec(
            num_scalar_prefetch=1,
            grid=(heads // group,),
            in_specs=[row_spec, ANY, gain_spec, row_spec, row_spec, probs_spec, sums_spec],
            out_specs=(row_spec, row_spec, ANY),
            scratch_shapes=[
                pltpu.VMEM((blocks, BLOCK, LANES), jnp.float32),
                pltpu.VMEM(terms, jnp.float32),
                pltpu.VMEM(terms, jnp.bfloat16),
                pltpu.VMEM((2,) + terms, jnp.bfloat16),
                pltpu.SemaphoreType.DMA((2 * terms[1],)),
                pltpu.SemaphoreType.DMA((2, 2 * terms[1])),
            ],
        ),
        input_output_aliases={2: 2},
        compiler_params=BIG,
        cost_estimate=pl.CostEstimate(
            flops=8 * rows * 3 * BLOCK * columns,
            bytes_accessed=70_000_000,
            transcendentals=0,
        ),
        name="attention_backward",
    )(tab, queries, pool, gain, grad_normed, attended, probs, sums)
    grad_k, grad_v = return_blocks(pool, tab, lay)
    return normed, grad_q, grad_k.reshape(rows, columns), grad_v.reshape(rows, columns)


def solution(mesh):
    in_specs = (
        P("ctx", "head"),
        P("ctx", "head"),
        P("ctx", "head"),
        P("head"),
        P(),
        P("ctx", "head"),
    )
    out_specs = (P("ctx", "head"), P("ctx", "head"), P("ctx", "head"), P("ctx", "head"))
    return jax.shard_map(
        on_device, mesh=mesh, in_specs=in_specs, out_specs=out_specs, check_vma=False
    )
```

```python
import functools
import math

import jax
import jax.numpy as jnp
import numpy as np
from jax import lax
from jax.experimental import pallas as pl
from jax.experimental.pallas import tpu as pltpu
from jax.sharding import PartitionSpec as P

HDIM = 128
BLOCK = 256
WIDTH = 5120
LANES = 128
ROW = 16
LEAD = 2
FIRST = 1024
STATIC_SLOTS = 9
SCALE = HDIM ** (-0.5)
SCALE_LOG2 = SCALE * math.log2(math.e)
ANY = pl.BlockSpec(memory_space=pl.ANY)
SMEM = pl.BlockSpec(memory_space=pltpu.SMEM)
VMEM = pl.BlockSpec(memory_space=pltpu.VMEM)
BIG = pltpu.CompilerParams(vmem_limit_bytes=56 * 1024 * 1024)


class Layout:
    def __init__(self, ctx_size, blocks):
        self.ctx_size = ctx_size
        self.blocks = blocks
        self.levels = ctx_size // 2
        line = self.levels * blocks
        self.value_line = line
        self.value_own = 2 * line
        self.over = 2 * line + blocks
        self.places = self.over + 2 * (blocks + 1)
        self.slots = 2 * (2 * line + 2 * self.levels + 2 * blocks + 4)
        self.rows = self.slots + 2 * LEAD
        self.info = self.rows * ROW
        self.key_picks = self.info
        self.value_picks = self.info + blocks + 1
        self.total = self.info + 2 * blocks + 2
        self.device = self.info + 2 * blocks + 3


def shift_rows(array, count, rows):
    n = array.shape[0]
    if abs(count) >= n:
        return jnp.zeros_like(array)
    rolled = pltpu.roll(array, (-count) % n, 0)
    inside = (rows < n - count) if count > 0 else (rows >= -count)
    return jnp.where(inside, rolled, 0.0)


def table_kernel(picks_ref, out_ref, *, lay):
    n = lay.ctx_size
    blocks = lay.blocks
    count = n * blocks
    width = -(-2 * count // LANES) * LANES
    rows = lax.broadcasted_iota(jnp.int32, (n, width), 0)
    lanes = lax.broadcasted_iota(jnp.int32, (n, width), 1)
    out_lanes = lax.broadcasted_iota(jnp.int32, (n, LANES), 1)
    values = lanes >= count
    block = jnp.where(lanes >= 2 * count, -2, jnp.where(values, lanes - count, lanes))
    owner = jnp.floor((block.astype(jnp.float32) + 0.5) / blocks).astype(jnp.int32)
    within = block - owner * blocks
    line = (owner >> 1) * blocks + within
    place = jnp.where(values, jnp.where(owner == rows, lay.value_own + within, lay.value_line + line), line)
    place = jnp.where(block < 0, 0, place).astype(jnp.float32)
    picks = picks_ref[...]
    side = rows & 1
    level = rows >> 1
    same_side = side == (owner & 1)
    travels = jnp.logical_xor(same_side, values)
    owned = owner == rows

    def other(array):
        return jnp.where(side == 0, pltpu.roll(array, n - 1, 0), pltpu.roll(array, 1, 0))

    need = jnp.zeros((n, width), jnp.float32)
    for j in range(blocks + 1):
        need = jnp.where(picks[:, j : j + 1] == block, 1.0, need)
    need = jnp.where(owned, 0.0, need)
    across = other(need)
    wanted = jnp.maximum(need, across)
    final = jnp.where(travels, across, 0.0)
    hops = jnp.where(wanted > 0, 1.0 + final, 0.0)
    up_hops = jnp.zeros_like(need)
    down_hops = jnp.zeros_like(need)
    for k in range(1, lay.levels):
        above = shift_rows(hops, 2 * k, rows)
        below = shift_rows(hops, -2 * k, rows)
        up_hops = jnp.maximum(up_hops, jnp.where(above > 0, above + (k - 1), 0.0))
        down_hops = jnp.maximum(down_hops, jnp.where(below > 0, below + (k - 1), 0.0))
    up = jnp.where(travels & (level >= (owner >> 1)) & (up_hops > 0), 1.0, 0.0)
    down = jnp.where(travels & (level <= (owner >> 1)) & (down_hops > 0), 1.0, 0.0)
    source = owned & jnp.logical_not(travels)
    most = jnp.maximum(up_hops, down_hops)
    over = jnp.where(source & ((most > 0) | (across > 0)), 1.0, final)
    spread = jnp.minimum(jnp.sum(need, axis=0, keepdims=True), 3.0)
    low = (width - 1 - lanes).astype(jnp.float32)
    up_rank = (up_hops * 4.0 + spread) * width + low
    down_rank = (down_hops * 4.0 + spread) * width + low
    over_rank = jnp.where(source, most * 4.0 + spread, 2.0) * width + low
    first_over = float(lay.over)

    out_ref[...] = jnp.full(out_ref.shape, -1, jnp.int32)

    def pick(pending, have, rank):
        score = jnp.where(pending * have > 0, rank, -1.0)
        best = jnp.max(score, axis=1, keepdims=True)
        return jnp.where((score == best) & (best >= 0), 1.0, 0.0)

    def where(chosen):
        return jnp.sum(chosen * (place + 1.0), axis=1, keepdims=True) - 1.0

    def pending(state):
        t, have, fresh, up, down, over, over_place, count = state
        return (t < lay.slots) & (jnp.sum(up + down + over) > 0)

    def step(state):
        t, have, fresh, up, down, over, over_place, count = state
        send_up = pick(up, have, up_rank)
        send_down = pick(down, have, down_rank)
        send_over = pick(over, have, over_rank)
        up = up - send_up
        down = down - send_down
        over = over - send_over
        got_up = shift_rows(send_up, -2, rows)
        got_down = shift_rows(send_down, 2, rows)
        got_over = other(send_over)
        got_final = jnp.where(travels, 0.0, got_over)
        any_final = jnp.max(got_final, axis=1, keepdims=True)
        over_at = jnp.where(any_final > 0, count + first_over, where(got_over))
        last = jnp.where((up + down + over + need > 0) | owned, 0.0, float(FIRST))

        def first_back(chosen):
            return jnp.max(chosen * last, axis=1, keepdims=True)

        columns = (
            where(send_up) + first_back(send_up),
            where(send_down) + first_back(send_down * (1.0 - send_up)),
            where(send_over) + first_back(send_over * (1.0 - send_up) * (1.0 - send_down)),
            where(got_up),
            where(got_down),
            over_at,
        )
        row = jnp.full((n, LANES), -1.0, jnp.float32)
        for k, column in enumerate(columns):
            row = jnp.where(out_lanes == k, column, row)
        out_ref[t + LEAD] = row.astype(jnp.int32)
        over_place = jnp.where(got_final > 0, count + first_over, over_place)
        have = jnp.maximum(have, fresh)
        fresh = jnp.maximum(got_up, jnp.maximum(got_down, got_over))
        return (t + 1, have, fresh, up, down, over, over_place, count + any_final)

    zeros = jnp.zeros_like(need)
    have = jnp.where(owned, 1.0, 0.0)
    state = (jnp.int32(0), have, zeros, up, down, over, zeros, jnp.zeros((n, 1), jnp.float32))
    state = lax.while_loop(pending, step, state)
    at = jnp.where(travels | owned, place, state[6])
    own_row = lax.broadcasted_iota(jnp.int32, (n, LANES), 0)
    row = jnp.zeros((n, LANES), jnp.float32)
    for kind in range(2):
        base = (own_row >> 1) * blocks if kind == 0 else jnp.full((n, LANES), lay.value_own)
        for j in range(blocks + 1):
            chosen = (picks[:, j : j + 1] == block) & (values if kind else jnp.logical_not(values))
            found = jnp.sum(jnp.where(chosen, at, 0.0), axis=1, keepdims=True)
            found = jnp.where(picks[:, j : j + 1] < 0, base[:, :1].astype(jnp.float32), found)
            row = jnp.where(out_lanes == kind * (blocks + 1) + j, found, row)
    row = jnp.where(out_lanes == 2 * blocks + 2, state[0].astype(jnp.float32), row)
    row = jnp.where(out_lanes == 2 * blocks + 3, own_row.astype(jnp.float32), row)
    out_ref[lay.rows] = row.astype(jnp.int32)


def routing_table(sort_index, lay):
    n, blocks = lay.ctx_size, lay.blocks
    before = (np.arange(n, dtype=np.int32) * blocks - 1)[:, None]
    picks = jnp.concatenate([sort_index.reshape(n, blocks), jnp.asarray(before)], axis=1)
    picks = jnp.pad(picks, ((0, 0), (0, LANES - blocks - 1)), constant_values=-1)
    table = pl.pallas_call(
        functools.partial(table_kernel, lay=lay),
        out_shape=jax.ShapeDtypeStruct((lay.rows + 1, n, LANES), jnp.int32),
        in_specs=[VMEM],
        out_specs=VMEM,
        name="routing_table",
    )(picks)
    mine = lax.dynamic_slice(table, (0, lax.axis_index("ctx"), 0), (lay.rows + 1, 1, ROW))
    return mine.reshape((lay.rows + 1) * ROW)


def routes(ctx_size):
    up = [(d, d + 2) for d in range(ctx_size - 2)]
    down = [(d + 2, d) for d in range(ctx_size - 2)]
    over = [(d, d ^ 1) for d in range(ctx_size)]
    return up, down, over


def copies(jobs, sems):
    started = []
    for k, (valid, source, target) in enumerate(jobs):
        copy = pltpu.make_async_copy(source, target, sems.at[k])
        pl.when(valid)(copy.start)
        started.append((valid, copy))
    for valid, copy in started:
        pl.when(valid)(copy.wait)


def entry(tab_ref, t, k):
    return tab_ref[(t + LEAD) * ROW + k]


def place_of(code):
    return jnp.maximum(code, 0) & (FIRST - 1)


def fill_kernel(tab_ref, key_ref, value_ref, pool_ref, held_ref, sems, *, lay):
    blocks = lay.blocks
    level = tab_ref[lay.device] >> 1
    loads = [
        pltpu.make_async_copy(key_ref, held_ref.at[pl.ds(0, blocks)], sems.at[0]),
        pltpu.make_async_copy(value_ref, held_ref.at[pl.ds(blocks, blocks)], sems.at[1]),
    ]
    stores = [
        pltpu.make_async_copy(
            held_ref.at[pl.ds(0, blocks)], pool_ref.at[pl.ds(level * blocks, blocks)], sems.at[2]
        ),
        pltpu.make_async_copy(
            held_ref.at[pl.ds(blocks, blocks)],
            pool_ref.at[pl.ds(lay.value_own, blocks)],
            sems.at[3],
        ),
    ]
    for load in loads:
        load.start()
    for load, store in zip(loads, stores):
        load.wait()
        store.start()
    for store in stores:
        store.wait()


def first_kernel(
    tab_ref, key_ref, value_ref, up_ref, down_ref, over_ref, held_ref, sems, *, lay, slot
):
    blocks = lay.blocks
    level = tab_ref[lay.device] >> 1
    loads, stores = [], []
    for k, out in enumerate((up_ref, down_ref, over_ref)):
        code = entry(tab_ref, slot, k)
        at = place_of(code)
        is_value = at >= lay.value_own
        key_at = jnp.clip(at - level * blocks, 0, blocks - 1)
        value_at = jnp.clip(at - lay.value_own, 0, blocks - 1)
        valid = code >= 0
        loads.append((valid & jnp.logical_not(is_value), key_ref.at[key_at], held_ref.at[k]))
        loads.append((valid & is_value, value_ref.at[value_at], held_ref.at[k]))
        stores.append((valid, held_ref.at[k], out))
    copies(loads, sems)
    copies(stores, sems)


def match(place, valid, places, valids):
    hits = [valid & v & (place == p) for p, v in zip(places, valids)]
    found = hits[0] | hits[1] | hits[2]
    return found, jnp.where(hits[0], 0, jnp.where(hits[1], 1, 2))


def step_kernel(
    t_ref, tab_ref, pool_in, in_up, in_down, in_over, pool_ref, up_ref, down_ref, over_ref,
    held_ref, sems,
):
    del pool_in
    t = t_ref[0]
    got_codes = [entry(tab_ref, t - 2, 3 + k) for k in range(3)]
    got_valid = [c >= 0 for c in got_codes]
    got_places = [place_of(c) for c in got_codes]
    loads = [
        (v, got, held_ref.at[k])
        for k, (v, got) in enumerate(zip(got_valid, (in_up, in_down, in_over)))
    ]
    stores = [
        (v, held_ref.at[k], pool_ref.at[p])
        for k, (v, p) in enumerate(zip(got_valid, got_places))
    ]
    for k, out in enumerate((up_ref, down_ref, over_ref)):
        code = entry(tab_ref, t, k)
        valid = code >= 0
        place = place_of(code)
        found, at = match(place, valid, got_places, got_valid)
        loads.append((valid & jnp.logical_not(found), pool_ref.at[place], held_ref.at[3 + k]))
        stores.append((valid, held_ref.at[jnp.where(found, at, 3 + k)], out))
    copies(loads, sems)
    copies(stores, sems)


def close_kernel(t_ref, tab_ref, pool_in, *refs):
    del pool_in
    arrived, (pool_ref, held_ref, sems) = refs[:6], refs[6:]
    t = t_ref[0]
    loads, stores = [], []
    for n, got in enumerate(arrived):
        code = entry(tab_ref, t - 2 + n // 3, 3 + n % 3)
        loads.append((code >= 0, got, held_ref.at[n]))
        stores.append((code >= 0, held_ref.at[n], pool_ref.at[place_of(code)]))
    copies(loads, sems)
    copies(stores, sems)


def traffic(byte_count):
    return pl.CostEstimate(flops=0, bytes_accessed=byte_count, transcendentals=0)


def send_all(sends, perms):
    return tuple(lax.ppermute(s, "ctx", p) for s, p in zip(sends, perms))


def slot_number(t):
    return jnp.full((1,), t, jnp.int32) if isinstance(t, int) else t.reshape(1)


def gather_blocks(keys, values, tab, lay):
    one = jax.ShapeDtypeStruct(keys.shape[1:], keys.dtype)
    pool_shape = jax.ShapeDtypeStruct((lay.places,) + one.shape, one.dtype)
    size = 2 * math.prod(one.shape)
    perms = routes(lay.ctx_size)
    six = [pltpu.VMEM((6,) + one.shape, one.dtype), pltpu.SemaphoreType.DMA((6,))]

    def first(slot):
        sends = pl.pallas_call(
            functools.partial(first_kernel, lay=lay, slot=slot),
            out_shape=(one,) * 3,
            in_specs=[SMEM, ANY, ANY],
            out_specs=(ANY,) * 3,
            scratch_shapes=six,
            compiler_params=BIG,
            cost_estimate=traffic(size * 6),
            name="gather_first",
        )(tab, keys, values)
        return send_all(sends, perms)

    older = first(0)
    newer = first(1)
    pool = pl.pallas_call(
        functools.partial(fill_kernel, lay=lay),
        out_shape=pool_shape,
        in_specs=[SMEM, ANY, ANY],
        out_specs=ANY,
        scratch_shapes=[
            pltpu.VMEM((2 * lay.blocks,) + one.shape, one.dtype),
            pltpu.SemaphoreType.DMA((4,)),
        ],
        compiler_params=BIG,
        cost_estimate=traffic(size * 4 * lay.blocks),
        name="gather_fill",
    )(tab, keys, values)

    def step(t, pool, got):
        pool, *sends = pl.pallas_call(
            step_kernel,
            out_shape=(pool_shape, one, one, one),
            in_specs=[SMEM, SMEM] + [ANY] * 4,
            out_specs=(ANY,) * 4,
            scratch_shapes=six,
            input_output_aliases={2: 0},
            compiler_params=BIG,
            cost_estimate=traffic(size * 12),
            name="gather_step",
        )(slot_number(t), tab, pool, *got)
        return pool, send_all(sends, perms)

    for t in range(2, STATIC_SLOTS):
        pool, latest = step(t, pool, older)
        older, newer = newer, latest

    def body(state):
        t, pool, older, newer = state
        pool, latest = step(t, pool, older)
        return t + 1, pool, newer, latest

    t, pool, older, newer = lax.while_loop(
        lambda state: state[0] < tab[lay.total],
        body,
        (jnp.int32(STATIC_SLOTS), pool, older, newer),
    )
    return pl.pallas_call(
        close_kernel,
        out_shape=pool_shape,
        in_specs=[SMEM, SMEM] + [ANY] * 7,
        out_specs=ANY,
        scratch_shapes=six,
        input_output_aliases={2: 0},
        compiler_params=BIG,
        cost_estimate=traffic(size * 12),
        name="gather_close",
    )(slot_number(t), tab, pool, *older, *newer)


def add(target_ref, to, source_ref, at):
    target_ref[to] = (
        target_ref[to].astype(jnp.float32) + source_ref[at].astype(jnp.float32)
    ).astype(target_ref.dtype)


def back_kernel(
    t_ref, tab_ref, pool_in, in_up, in_down, in_over, pool_ref, up_ref, down_ref, over_ref,
    held_ref, got_ref, sems,
):
    del pool_in
    t = t_ref[0]
    codes = [entry(tab_ref, t + 2, k) for k in range(3)]
    places = [place_of(c) for c in codes]
    valid = [c >= 0 for c in codes]
    fresh = [c >= FIRST for c in codes]
    same_10 = valid[1] & valid[0] & (places[1] == places[0])
    same_20 = valid[2] & valid[0] & (places[2] == places[0])
    same_21 = valid[2] & valid[1] & (places[2] == places[1]) & jnp.logical_not(same_20)
    alone = [
        valid[0],
        valid[1] & jnp.logical_not(same_10),
        valid[2] & jnp.logical_not(same_20 | same_21),
    ]
    loads = [
        (v, got, got_ref.at[k]) for k, (v, got) in enumerate(zip(valid, (in_up, in_down, in_over)))
    ]
    loads += [
        (a & jnp.logical_not(f), pool_ref.at[p], held_ref.at[k])
        for k, (a, f, p) in enumerate(zip(alone, fresh, places))
    ]
    stores = []
    leaves = [False] * 3
    for k, out in enumerate((up_ref, down_ref, over_ref)):
        code = entry(tab_ref, t, 3 + k)
        takes = code >= 0
        place = place_of(code)
        found, at = match(place, takes, places, alone)
        loads.append((takes & jnp.logical_not(found), pool_ref.at[place], held_ref.at[3 + k]))
        stores.append((takes, held_ref.at[jnp.where(found, at, 3 + k)], out))
        leaves = [leave | (found & (at == n)) for n, leave in enumerate(leaves)]
    copies(loads, sems)
    for k in range(3):

        @pl.when(alone[k] & fresh[k])
        def _(k=k):
            held_ref[k] = got_ref[k]

        @pl.when(alone[k] & jnp.logical_not(fresh[k]))
        def _(k=k):
            add(held_ref, k, got_ref, k)

    for k, to, here in ((1, 0, same_10), (2, 0, same_20), (2, 1, same_21)):

        @pl.when(here)
        def _(k=k, to=to):
            add(held_ref, to, got_ref, k)

    stores += [
        (a & jnp.logical_not(leave), held_ref.at[k], pool_ref.at[p])
        for k, (a, leave, p) in enumerate(zip(alone, leaves, places))
    ]
    copies(stores, sems)


def home_kernel(tab_ref, pool_ref, *refs, lay):
    arrived, (key_ref, value_ref, own_ref, got_ref, sems) = refs[:6], refs[6:]
    blocks = lay.blocks
    level = tab_ref[lay.device] >> 1
    halves = (
        (pool_ref.at[pl.ds(level * blocks, blocks)], key_ref),
        (pool_ref.at[pl.ds(lay.value_own, blocks)], value_ref),
    )
    loads, stores = [], []
    for k, (source, target) in enumerate(halves):
        held = own_ref.at[pl.ds(k * blocks, blocks)]
        loads.append((level >= 0, source, held))
        stores.append((level >= 0, held, target))
    codes = [entry(tab_ref, 1 - n // 3, n % 3) for n in range(6)]
    for n, (code, got) in enumerate(zip(codes, arrived)):
        loads.append((code >= 0, got, got_ref.at[n]))
    copies(loads, sems)
    for n, code in enumerate(codes):
        place = place_of(code)
        at = jnp.where(
            place >= lay.value_own, place - lay.value_own + blocks, place - level * blocks
        )

        @pl.when(code >= 0)
        def _(n=n, at=at):
            add(own_ref, jnp.clip(at, 0, 2 * blocks - 1), got_ref, n)

    copies(stores, sems)


def return_blocks(pool, tab, lay):
    one = jax.ShapeDtypeStruct(pool.shape[1:], pool.dtype)
    pool_shape = jax.ShapeDtypeStruct(pool.shape, pool.dtype)
    own_shape = jax.ShapeDtypeStruct((lay.blocks,) + one.shape, one.dtype)
    size = 2 * math.prod(one.shape)
    up, down, over = routes(lay.ctx_size)
    perms = ([(b, a) for a, b in up], [(b, a) for a, b in down], over)

    def step(t, pool, got):
        pool, *sends = pl.pallas_call(
            back_kernel,
            out_shape=(pool_shape, one, one, one),
            in_specs=[SMEM, SMEM] + [ANY] * 4,
            out_specs=(ANY,) * 4,
            scratch_shapes=[
                pltpu.VMEM((6,) + one.shape, one.dtype),
                pltpu.VMEM((3,) + one.shape, one.dtype),
                pltpu.SemaphoreType.DMA((9,)),
            ],
            input_output_aliases={2: 0},
            compiler_params=BIG,
            cost_estimate=traffic(size * 15),
            name="return_step",
        )(slot_number(t), tab, pool, *got)
        return pool, send_all(sends, perms)

    def body(state):
        t, pool, older, newer = state
        pool, latest = step(t, pool, older)
        return t - 1, pool, newer, latest

    nothing = (jnp.zeros(one.shape, one.dtype),) * 3
    _, pool, older, newer = lax.while_loop(
        lambda state: state[0] >= STATIC_SLOTS,
        body,
        (tab[lay.total] - 1, pool, nothing, nothing),
    )
    for t in range(STATIC_SLOTS - 1, -1, -1):
        pool, latest = step(t, pool, older)
        older, newer = newer, latest
    return pl.pallas_call(
        functools.partial(home_kernel, lay=lay),
        out_shape=(own_shape, own_shape),
        in_specs=[SMEM] + [ANY] * 7,
        out_specs=(ANY, ANY),
        scratch_shapes=[
            pltpu.VMEM((2 * lay.blocks,) + one.shape, one.dtype),
            pltpu.VMEM((6,) + one.shape, one.dtype),
            pltpu.SemaphoreType.DMA((8,)),
        ],
        compiler_params=BIG,
        cost_estimate=traffic(size * 30),
        name="return_home",
    )(tab, pool, *older, *newer)


QK = (((1,), (1,)), ((), ()))
AB = (((1,), (0,)), ((), ()))
TA = (((0,), (0,)), ((), ()))


def dot(a, b, dims):
    return lax.dot_general(a, b, dims, preferred_element_type=jnp.float32)


def rows_of(i):
    return slice(i * BLOCK, (i + 1) * BLOCK)


def parts_of(i, cols, own_ref, pick_refs):
    blocks = len(pick_refs) - 1
    before = pick_refs[blocks][0, :, cols] if i == 0 else own_ref[i - 1, :, cols]
    return own_ref[i, :, cols], before, pick_refs[i][0, :, cols]


def term_places(tab_ref, lay):
    level = tab_ref[lay.device] >> 1
    result = []
    for base, picks in ((level * lay.blocks, lay.key_picks), (lay.value_own, lay.value_picks)):
        places = [base + o for o in range(lay.blocks)]
        places += [tab_ref[picks + j] for j in range(lay.blocks + 1)]
        result.append(places)
    return result


def forward_kernel(tab_ref, *refs, lay, group):
    blocks = lay.blocks
    count = blocks + 2
    q_ref, key_refs, value_refs = refs[0], refs[1 : 1 + count], refs[1 + count : 1 + 2 * count]
    gain_ref, grad_ref, attended_ref, probs_ref, sums_ref, acc_ref = refs[1 + 2 * count :]
    h = pl.program_id(0)
    causal = lax.broadcasted_iota(jnp.int32, (BLOCK, BLOCK), 1) <= lax.broadcasted_iota(
        jnp.int32, (BLOCK, BLOCK), 0
    )
    hide = jnp.where(tab_ref[lay.device] > 0, 0.0, -jnp.inf).astype(jnp.float32)
    lane = lax.broadcasted_iota(jnp.int32, (BLOCK, LANES), 1)

    @pl.when(h == 0)
    def _():
        acc_ref[...] = jnp.zeros_like(acc_ref)

    for i in range(blocks):
        squares = jnp.zeros((BLOCK, 1), jnp.float32)
        center = jnp.zeros((BLOCK, 1), jnp.float32)
        for g in range(group):
            cols = slice(g * HDIM, (g + 1) * HDIM)
            q = q_ref[rows_of(i), cols]
            scores = [dot(q, k, QK) for k in parts_of(i, cols, key_refs[0], key_refs[1:])]
            scores[0] = jnp.where(causal, scores[0], -jnp.inf)
            if i == 0:
                scores[1] = scores[1] + hide
            top = jnp.max(
                jnp.maximum(jnp.maximum(scores[0], scores[1]), scores[2]), axis=1, keepdims=True
            )
            weights = [jnp.exp2((s - top) * SCALE_LOG2) for s in scores]
            scale = 1.0 / jnp.sum(weights[0] + weights[1] + weights[2], axis=1, keepdims=True)
            attended = 0.0
            values = parts_of(i, cols, value_refs[0], value_refs[1:])
            for j, (w, v) in enumerate(zip(weights, values)):
                low = (w * scale).astype(jnp.bfloat16)
                probs_ref[i, g, :, j * BLOCK : (j + 1) * BLOCK] = low
                attended += dot(low, v, AB)
            attended_ref[rows_of(i), cols] = attended
            lifted = gain_ref[:, cols] * grad_ref[rows_of(i), cols].astype(jnp.float32)
            squares += jnp.sum(attended * attended, axis=1, keepdims=True)
            center += jnp.sum(lifted * attended, axis=1, keepdims=True)
        acc_ref[i] += jnp.where(lane == 0, squares, jnp.where(lane == 1, center, 0.0))

    @pl.when(h == pl.num_programs(0) - 1)
    def _():
        for i in range(blocks):
            sums_ref[:, rows_of(i)] = jnp.transpose(acc_ref[i])[:8]


def backward_kernel(
    tab_ref, q_ref, pool_in, gain_ref, grad_ref, attended_ref, probs_ref, sums_ref,
    normed_ref, gq_ref, pool_ref, rms_ref, acc_ref, out_ref, kv_ref, sems, load_sems,
    *, lay, group,
):
    del pool_in
    blocks = lay.blocks
    h = pl.program_id(0)
    steps = pl.num_programs(0)
    width = group * HDIM
    terms = 2 * blocks + 1
    places = term_places(tab_ref, lay)
    buffer = lax.rem(h, 2)

    def columns(at):
        return pl.ds(pl.multiple_of(at * width, width), width)

    def loads(at, buffer):
        return [
            pltpu.make_async_copy(
                pool_ref.at[places[kind][n], :, columns(at)],
                kv_ref.at[buffer, kind, n],
                load_sems.at[buffer, kind * terms + n],
            )
            for kind in range(2)
            for n in range(terms)
        ]

    @pl.when(h == 0)
    def _():
        for load in loads(0, 0):
            load.start()

    for load in loads(h, buffer):
        load.wait()

    @pl.when(h + 1 < steps)
    def _():
        for load in loads(h + 1, 1 - buffer):
            load.start()

    @pl.when(h == 0)
    def _():
        squares = sums_ref[0:1]
        center = sums_ref[1:2]
        inv = lax.rsqrt(squares / WIDTH + 1e-05)
        factor = inv * inv * inv * center / WIDTH
        both = jnp.concatenate([inv, factor, jnp.zeros((6,) + inv.shape[1:], jnp.float32)], axis=0)
        for i in range(blocks):
            wide = jnp.concatenate([both[:, rows_of(i)]] * (LANES // 8), axis=0)
            rms_ref[i] = jnp.transpose(wide)

    for i in range(blocks):
        inv_rms = rms_ref[i, :, 0:1]
        factor = rms_ref[i, :, 1:2]
        for g in range(group):
            cols = slice(g * HDIM, (g + 1) * HDIM)
            q = q_ref[rows_of(i), cols]
            attended = attended_ref[rows_of(i), cols]
            gain = gain_ref[:, cols]
            normed_ref[rows_of(i), cols] = (attended * inv_rms * gain).astype(jnp.bfloat16)
            lifted = gain * grad_ref[rows_of(i), cols].astype(jnp.float32)
            grad = (inv_rms * lifted - attended * factor).astype(jnp.bfloat16)
            row = jnp.sum(grad.astype(jnp.float32) * attended, axis=1, keepdims=True)
            at = (i, 2 * blocks if i == 0 else i - 1, blocks + i)
            keys = [kv_ref[buffer, 0, n, :, cols] for n in at]
            values = [kv_ref[buffer, 1, n, :, cols] for n in at]
            gq = 0.0
            for j in range(3):
                low = probs_ref[i, g, :, j * BLOCK : (j + 1) * BLOCK]
                gv = dot(low, grad, TA)
                gp = dot(grad, values[j], QK)
                gs = (low.astype(jnp.float32) * (gp - row)).astype(jnp.bfloat16)
                gq += dot(gs, keys[j], AB)
                gk = dot(gs, q, TA) * SCALE
                if j == 1 and i > 0:
                    acc_ref[0, at[j], :, cols] += gk
                    acc_ref[1, at[j], :, cols] += gv
                else:
                    acc_ref[0, at[j], :, cols] = gk
                    acc_ref[1, at[j], :, cols] = gv
            gq_ref[rows_of(i), cols] = (gq * SCALE).astype(jnp.bfloat16)

    jobs = []
    for kind in range(2):
        writes = [steps > 0] * blocks
        for at in range(terms - 1, blocks - 1, -1):
            taken = False
            for to in list(range(blocks)) + list(range(at - 1, blocks - 1, -1)):
                here = (places[kind][at] == places[kind][to]) & jnp.logical_not(taken)
                taken = taken | here

                @pl.when(here)
                def _(kind=kind, at=at, to=to):
                    acc_ref[kind, to] += acc_ref[kind, at]

            writes.insert(blocks, jnp.logical_not(taken))
        for at in range(terms):
            jobs.append((kind, at, places[kind][at], writes[at]))

    def store(n, job, slot_h):
        kind, at, place, valid = job
        return valid, pltpu.make_async_copy(
            out_ref.at[kind, at],
            pool_ref.at[place, :, columns(slot_h)],
            sems.at[n],
        )

    for n, job in enumerate(jobs):
        valid, copy = store(n, job, jnp.maximum(h - 1, 0))
        pl.when(valid & (h > 0))(copy.wait)
    out_ref[...] = acc_ref[...].astype(out_ref.dtype)
    for n, job in enumerate(jobs):
        valid, copy = store(n, job, h)
        pl.when(valid)(copy.start)

    @pl.when(h == steps - 1)
    def _():
        for n, job in enumerate(jobs):
            valid, copy = store(n, job, h)
            pl.when(valid)(copy.wait)


def attention(queries, pool, gain, grad_normed, tab, lay):
    rows, columns = queries.shape
    blocks = lay.blocks
    heads = columns // HDIM
    group = 2 if heads % 2 == 0 else 1
    width = group * HDIM
    row_spec = pl.BlockSpec((rows, width), lambda h, tab: (0, h))
    gain_spec = pl.BlockSpec((1, width), lambda h, tab: (0, h))
    probs_spec = pl.BlockSpec((blocks, group, BLOCK, 3 * BLOCK), lambda h, tab: (0, h, 0, 0))
    sums_spec = pl.BlockSpec((8, rows), lambda h, tab: (0, 0))

    def pick_specs(own, picks):
        specs = [pl.BlockSpec((blocks, BLOCK, width), own)]
        for j in range(blocks + 1):
            specs.append(
                pl.BlockSpec((1, BLOCK, width), lambda h, tab, j=j: (tab[picks + j], 0, h))
            )
        return specs

    pool_specs = pick_specs(lambda h, tab: (tab[lay.device] >> 1, 0, h), lay.key_picks)
    pool_specs += pick_specs(lambda h, tab: (lay.value_own // blocks, 0, h), lay.value_picks)
    common = [row_spec] + pool_specs + [gain_spec, row_spec]
    operands = (queries,) + (pool,) * len(pool_specs) + (gain, grad_normed)

    attended, probs, sums = pl.pallas_call(
        functools.partial(forward_kernel, lay=lay, group=group),
        out_shape=(
            jax.ShapeDtypeStruct((rows, columns), jnp.float32),
            jax.ShapeDtypeStruct((blocks, heads, BLOCK, 3 * BLOCK), jnp.bfloat16),
            jax.ShapeDtypeStruct((8, rows), jnp.float32),
        ),
        grid_spec=pltpu.PrefetchScalarGridSpec(
            num_scalar_prefetch=1,
            grid=(heads // group,),
            in_specs=common,
            out_specs=(row_spec, probs_spec, sums_spec),
            scratch_shapes=[pltpu.VMEM((blocks, BLOCK, LANES), jnp.float32)],
        ),
        compiler_params=BIG,
        cost_estimate=pl.CostEstimate(
            flops=4 * rows * 3 * BLOCK * columns,
            bytes_accessed=50_000_000,
            transcendentals=rows * 3 * BLOCK * heads,
        ),
        name="attention_forward",
    )(tab, *operands)

    sums = lax.psum(sums, "head")

    wide = jax.ShapeDtypeStruct((rows, columns), jnp.bfloat16)
    terms = (2, 2 * blocks + 1, BLOCK, width)
    normed, grad_q, pool = pl.pallas_call(
        functools.partial(backward_kernel, lay=lay, group=group),
        out_shape=(wide, wide, jax.ShapeDtypeStruct(pool.shape, pool.dtype)),
        grid_spec=pltpu.PrefetchScalarGridSpec(
            num_scalar_prefetch=1,
            grid=(heads // group,),
            in_specs=[row_spec, ANY, gain_spec, row_spec, row_spec, probs_spec, sums_spec],
            out_specs=(row_spec, row_spec, ANY),
            scratch_shapes=[
                pltpu.VMEM((blocks, BLOCK, LANES), jnp.float32),
                pltpu.VMEM(terms, jnp.float32),
                pltpu.VMEM(terms, jnp.bfloat16),
                pltpu.VMEM((2,) + terms, jnp.bfloat16),
                pltpu.SemaphoreType.DMA((2 * terms[1],)),
                pltpu.SemaphoreType.DMA((2, 2 * terms[1])),
            ],
        ),
        input_output_aliases={2: 2},
        compiler_params=BIG,
        cost_estimate=pl.CostEstimate(
            flops=8 * rows * 3 * BLOCK * columns,
            bytes_accessed=70_000_000,
            transcendentals=0,
        ),
        name="attention_backward",
    )(tab, queries, pool, gain, grad_normed, attended, probs, sums)
    return normed, grad_q, pool


def on_device(queries, key_rows, value_rows, norm_gain, sort_index, grad_normed):
    rows, columns = queries.shape
    blocks = rows // BLOCK
    lay = Layout(lax.axis_size("ctx"), blocks)
    tab = routing_table(sort_index, lay)
    gain = norm_gain.reshape(1, columns)

    shape3 = (blocks, BLOCK, columns)
    pool = gather_blocks(key_rows.reshape(shape3), value_rows.reshape(shape3), tab, lay)

    normed, grad_q, pool = attention(queries, pool, gain, grad_normed, tab, lay)
    grad_k, grad_v = return_blocks(pool, tab, lay)
    return normed, grad_q, grad_k.reshape(rows, columns), grad_v.reshape(rows, columns)


def solution(mesh):
    in_specs = (
        P("ctx", "head"),
        P("ctx", "head"),
        P("ctx", "head"),
        P("head"),
        P(),
        P("ctx", "head"),
    )
    out_specs = (P("ctx", "head"), P("ctx", "head"), P("ctx", "head"), P("ctx", "head"))
    return jax.shard_map(
        on_device, mesh=mesh, in_specs=in_specs, out_specs=out_specs, check_vma=False
    )
```

```python
import functools
import math

import jax
import jax.numpy as jnp
import numpy as np
from jax import lax
from jax.experimental import pallas as pl
from jax.experimental.pallas import tpu as pltpu
from jax.sharding import PartitionSpec as P

HDIM = 128
BLOCK = 256
WIDTH = 5120
LANES = 128
ROW = 16
LEAD = 2
FIRST = 1024
STATIC_SLOTS = 9
SCALE = HDIM ** (-0.5)
SCALE_LOG2 = SCALE * math.log2(math.e)
ANY = pl.BlockSpec(memory_space=pl.ANY)
SMEM = pl.BlockSpec(memory_space=pltpu.SMEM)
VMEM = pl.BlockSpec(memory_space=pltpu.VMEM)
BIG = pltpu.CompilerParams(vmem_limit_bytes=56 * 1024 * 1024)
MOVE = pltpu.CompilerParams(vmem_limit_bytes=56 * 1024 * 1024)


class Layout:
    def __init__(self, ctx_size, blocks):
        self.ctx_size = ctx_size
        self.blocks = blocks
        self.levels = ctx_size // 2
        line = self.levels * blocks
        self.value_line = line
        self.value_own = 2 * line
        self.over = 2 * line + blocks
        self.places = self.over + 2 * (blocks + 1)
        self.slots = 2 * (2 * line + 2 * self.levels + 2 * blocks + 4)
        self.rows = self.slots + 2 * LEAD
        self.info = self.rows * ROW
        self.key_picks = self.info
        self.value_picks = self.info + blocks + 1
        self.total = self.info + 2 * blocks + 2
        self.device = self.info + 2 * blocks + 3


def shift_rows(array, count, rows):
    n = array.shape[0]
    if abs(count) >= n:
        return jnp.zeros_like(array)
    rolled = pltpu.roll(array, (-count) % n, 0)
    inside = (rows < n - count) if count > 0 else (rows >= -count)
    return jnp.where(inside, rolled, 0.0)


def table_kernel(picks_ref, gain_ref, out_ref, gain_row_ref, *, lay):
    n = lay.ctx_size
    blocks = lay.blocks
    count = n * blocks
    width = -(-2 * count // LANES) * LANES
    rows = lax.broadcasted_iota(jnp.int32, (n, width), 0)
    lanes = lax.broadcasted_iota(jnp.int32, (n, width), 1)
    out_lanes = lax.broadcasted_iota(jnp.int32, (n, LANES), 1)
    values = lanes >= count
    block = jnp.where(lanes >= 2 * count, -2, jnp.where(values, lanes - count, lanes))
    owner = jnp.floor((block.astype(jnp.float32) + 0.5) / blocks).astype(jnp.int32)
    within = block - owner * blocks
    line = (owner >> 1) * blocks + within
    place = jnp.where(values, jnp.where(owner == rows, lay.value_own + within, lay.value_line + line), line)
    place = jnp.where(block < 0, 0, place).astype(jnp.float32)
    picks = picks_ref[...]
    side = rows & 1
    level = rows >> 1
    same_side = side == (owner & 1)
    travels = jnp.logical_xor(same_side, values)
    owned = owner == rows

    def other(array):
        return jnp.where(side == 0, pltpu.roll(array, n - 1, 0), pltpu.roll(array, 1, 0))

    need = jnp.zeros((n, width), jnp.float32)
    for j in range(blocks + 1):
        need = jnp.where(picks[:, j : j + 1] == block, 1.0, need)
    need = jnp.where(owned, 0.0, need)
    across = other(need)
    wanted = jnp.maximum(need, across)
    final = jnp.where(travels, across, 0.0)
    hops = jnp.where(wanted > 0, 1.0 + final, 0.0)
    up_hops = jnp.zeros_like(need)
    down_hops = jnp.zeros_like(need)
    for k in range(1, lay.levels):
        above = shift_rows(hops, 2 * k, rows)
        below = shift_rows(hops, -2 * k, rows)
        up_hops = jnp.maximum(up_hops, jnp.where(above > 0, above + (k - 1), 0.0))
        down_hops = jnp.maximum(down_hops, jnp.where(below > 0, below + (k - 1), 0.0))
    up = jnp.where(travels & (level >= (owner >> 1)) & (up_hops > 0), 1.0, 0.0)
    down = jnp.where(travels & (level <= (owner >> 1)) & (down_hops > 0), 1.0, 0.0)
    source = owned & jnp.logical_not(travels)
    most = jnp.maximum(up_hops, down_hops)
    over = jnp.where(source & ((most > 0) | (across > 0)), 1.0, final)
    spread = jnp.minimum(jnp.sum(need, axis=0, keepdims=True), 3.0)
    low = (width - 1 - lanes).astype(jnp.float32)
    up_rank = (up_hops * 4.0 + spread) * width + low
    down_rank = (down_hops * 4.0 + spread) * width + low
    over_rank = jnp.where(source, most * 4.0 + spread, 2.0) * width + low
    first_over = float(lay.over)

    gain_row_ref[0, :] = gain_ref[:]
    out_ref[...] = jnp.full(out_ref.shape, -1, jnp.int32)

    def pick(pending, have, rank):
        score = jnp.where(pending * have > 0, rank, -1.0)
        best = jnp.max(score, axis=1, keepdims=True)
        return jnp.where((score == best) & (best >= 0), 1.0, 0.0)

    def where(chosen):
        return jnp.sum(chosen * (place + 1.0), axis=1, keepdims=True) - 1.0

    def pending(state):
        t, have, fresh, up, down, over, over_place, count = state
        return (t < lay.slots) & (jnp.sum(up + down + over) > 0)

    def step(state):
        t, have, fresh, up, down, over, over_place, count = state
        send_up = pick(up, have, up_rank)
        send_down = pick(down, have, down_rank)
        send_over = pick(over, have, over_rank)
        up = up - send_up
        down = down - send_down
        over = over - send_over
        got_up = shift_rows(send_up, -2, rows)
        got_down = shift_rows(send_down, 2, rows)
        got_over = other(send_over)
        got_final = jnp.where(travels, 0.0, got_over)
        any_final = jnp.max(got_final, axis=1, keepdims=True)
        over_at = jnp.where(any_final > 0, count + first_over, where(got_over))
        last = jnp.where((up + down + over + need > 0) | owned, 0.0, float(FIRST))

        def first_back(chosen):
            return jnp.max(chosen * last, axis=1, keepdims=True)

        columns = (
            where(send_up) + first_back(send_up),
            where(send_down) + first_back(send_down * (1.0 - send_up)),
            where(send_over) + first_back(send_over * (1.0 - send_up) * (1.0 - send_down)),
            where(got_up),
            where(got_down),
            over_at,
        )
        row = jnp.full((n, LANES), -1.0, jnp.float32)
        for k, column in enumerate(columns):
            row = jnp.where(out_lanes == k, column, row)
        out_ref[t + LEAD] = row.astype(jnp.int32)
        over_place = jnp.where(got_final > 0, count + first_over, over_place)
        have = jnp.maximum(have, fresh)
        fresh = jnp.maximum(got_up, jnp.maximum(got_down, got_over))
        return (t + 1, have, fresh, up, down, over, over_place, count + any_final)

    zeros = jnp.zeros_like(need)
    have = jnp.where(owned, 1.0, 0.0)
    state = (jnp.int32(0), have, zeros, up, down, over, zeros, jnp.zeros((n, 1), jnp.float32))
    state = lax.while_loop(pending, step, state)
    at = jnp.where(travels | owned, place, state[6])
    own_row = lax.broadcasted_iota(jnp.int32, (n, LANES), 0)
    row = jnp.zeros((n, LANES), jnp.float32)
    for kind in range(2):
        base = (own_row >> 1) * blocks if kind == 0 else jnp.full((n, LANES), lay.value_own)
        for j in range(blocks + 1):
            chosen = (picks[:, j : j + 1] == block) & (values if kind else jnp.logical_not(values))
            found = jnp.sum(jnp.where(chosen, at, 0.0), axis=1, keepdims=True)
            found = jnp.where(picks[:, j : j + 1] < 0, base[:, :1].astype(jnp.float32), found)
            row = jnp.where(out_lanes == kind * (blocks + 1) + j, found, row)
    row = jnp.where(out_lanes == 2 * blocks + 2, state[0].astype(jnp.float32), row)
    row = jnp.where(out_lanes == 2 * blocks + 3, own_row.astype(jnp.float32), row)
    out_ref[lay.rows] = row.astype(jnp.int32)


def routing_table(sort_index, norm_gain, lay):
    n, blocks = lay.ctx_size, lay.blocks
    before = (np.arange(n, dtype=np.int32) * blocks - 1)[:, None]
    picks = jnp.concatenate([sort_index.reshape(n, blocks), jnp.asarray(before)], axis=1)
    picks = jnp.pad(picks, ((0, 0), (0, LANES - blocks - 1)), constant_values=-1)
    table, gain = pl.pallas_call(
        functools.partial(table_kernel, lay=lay),
        out_shape=(
            jax.ShapeDtypeStruct((lay.rows + 1, n, LANES), jnp.int32),
            jax.ShapeDtypeStruct((1,) + norm_gain.shape, norm_gain.dtype),
        ),
        in_specs=[VMEM, VMEM],
        out_specs=(VMEM, VMEM),
        name="routing_table",
    )(picks, norm_gain)
    mine = lax.dynamic_slice(table, (0, lax.axis_index("ctx"), 0), (lay.rows + 1, 1, ROW))
    return mine.reshape((lay.rows + 1) * ROW), gain


def routes(ctx_size):
    up = [(d, d + 2) for d in range(ctx_size - 2)]
    down = [(d + 2, d) for d in range(ctx_size - 2)]
    over = [(d, d ^ 1) for d in range(ctx_size)]
    return up, down, over


def copies(jobs, sems):
    started = []
    for k, (valid, source, target) in enumerate(jobs):
        copy = pltpu.make_async_copy(source, target, sems.at[k])
        pl.when(valid)(copy.start)
        started.append((valid, copy))
    for valid, copy in started:
        pl.when(valid)(copy.wait)


def entry(tab_ref, t, k):
    return tab_ref[(t + LEAD) * ROW + k]


def place_of(code):
    return jnp.maximum(code, 0) & (FIRST - 1)


def fill_kernel(tab_ref, key_ref, value_ref, pool_ref, held_ref, sems, *, lay):
    blocks = lay.blocks
    level = tab_ref[lay.device] >> 1
    loads = [
        pltpu.make_async_copy(key_ref, held_ref.at[pl.ds(0, blocks)], sems.at[0]),
        pltpu.make_async_copy(value_ref, held_ref.at[pl.ds(blocks, blocks)], sems.at[1]),
    ]
    stores = [
        pltpu.make_async_copy(
            held_ref.at[pl.ds(0, blocks)], pool_ref.at[pl.ds(level * blocks, blocks)], sems.at[2]
        ),
        pltpu.make_async_copy(
            held_ref.at[pl.ds(blocks, blocks)],
            pool_ref.at[pl.ds(lay.value_own, blocks)],
            sems.at[3],
        ),
    ]
    for load in loads:
        load.start()
    for load, store in zip(loads, stores):
        load.wait()
        store.start()
    for store in stores:
        store.wait()


def first_kernel(
    tab_ref, key_ref, value_ref, up_ref, down_ref, over_ref, held_ref, sems, *, lay, slot
):
    blocks = lay.blocks
    level = tab_ref[lay.device] >> 1
    loads, stores = [], []
    for k, out in enumerate((up_ref, down_ref, over_ref)):
        code = entry(tab_ref, slot, k)
        at = place_of(code)
        is_value = at >= lay.value_own
        key_at = jnp.clip(at - level * blocks, 0, blocks - 1)
        value_at = jnp.clip(at - lay.value_own, 0, blocks - 1)
        valid = code >= 0
        loads.append((valid & jnp.logical_not(is_value), key_ref.at[key_at], held_ref.at[k]))
        loads.append((valid & is_value, value_ref.at[value_at], held_ref.at[k]))
        stores.append((valid, held_ref.at[k], out))
    copies(loads, sems)
    copies(stores, sems)


def slot_and_rest(slot, refs):
    return (refs[0][0], refs[1:]) if slot is None else (slot, refs)


def match(place, valid, places, valids):
    hits = [valid & v & (place == p) for p, v in zip(places, valids)]
    found = hits[0] | hits[1] | hits[2]
    return found, jnp.where(hits[0], 0, jnp.where(hits[1], 1, 2))


def step_kernel(*refs, slot):
    t, refs = slot_and_rest(slot, refs)
    (
        tab_ref, _, in_up, in_down, in_over, pool_ref, up_ref, down_ref, over_ref, held_ref, sems,
    ) = refs
    got_codes = [entry(tab_ref, t - 2, 3 + k) for k in range(3)]
    got_valid = [c >= 0 for c in got_codes]
    got_places = [place_of(c) for c in got_codes]
    loads = [
        (v, got, held_ref.at[k])
        for k, (v, got) in enumerate(zip(got_valid, (in_up, in_down, in_over)))
    ]
    stores = [
        (v, held_ref.at[k], pool_ref.at[p])
        for k, (v, p) in enumerate(zip(got_valid, got_places))
    ]
    for k, out in enumerate((up_ref, down_ref, over_ref)):
        code = entry(tab_ref, t, k)
        valid = code >= 0
        place = place_of(code)
        found, at = match(place, valid, got_places, got_valid)
        loads.append((valid & jnp.logical_not(found), pool_ref.at[place], held_ref.at[3 + k]))
        stores.append((valid, held_ref.at[jnp.where(found, at, 3 + k)], out))
    copies(loads, sems)
    copies(stores, sems)


def close_kernel(*refs, slot, back):
    t, refs = slot_and_rest(slot, refs)
    tab_ref, _, in_up, in_down, in_over, pool_ref, held_ref, sems = refs
    loads, stores = [], []
    for k, got in enumerate((in_up, in_down, in_over)):
        code = entry(tab_ref, t - back, 3 + k)
        loads.append((code >= 0, got, held_ref.at[k]))
        stores.append((code >= 0, held_ref.at[k], pool_ref.at[place_of(code)]))
    copies(loads, sems)
    copies(stores, sems)


def traffic(byte_count):
    return pl.CostEstimate(flops=0, bytes_accessed=byte_count, transcendentals=0)


def send_all(sends, perms):
    return tuple(lax.ppermute(s, "ctx", p) for s, p in zip(sends, perms))


def numbered(kernel, t, call):
    known = isinstance(t, int)
    extra = [] if known else [t.reshape(1)]
    specs = [] if known else [SMEM]
    return functools.partial(
        pl.pallas_call(
            functools.partial(kernel, slot=t if known else None),
            in_specs=specs + call.pop("in_specs"),
            input_output_aliases={1 + len(extra): 0},
            compiler_params=MOVE,
            **call,
        ),
        *extra,
    )


def gather_blocks(keys, values, tab, lay):
    one = jax.ShapeDtypeStruct(keys.shape[1:], keys.dtype)
    pool_shape = jax.ShapeDtypeStruct((lay.places,) + one.shape, one.dtype)
    size = 2 * math.prod(one.shape)
    perms = routes(lay.ctx_size)
    six = [pltpu.VMEM((6,) + one.shape, one.dtype), pltpu.SemaphoreType.DMA((6,))]

    def first(slot):
        sends = pl.pallas_call(
            functools.partial(first_kernel, lay=lay, slot=slot),
            out_shape=(one,) * 3,
            in_specs=[SMEM, ANY, ANY],
            out_specs=(ANY,) * 3,
            scratch_shapes=six,
            compiler_params=MOVE,
            cost_estimate=traffic(size * 6),
            name="gather_first",
        )(tab, keys, values)
        return send_all(sends, perms)

    older = first(0)
    newer = first(1)
    pool = pl.pallas_call(
        functools.partial(fill_kernel, lay=lay),
        out_shape=pool_shape,
        in_specs=[SMEM, ANY, ANY],
        out_specs=ANY,
        scratch_shapes=[
            pltpu.VMEM((2 * lay.blocks,) + one.shape, one.dtype),
            pltpu.SemaphoreType.DMA((4,)),
        ],
        compiler_params=MOVE,
        cost_estimate=traffic(size * 4 * lay.blocks),
        name="gather_fill",
    )(tab, keys, values)

    def step(t, pool, got):
        call = dict(
            out_shape=(pool_shape, one, one, one),
            in_specs=[SMEM] + [ANY] * 4,
            out_specs=(ANY,) * 4,
            scratch_shapes=six,
            cost_estimate=traffic(size * 12),
            name="gather_step",
        )
        pool, *sends = numbered(step_kernel, t, call)(tab, pool, *got)
        return pool, send_all(sends, perms)

    for t in range(2, STATIC_SLOTS):
        pool, latest = step(t, pool, older)
        older, newer = newer, latest

    def body(state):
        t, pool, older, newer = state
        pool, latest = step(t, pool, older)
        return t + 1, pool, newer, latest

    t, pool, older, newer = lax.while_loop(
        lambda state: state[0] < tab[lay.total],
        body,
        (jnp.int32(STATIC_SLOTS), pool, older, newer),
    )
    for back, got in ((2, older), (1, newer)):
        call = dict(
            out_shape=pool_shape,
            in_specs=[SMEM] + [ANY] * 4,
            out_specs=ANY,
            scratch_shapes=six,
            cost_estimate=traffic(size * 6),
            name="gather_close",
        )
        pool = numbered(functools.partial(close_kernel, back=back), t, call)(tab, pool, *got)
    return pool


def add(target_ref, to, source_ref, at):
    target_ref[to] = (
        target_ref[to].astype(jnp.float32) + source_ref[at].astype(jnp.float32)
    ).astype(target_ref.dtype)


def back_kernel(*refs, slot):
    t, refs = slot_and_rest(slot, refs)
    (
        tab_ref, _, in_up, in_down, in_over, pool_ref, up_ref, down_ref, over_ref,
        held_ref, got_ref, sems,
    ) = refs
    codes = [entry(tab_ref, t + 2, k) for k in range(3)]
    places = [place_of(c) for c in codes]
    valid = [c >= 0 for c in codes]
    fresh = [c >= FIRST for c in codes]
    same_10 = valid[1] & valid[0] & (places[1] == places[0])
    same_20 = valid[2] & valid[0] & (places[2] == places[0])
    same_21 = valid[2] & valid[1] & (places[2] == places[1]) & jnp.logical_not(same_20)
    alone = [
        valid[0],
        valid[1] & jnp.logical_not(same_10),
        valid[2] & jnp.logical_not(same_20 | same_21),
    ]
    loads = [
        (v, got, got_ref.at[k]) for k, (v, got) in enumerate(zip(valid, (in_up, in_down, in_over)))
    ]
    loads += [
        (a & jnp.logical_not(f), pool_ref.at[p], held_ref.at[k])
        for k, (a, f, p) in enumerate(zip(alone, fresh, places))
    ]
    stores = []
    leaves = [False] * 3
    for k, out in enumerate((up_ref, down_ref, over_ref)):
        code = entry(tab_ref, t, 3 + k)
        takes = code >= 0
        place = place_of(code)
        found, at = match(place, takes, places, alone)
        loads.append((takes & jnp.logical_not(found), pool_ref.at[place], held_ref.at[3 + k]))
        stores.append((takes, held_ref.at[jnp.where(found, at, 3 + k)], out))
        leaves = [leave | (found & (at == n)) for n, leave in enumerate(leaves)]
    copies(loads, sems)
    for k in range(3):

        @pl.when(alone[k] & fresh[k])
        def _(k=k):
            held_ref[k] = got_ref[k]

        @pl.when(alone[k] & jnp.logical_not(fresh[k]))
        def _(k=k):
            add(held_ref, k, got_ref, k)

    for k, to, here in ((1, 0, same_10), (2, 0, same_20), (2, 1, same_21)):

        @pl.when(here)
        def _(k=k, to=to):
            add(held_ref, to, got_ref, k)

    stores += [
        (a & jnp.logical_not(leave), held_ref.at[k], pool_ref.at[p])
        for k, (a, leave, p) in enumerate(zip(alone, leaves, places))
    ]
    copies(stores, sems)


def home_kernel(tab_ref, pool_ref, *refs, lay):
    arrived, (key_ref, value_ref, own_ref, got_ref, sems) = refs[:6], refs[6:]
    blocks = lay.blocks
    level = tab_ref[lay.device] >> 1
    halves = (
        (pool_ref.at[pl.ds(level * blocks, blocks)], key_ref),
        (pool_ref.at[pl.ds(lay.value_own, blocks)], value_ref),
    )
    loads, stores = [], []
    for k, (source, target) in enumerate(halves):
        held = own_ref.at[pl.ds(k * blocks, blocks)]
        loads.append((level >= 0, source, held))
        stores.append((level >= 0, held, target))
    codes = [entry(tab_ref, 1 - n // 3, n % 3) for n in range(6)]
    for n, (code, got) in enumerate(zip(codes, arrived)):
        loads.append((code >= 0, got, got_ref.at[n]))
    copies(loads, sems)
    for n, code in enumerate(codes):
        place = place_of(code)
        at = jnp.where(
            place >= lay.value_own, place - lay.value_own + blocks, place - level * blocks
        )

        @pl.when(code >= 0)
        def _(n=n, at=at):
            add(own_ref, jnp.clip(at, 0, 2 * blocks - 1), got_ref, n)

    copies(stores, sems)


def return_blocks(pool, tab, lay):
    one = jax.ShapeDtypeStruct(pool.shape[1:], pool.dtype)
    pool_shape = jax.ShapeDtypeStruct(pool.shape, pool.dtype)
    own_shape = jax.ShapeDtypeStruct((lay.blocks,) + one.shape, one.dtype)
    size = 2 * math.prod(one.shape)
    up, down, over = routes(lay.ctx_size)
    perms = ([(b, a) for a, b in up], [(b, a) for a, b in down], over)

    def step(t, pool, got):
        call = dict(
            out_shape=(pool_shape, one, one, one),
            in_specs=[SMEM] + [ANY] * 4,
            out_specs=(ANY,) * 4,
            scratch_shapes=[
                pltpu.VMEM((6,) + one.shape, one.dtype),
                pltpu.VMEM((3,) + one.shape, one.dtype),
                pltpu.SemaphoreType.DMA((9,)),
            ],
            cost_estimate=traffic(size * 15),
            name="return_step",
        )
        pool, *sends = numbered(back_kernel, t, call)(tab, pool, *got)
        return pool, send_all(sends, perms)

    def body(state):
        t, pool, older, newer = state
        pool, latest = step(t, pool, older)
        return t - 1, pool, newer, latest

    nothing = (jnp.zeros(one.shape, one.dtype),) * 3
    _, pool, older, newer = lax.while_loop(
        lambda state: state[0] >= STATIC_SLOTS,
        body,
        (tab[lay.total] - 1, pool, nothing, nothing),
    )
    for t in range(STATIC_SLOTS - 1, -1, -1):
        pool, latest = step(t, pool, older)
        older, newer = newer, latest
    return pl.pallas_call(
        functools.partial(home_kernel, lay=lay),
        out_shape=(own_shape, own_shape),
        in_specs=[SMEM] + [ANY] * 7,
        out_specs=(ANY, ANY),
        scratch_shapes=[
            pltpu.VMEM((2 * lay.blocks,) + one.shape, one.dtype),
            pltpu.VMEM((6,) + one.shape, one.dtype),
            pltpu.SemaphoreType.DMA((8,)),
        ],
        compiler_params=MOVE,
        cost_estimate=traffic(size * 30),
        name="return_home",
    )(tab, pool, *older, *newer)


QK = (((1,), (1,)), ((), ()))
AB = (((1,), (0,)), ((), ()))
TA = (((0,), (0,)), ((), ()))


def dot(a, b, dims):
    return lax.dot_general(a, b, dims, preferred_element_type=jnp.float32)


def rows_of(i):
    return slice(i * BLOCK, (i + 1) * BLOCK)


def parts_of(i, cols, own_ref, pick_refs):
    blocks = len(pick_refs) - 1
    before = pick_refs[blocks][0, :, cols] if i == 0 else own_ref[i - 1, :, cols]
    return own_ref[i, :, cols], before, pick_refs[i][0, :, cols]


def term_places(tab_ref, lay):
    level = tab_ref[lay.device] >> 1
    result = []
    for base, picks in ((level * lay.blocks, lay.key_picks), (lay.value_own, lay.value_picks)):
        places = [base + o for o in range(lay.blocks)]
        places += [tab_ref[picks + j] for j in range(lay.blocks + 1)]
        result.append(places)
    return result


def forward_kernel(tab_ref, *refs, lay, group):
    blocks = lay.blocks
    count = blocks + 2
    q_ref, key_refs, value_refs = refs[0], refs[1 : 1 + count], refs[1 + count : 1 + 2 * count]
    gain_ref, grad_ref, attended_ref, probs_ref, sums_ref, acc_ref = refs[1 + 2 * count :]
    h = pl.program_id(0)
    causal = lax.broadcasted_iota(jnp.int32, (BLOCK, BLOCK), 0) <= lax.broadcasted_iota(
        jnp.int32, (BLOCK, BLOCK), 1
    )
    hide = jnp.where(tab_ref[lay.device] > 0, 0.0, -jnp.inf).astype(jnp.float32)
    lane = lax.broadcasted_iota(jnp.int32, (BLOCK, LANES), 1)

    @pl.when(h == 0)
    def _():
        acc_ref[...] = jnp.zeros_like(acc_ref)

    def score(i, g):
        cols = slice(g * HDIM, (g + 1) * HDIM)
        q = q_ref[rows_of(i), cols]
        return [dot(k, q, QK) for k in parts_of(i, cols, key_refs[0], key_refs[1:])]

    tasks = [(i, g) for i in range(blocks) for g in range(group)]
    following = score(*tasks[0])
    for n, (i, g) in enumerate(tasks):
        scores = following
        if n + 1 < len(tasks):
            following = score(*tasks[n + 1])
        cols = slice(g * HDIM, (g + 1) * HDIM)
        scores[0] = jnp.where(causal, scores[0], -jnp.inf)
        if i == 0:
            scores[1] = scores[1] + hide
        top = jnp.max(
            jnp.maximum(jnp.maximum(scores[0], scores[1]), scores[2]), axis=0, keepdims=True
        )
        weights = [jnp.exp2((s - top) * SCALE_LOG2) for s in scores]
        scale = 1.0 / jnp.sum(weights[0] + weights[1] + weights[2], axis=0, keepdims=True)
        turned = 0.0
        values = parts_of(i, cols, value_refs[0], value_refs[1:])
        for j, (w, v) in enumerate(zip(weights, values)):
            low = (w * scale).astype(jnp.bfloat16)
            probs_ref[i, g, rows_of(j)] = low
            turned += dot(v, low, TA)
        attended = jnp.transpose(turned)
        attended_ref[rows_of(i), cols] = attended
        lifted = gain_ref[:, cols] * grad_ref[rows_of(i), cols].astype(jnp.float32)
        squares = jnp.sum(attended * attended, axis=1, keepdims=True)
        center = jnp.sum(lifted * attended, axis=1, keepdims=True)
        acc_ref[i] += jnp.where(lane == 0, squares, jnp.where(lane == 1, center, 0.0))

    @pl.when(h == pl.num_programs(0) - 1)
    def _():
        for i in range(blocks):
            sums_ref[:, rows_of(i)] = jnp.transpose(acc_ref[i])[:8]


def backward_kernel(
    tab_ref, q_ref, pool_in, gain_ref, grad_ref, attended_ref, probs_ref, *refs, lay, group
):
    del pool_in
    sums_refs, refs = refs[:-9], refs[-9:]
    normed_ref, gq_ref, pool_ref, rms_ref, acc_ref, out_ref, kv_ref, sems, load_sems = refs
    blocks = lay.blocks
    h = pl.program_id(0)
    steps = pl.num_programs(0)
    width = group * HDIM
    terms = 2 * blocks + 1
    places = term_places(tab_ref, lay)
    buffer = lax.rem(h, 2)

    def columns(at):
        return pl.ds(pl.multiple_of(at * width, width), width)

    def loads(at, buffer):
        return [
            pltpu.make_async_copy(
                pool_ref.at[places[kind][n], :, columns(at)],
                kv_ref.at[buffer, kind, n],
                load_sems.at[buffer, kind * terms + n],
            )
            for kind in range(2)
            for n in range(terms)
        ]

    @pl.when(h == 0)
    def _():
        for load in loads(0, 0):
            load.start()

    for load in loads(h, buffer):
        load.wait()

    @pl.when(h + 1 < steps)
    def _():
        for load in loads(h + 1, 1 - buffer):
            load.start()

    @pl.when(h == 0)
    def _():
        sums = sum(ref[...] for ref in sums_refs)
        squares = sums[0:1]
        center = sums[1:2]
        inv = lax.rsqrt(squares / WIDTH + 1e-05)
        factor = inv * inv * inv * center / WIDTH
        both = jnp.concatenate([inv, factor, jnp.zeros((6,) + inv.shape[1:], jnp.float32)], axis=0)
        for i in range(blocks):
            wide = jnp.concatenate([both[:, rows_of(i)]] * (LANES // 8), axis=0)
            rms_ref[i] = jnp.transpose(wide)

    def places_in(i):
        return (i, 2 * blocks if i == 0 else i - 1, blocks + i)

    def prepare(i, g):
        cols = slice(g * HDIM, (g + 1) * HDIM)
        inv_rms = rms_ref[i, :, 0:1]
        factor = rms_ref[i, :, 1:2]
        attended = attended_ref[rows_of(i), cols]
        gain = gain_ref[:, cols]
        normed_ref[rows_of(i), cols] = (attended * inv_rms * gain).astype(jnp.bfloat16)
        lifted = gain * grad_ref[rows_of(i), cols].astype(jnp.float32)
        grad = (inv_rms * lifted - attended * factor).astype(jnp.bfloat16)
        row = jnp.sum(jnp.transpose(grad.astype(jnp.float32) * attended), axis=0, keepdims=True)
        gps = [dot(kv_ref[buffer, 1, n, :, cols], grad, QK) for n in places_in(i)]
        return grad, row, gps

    tasks = [(i, g) for i in range(blocks) for g in range(group)]
    following = prepare(*tasks[0])
    for n, (i, g) in enumerate(tasks):
        grad, row, gps = following
        if n + 1 < len(tasks):
            following = prepare(*tasks[n + 1])
        cols = slice(g * HDIM, (g + 1) * HDIM)
        q = q_ref[rows_of(i), cols]
        gq = 0.0
        for j, at in enumerate(places_in(i)):
            low = probs_ref[i, g, rows_of(j)]
            gv = dot(low, grad, AB)
            gs = (low.astype(jnp.float32) * (gps[j] - row)).astype(jnp.bfloat16)
            gq += dot(kv_ref[buffer, 0, at, :, cols], gs, TA)
            gk = dot(gs, q, AB) * SCALE
            for kind, term in ((0, gk), (1, gv)):
                if j == 0 and i + 1 < blocks:
                    acc_ref[kind, i % 2, g] = term
                elif j == 1 and i > 0:
                    total = acc_ref[kind, at % 2, g] + term
                    out_ref[buffer, kind, at, :, cols] = total.astype(jnp.bfloat16)
                else:
                    out_ref[buffer, kind, at, :, cols] = term.astype(jnp.bfloat16)
        gq_ref[rows_of(i), cols] = (jnp.transpose(gq) * SCALE).astype(jnp.bfloat16)

    jobs = []
    for kind in range(2):
        writes = [steps > 0] * blocks
        for at in range(terms - 1, blocks - 1, -1):
            taken = False
            for to in list(range(blocks)) + list(range(at - 1, blocks - 1, -1)):
                here = (places[kind][at] == places[kind][to]) & jnp.logical_not(taken)
                taken = taken | here

                @pl.when(here)
                def _(kind=kind, at=at, to=to):
                    out_ref[buffer, kind, to] = (
                        out_ref[buffer, kind, to].astype(jnp.float32)
                        + out_ref[buffer, kind, at].astype(jnp.float32)
                    ).astype(jnp.bfloat16)

            writes.insert(blocks, jnp.logical_not(taken))
        for at in range(terms):
            jobs.append((kind, at, places[kind][at], writes[at]))

    def store(n, job, slot_h, buffer):
        kind, at, place, valid = job
        return valid, pltpu.make_async_copy(
            out_ref.at[buffer, kind, at],
            pool_ref.at[place, :, columns(slot_h)],
            sems.at[n],
        )

    for n, job in enumerate(jobs):
        valid, copy = store(n, job, jnp.maximum(h - 1, 0), 1 - buffer)
        pl.when(valid & (h > 0))(copy.wait)
    for n, job in enumerate(jobs):
        valid, copy = store(n, job, h, buffer)
        pl.when(valid)(copy.start)

    @pl.when(h == steps - 1)
    def _():
        for n, job in enumerate(jobs):
            valid, copy = store(n, job, h, buffer)
            pl.when(valid)(copy.wait)


def attention(queries, pool, gain, grad_normed, tab, lay):
    rows, columns = queries.shape
    blocks = lay.blocks
    heads = columns // HDIM
    group = 2 if heads % 2 == 0 else 1
    width = group * HDIM
    row_spec = pl.BlockSpec((rows, width), lambda h, tab: (0, h))
    gain_spec = pl.BlockSpec((1, width), lambda h, tab: (0, h))
    probs_spec = pl.BlockSpec((blocks, group, 3 * BLOCK, BLOCK), lambda h, tab: (0, h, 0, 0))
    sums_spec = pl.BlockSpec((8, rows), lambda h, tab: (0, 0))

    def pick_specs(own, picks):
        specs = [pl.BlockSpec((blocks, BLOCK, width), own)]
        for j in range(blocks + 1):
            specs.append(
                pl.BlockSpec((1, BLOCK, width), lambda h, tab, j=j: (tab[picks + j], 0, h))
            )
        return specs

    pool_specs = pick_specs(lambda h, tab: (tab[lay.device] >> 1, 0, h), lay.key_picks)
    pool_specs += pick_specs(lambda h, tab: (lay.value_own // blocks, 0, h), lay.value_picks)
    common = [row_spec] + pool_specs + [gain_spec, row_spec]
    operands = (queries,) + (pool,) * len(pool_specs) + (gain, grad_normed)

    attended, probs, sums = pl.pallas_call(
        functools.partial(forward_kernel, lay=lay, group=group),
        out_shape=(
            jax.ShapeDtypeStruct((rows, columns), jnp.float32),
            jax.ShapeDtypeStruct((blocks, heads, 3 * BLOCK, BLOCK), jnp.bfloat16),
            jax.ShapeDtypeStruct((8, rows), jnp.float32),
        ),
        grid_spec=pltpu.PrefetchScalarGridSpec(
            num_scalar_prefetch=1,
            grid=(heads // group,),
            in_specs=common,
            out_specs=(row_spec, probs_spec, sums_spec),
            scratch_shapes=[pltpu.VMEM((blocks, BLOCK, LANES), jnp.float32)],
        ),
        compiler_params=BIG,
        cost_estimate=pl.CostEstimate(
            flops=4 * rows * 3 * BLOCK * columns,
            bytes_accessed=50_000_000,
            transcendentals=rows * 3 * BLOCK * heads,
        ),
        name="attention_forward",
    )(tab, *operands)

    heads_size = lax.axis_size("head")
    sums = [sums] + [
        lax.ppermute(sums, "head", [(d, (d + k) % heads_size) for d in range(heads_size)])
        for k in range(1, heads_size)
    ]

    wide = jax.ShapeDtypeStruct((rows, columns), jnp.bfloat16)
    terms = (2, 2 * blocks + 1, BLOCK, width)
    normed, grad_q, pool = pl.pallas_call(
        functools.partial(backward_kernel, lay=lay, group=group),
        out_shape=(wide, wide, jax.ShapeDtypeStruct(pool.shape, pool.dtype)),
        grid_spec=pltpu.PrefetchScalarGridSpec(
            num_scalar_prefetch=1,
            grid=(heads // group,),
            in_specs=[row_spec, ANY, gain_spec, row_spec, row_spec, probs_spec]
            + [sums_spec] * len(sums),
            out_specs=(row_spec, row_spec, ANY),
            scratch_shapes=[
                pltpu.VMEM((blocks, BLOCK, LANES), jnp.float32),
                pltpu.VMEM((2, 2, group, BLOCK, HDIM), jnp.float32),
                pltpu.VMEM((2,) + terms, jnp.bfloat16),
                pltpu.VMEM((2,) + terms, jnp.bfloat16),
                pltpu.SemaphoreType.DMA((2 * terms[1],)),
                pltpu.SemaphoreType.DMA((2, 2 * terms[1])),
            ],
        ),
        input_output_aliases={2: 2},
        compiler_params=BIG,
        cost_estimate=pl.CostEstimate(
            flops=8 * rows * 3 * BLOCK * columns,
            bytes_accessed=70_000_000,
            transcendentals=0,
        ),
        name="attention_backward",
    )(tab, queries, pool, gain, grad_normed, attended, probs, *sums)
    return normed, grad_q, pool


def on_device(queries, key_rows, value_rows, norm_gain, sort_index, grad_normed):
    rows, columns = queries.shape
    blocks = rows // BLOCK
    lay = Layout(lax.axis_size("ctx"), blocks)
    tab, gain = routing_table(sort_index, norm_gain, lay)

    shape3 = (blocks, BLOCK, columns)
    own = (key_rows.reshape(shape3), value_rows.reshape(shape3))
    pool = gather_blocks(*own, tab, lay)

    normed, grad_q, pool = attention(queries, pool, gain, grad_normed, tab, lay)
    grad_k, grad_v = return_blocks(pool, tab, lay)
    return normed, grad_q, grad_k.reshape(rows, columns), grad_v.reshape(rows, columns)


def solution(mesh):
    in_specs = (
        P("ctx", "head"),
        P("ctx", "head"),
        P("ctx", "head"),
        P("head"),
        P(),
        P("ctx", "head"),
    )
    out_specs = (P("ctx", "head"), P("ctx", "head"), P("ctx", "head"), P("ctx", "head"))
    return jax.shard_map(
        on_device, mesh=mesh, in_specs=in_specs, out_specs=out_specs, check_vma=False
    )
```

```python
import functools
import math

import jax
import jax.numpy as jnp
import numpy as np
from jax import lax
from jax.experimental import pallas as pl
from jax.experimental.pallas import tpu as pltpu
from jax.sharding import PartitionSpec as P

HDIM = 128
BLOCK = 256
WIDTH = 5120
LANES = 128
ROW = 16
LEAD = 2
FIRST = 1024
STATIC_SLOTS = 9
SCALE = HDIM ** (-0.5)
SCALE_LOG2 = SCALE * math.log2(math.e)
ANY = pl.BlockSpec(memory_space=pl.ANY)
SMEM = pl.BlockSpec(memory_space=pltpu.SMEM)
VMEM = pl.BlockSpec(memory_space=pltpu.VMEM)
BIG = pltpu.CompilerParams(vmem_limit_bytes=56 * 1024 * 1024)
MOVE = pltpu.CompilerParams(vmem_limit_bytes=56 * 1024 * 1024)


class Layout:
    def __init__(self, ctx_size, blocks):
        self.ctx_size = ctx_size
        self.blocks = blocks
        self.levels = ctx_size // 2
        line = self.levels * blocks
        self.value_line = line
        self.value_own = 2 * line
        self.over = 2 * line + blocks
        self.places = self.over + 2 * (blocks + 1)
        self.slots = 2 * (2 * line + 2 * self.levels + 2 * blocks + 4)
        self.rows = self.slots + 2 * LEAD
        self.info = self.rows * ROW
        self.key_picks = self.info
        self.value_picks = self.info + blocks + 1
        self.total = self.info + 2 * blocks + 2
        self.device = self.info + 2 * blocks + 3


def shift_rows(array, count, rows):
    n = array.shape[0]
    if abs(count) >= n:
        return jnp.zeros_like(array)
    rolled = pltpu.roll(array, (-count) % n, 0)
    inside = (rows < n - count) if count > 0 else (rows >= -count)
    return jnp.where(inside, rolled, 0.0)


def table_kernel(picks_ref, gain_ref, out_ref, gain_row_ref, *, lay):
    n = lay.ctx_size
    blocks = lay.blocks
    count = n * blocks
    width = -(-2 * count // LANES) * LANES
    rows = lax.broadcasted_iota(jnp.int32, (n, width), 0)
    lanes = lax.broadcasted_iota(jnp.int32, (n, width), 1)
    out_lanes = lax.broadcasted_iota(jnp.int32, (n, LANES), 1)
    values = lanes >= count
    block = jnp.where(lanes >= 2 * count, -2, jnp.where(values, lanes - count, lanes))
    owner = jnp.floor((block.astype(jnp.float32) + 0.5) / blocks).astype(jnp.int32)
    within = block - owner * blocks
    line = (owner >> 1) * blocks + within
    place = jnp.where(values, jnp.where(owner == rows, lay.value_own + within, lay.value_line + line), line)
    place = jnp.where(block < 0, 0, place).astype(jnp.float32)
    picks = picks_ref[...]
    side = rows & 1
    level = rows >> 1
    same_side = side == (owner & 1)
    travels = jnp.logical_xor(same_side, values)
    owned = owner == rows

    def other(array):
        return jnp.where(side == 0, pltpu.roll(array, n - 1, 0), pltpu.roll(array, 1, 0))

    need = jnp.zeros((n, width), jnp.float32)
    for j in range(blocks + 1):
        need = jnp.where(picks[:, j : j + 1] == block, 1.0, need)
    need = jnp.where(owned, 0.0, need)
    across = other(need)
    wanted = jnp.maximum(need, across)
    final = jnp.where(travels, across, 0.0)
    hops = jnp.where(wanted > 0, 1.0 + final, 0.0)
    up_hops = jnp.zeros_like(need)
    down_hops = jnp.zeros_like(need)
    for k in range(1, lay.levels):
        above = shift_rows(hops, 2 * k, rows)
        below = shift_rows(hops, -2 * k, rows)
        up_hops = jnp.maximum(up_hops, jnp.where(above > 0, above + (k - 1), 0.0))
        down_hops = jnp.maximum(down_hops, jnp.where(below > 0, below + (k - 1), 0.0))
    up = jnp.where(travels & (level >= (owner >> 1)) & (up_hops > 0), 1.0, 0.0)
    down = jnp.where(travels & (level <= (owner >> 1)) & (down_hops > 0), 1.0, 0.0)
    source = owned & jnp.logical_not(travels)
    most = jnp.maximum(up_hops, down_hops)
    over = jnp.where(source & ((most > 0) | (across > 0)), 1.0, final)
    spread = jnp.minimum(jnp.sum(need, axis=0, keepdims=True), 3.0)
    low = (width - 1 - lanes).astype(jnp.float32)
    up_rank = (up_hops * 4.0 + spread) * width + low
    down_rank = (down_hops * 4.0 + spread) * width + low
    over_rank = jnp.where(source, most * 4.0 + spread, 2.0) * width + low
    first_over = float(lay.over)

    gain_row_ref[0, :] = gain_ref[:]
    out_ref[...] = jnp.full(out_ref.shape, -1, jnp.int32)

    def pick(pending, have, rank):
        score = jnp.where(pending * have > 0, rank, -1.0)
        best = jnp.max(score, axis=1, keepdims=True)
        return jnp.where((score == best) & (best >= 0), 1.0, 0.0)

    def where(chosen):
        return jnp.sum(chosen * (place + 1.0), axis=1, keepdims=True) - 1.0

    def pending(state):
        t, have, fresh, up, down, over, over_place, count = state
        return (t < lay.slots) & (jnp.sum(up + down + over) > 0)

    def step(state):
        t, have, fresh, up, down, over, over_place, count = state
        send_up = pick(up, have, up_rank)
        send_down = pick(down, have, down_rank)
        send_over = pick(over, have, over_rank)
        up = up - send_up
        down = down - send_down
        over = over - send_over
        got_up = shift_rows(send_up, -2, rows)
        got_down = shift_rows(send_down, 2, rows)
        got_over = other(send_over)
        got_final = jnp.where(travels, 0.0, got_over)
        any_final = jnp.max(got_final, axis=1, keepdims=True)
        over_at = jnp.where(any_final > 0, count + first_over, where(got_over))
        last = jnp.where((up + down + over + need > 0) | owned, 0.0, float(FIRST))

        def first_back(chosen):
            return jnp.max(chosen * last, axis=1, keepdims=True)

        columns = (
            where(send_up) + first_back(send_up),
            where(send_down) + first_back(send_down * (1.0 - send_up)),
            where(send_over) + first_back(send_over * (1.0 - send_up) * (1.0 - send_down)),
            where(got_up),
            where(got_down),
            over_at,
        )
        row = jnp.full((n, LANES), -1.0, jnp.float32)
        for k, column in enumerate(columns):
            row = jnp.where(out_lanes == k, column, row)
        out_ref[t + LEAD] = row.astype(jnp.int32)
        over_place = jnp.where(got_final > 0, count + first_over, over_place)
        have = jnp.maximum(have, fresh)
        fresh = jnp.maximum(got_up, jnp.maximum(got_down, got_over))
        return (t + 1, have, fresh, up, down, over, over_place, count + any_final)

    zeros = jnp.zeros_like(need)
    have = jnp.where(owned, 1.0, 0.0)
    state = (jnp.int32(0), have, zeros, up, down, over, zeros, jnp.zeros((n, 1), jnp.float32))
    state = lax.while_loop(pending, step, state)
    at = jnp.where(travels | owned, place, state[6])
    own_row = lax.broadcasted_iota(jnp.int32, (n, LANES), 0)
    row = jnp.zeros((n, LANES), jnp.float32)
    for kind in range(2):
        base = (own_row >> 1) * blocks if kind == 0 else jnp.full((n, LANES), lay.value_own)
        for j in range(blocks + 1):
            chosen = (picks[:, j : j + 1] == block) & (values if kind else jnp.logical_not(values))
            found = jnp.sum(jnp.where(chosen, at, 0.0), axis=1, keepdims=True)
            found = jnp.where(picks[:, j : j + 1] < 0, base[:, :1].astype(jnp.float32), found)
            row = jnp.where(out_lanes == kind * (blocks + 1) + j, found, row)
    row = jnp.where(out_lanes == 2 * blocks + 2, state[0].astype(jnp.float32), row)
    row = jnp.where(out_lanes == 2 * blocks + 3, own_row.astype(jnp.float32), row)
    out_ref[lay.rows] = row.astype(jnp.int32)


def routing_table(sort_index, norm_gain, lay):
    n, blocks = lay.ctx_size, lay.blocks
    before = (np.arange(n, dtype=np.int32) * blocks - 1)[:, None]
    picks = jnp.concatenate([sort_index.reshape(n, blocks), jnp.asarray(before)], axis=1)
    picks = jnp.pad(picks, ((0, 0), (0, LANES - blocks - 1)), constant_values=-1)
    table, gain = pl.pallas_call(
        functools.partial(table_kernel, lay=lay),
        out_shape=(
            jax.ShapeDtypeStruct((lay.rows + 1, n, LANES), jnp.int32),
            jax.ShapeDtypeStruct((1,) + norm_gain.shape, norm_gain.dtype),
        ),
        in_specs=[VMEM, VMEM],
        out_specs=(VMEM, VMEM),
        name="routing_table",
    )(picks, norm_gain)
    mine = lax.dynamic_slice(table, (0, lax.axis_index("ctx"), 0), (lay.rows + 1, 1, ROW))
    return mine.reshape((lay.rows + 1) * ROW), gain


def routes(ctx_size):
    up = [(d, d + 2) for d in range(ctx_size - 2)]
    down = [(d + 2, d) for d in range(ctx_size - 2)]
    over = [(d, d ^ 1) for d in range(ctx_size)]
    return up, down, over


def copies(jobs, sems):
    started = []
    for k, (valid, source, target) in enumerate(jobs):
        copy = pltpu.make_async_copy(source, target, sems.at[k])
        pl.when(valid)(copy.start)
        started.append((valid, copy))
    for valid, copy in started:
        pl.when(valid)(copy.wait)


def entry(tab_ref, t, k):
    return tab_ref[(t + LEAD) * ROW + k]


def place_of(code):
    return jnp.maximum(code, 0) & (FIRST - 1)


def fill_kernel(tab_ref, key_ref, value_ref, pool_ref, held_ref, sems, *, lay):
    blocks = lay.blocks
    level = tab_ref[lay.device] >> 1
    loads = [
        pltpu.make_async_copy(key_ref, held_ref.at[pl.ds(0, blocks)], sems.at[0]),
        pltpu.make_async_copy(value_ref, held_ref.at[pl.ds(blocks, blocks)], sems.at[1]),
    ]
    stores = [
        pltpu.make_async_copy(
            held_ref.at[pl.ds(0, blocks)], pool_ref.at[pl.ds(level * blocks, blocks)], sems.at[2]
        ),
        pltpu.make_async_copy(
            held_ref.at[pl.ds(blocks, blocks)],
            pool_ref.at[pl.ds(lay.value_own, blocks)],
            sems.at[3],
        ),
    ]
    for load in loads:
        load.start()
    for load, store in zip(loads, stores):
        load.wait()
        store.start()
    for store in stores:
        store.wait()


def first_kernel(
    tab_ref, key_ref, value_ref, up_ref, down_ref, over_ref, held_ref, sems, *, lay, slot
):
    blocks = lay.blocks
    level = tab_ref[lay.device] >> 1
    loads, stores = [], []
    for k, out in enumerate((up_ref, down_ref, over_ref)):
        code = entry(tab_ref, slot, k)
        at = place_of(code)
        is_value = at >= lay.value_own
        key_at = jnp.clip(at - level * blocks, 0, blocks - 1)
        value_at = jnp.clip(at - lay.value_own, 0, blocks - 1)
        valid = code >= 0
        loads.append((valid & jnp.logical_not(is_value), key_ref.at[key_at], held_ref.at[k]))
        loads.append((valid & is_value, value_ref.at[value_at], held_ref.at[k]))
        stores.append((valid, held_ref.at[k], out))
    copies(loads, sems)
    copies(stores, sems)


def slot_and_rest(slot, refs):
    return (refs[0][0], refs[1:]) if slot is None else (slot, refs)


def match(place, valid, places, valids):
    hits = [valid & v & (place == p) for p, v in zip(places, valids)]
    found = hits[0] | hits[1] | hits[2]
    return found, jnp.where(hits[0], 0, jnp.where(hits[1], 1, 2))


def step_kernel(*refs, slot):
    t, refs = slot_and_rest(slot, refs)
    (
        tab_ref, _, in_up, in_down, in_over, pool_ref, up_ref, down_ref, over_ref, held_ref, sems,
    ) = refs
    got_codes = [entry(tab_ref, t - 2, 3 + k) for k in range(3)]
    got_valid = [c >= 0 for c in got_codes]
    got_places = [place_of(c) for c in got_codes]
    loads = [
        (v, got, held_ref.at[k])
        for k, (v, got) in enumerate(zip(got_valid, (in_up, in_down, in_over)))
    ]
    stores = [
        (v, held_ref.at[k], pool_ref.at[p])
        for k, (v, p) in enumerate(zip(got_valid, got_places))
    ]
    for k, out in enumerate((up_ref, down_ref, over_ref)):
        code = entry(tab_ref, t, k)
        valid = code >= 0
        place = place_of(code)
        found, at = match(place, valid, got_places, got_valid)
        loads.append((valid & jnp.logical_not(found), pool_ref.at[place], held_ref.at[3 + k]))
        stores.append((valid, held_ref.at[jnp.where(found, at, 3 + k)], out))
    copies(loads, sems)
    copies(stores, sems)


def close_kernel(*refs, slot):
    t, refs = slot_and_rest(slot, refs)
    tab_ref, _, in_up, in_down, in_over, pool_ref, held_ref, sems = refs
    loads, stores = [], []
    for k, got in enumerate((in_up, in_down, in_over)):
        code = entry(tab_ref, t, 3 + k)
        loads.append((code >= 0, got, held_ref.at[k]))
        stores.append((code >= 0, held_ref.at[k], pool_ref.at[place_of(code)]))
    copies(loads, sems)
    copies(stores, sems)


def take_kernel(*refs, slot, first):
    t, refs = slot_and_rest(slot, refs)
    tab_ref, pool_ref, up_ref, down_ref, over_ref, held_ref, sems = refs
    loads, stores = [], []
    for k, out in enumerate((up_ref, down_ref, over_ref)):
        code = entry(tab_ref, t, first + k)
        loads.append((code >= 0, pool_ref.at[place_of(code)], held_ref.at[k]))
        stores.append((code >= 0, held_ref.at[k], out))
    copies(loads, sems)
    copies(stores, sems)


def traffic(byte_count):
    return pl.CostEstimate(flops=0, bytes_accessed=byte_count, transcendentals=0)


def take(t, tab, pool, first):
    one = jax.ShapeDtypeStruct(pool.shape[1:], pool.dtype)
    call = dict(
        out_shape=(one,) * 3,
        in_specs=[SMEM, ANY],
        out_specs=(ANY,) * 3,
        scratch_shapes=[pltpu.VMEM((3,) + one.shape, one.dtype), pltpu.SemaphoreType.DMA((3,))],
        cost_estimate=traffic(12 * math.prod(one.shape)),
        name="take_step",
        in_place=False,
    )
    return numbered(functools.partial(take_kernel, first=first), t, call)(tab, pool)


def send_all(sends, perms):
    return tuple(lax.ppermute(s, "ctx", p) for s, p in zip(sends, perms))


def numbered(kernel, t, call):
    known = isinstance(t, int)
    extra = [] if known else [t.reshape(1)]
    specs = [] if known else [SMEM]
    return functools.partial(
        pl.pallas_call(
            functools.partial(kernel, slot=t if known else None),
            in_specs=specs + call.pop("in_specs"),
            input_output_aliases={1 + len(extra): 0} if call.pop("in_place", True) else {},
            compiler_params=MOVE,
            **call,
        ),
        *extra,
    )


def gather_blocks(keys, values, tab, total, lay):
    one = jax.ShapeDtypeStruct(keys.shape[1:], keys.dtype)
    pool_shape = jax.ShapeDtypeStruct((lay.places,) + one.shape, one.dtype)
    size = 2 * math.prod(one.shape)
    perms = routes(lay.ctx_size)
    six = [pltpu.VMEM((6,) + one.shape, one.dtype), pltpu.SemaphoreType.DMA((6,))]

    def first(slot):
        sends = pl.pallas_call(
            functools.partial(first_kernel, lay=lay, slot=slot),
            out_shape=(one,) * 3,
            in_specs=[SMEM, ANY, ANY],
            out_specs=(ANY,) * 3,
            scratch_shapes=six,
            compiler_params=MOVE,
            cost_estimate=traffic(size * 6),
            name="gather_first",
        )(tab, keys, values)
        return send_all(sends, perms)

    older = first(0)
    newer = first(1)
    pool = pl.pallas_call(
        functools.partial(fill_kernel, lay=lay),
        out_shape=pool_shape,
        in_specs=[SMEM, ANY, ANY],
        out_specs=ANY,
        scratch_shapes=[
            pltpu.VMEM((2 * lay.blocks,) + one.shape, one.dtype),
            pltpu.SemaphoreType.DMA((4,)),
        ],
        compiler_params=MOVE,
        cost_estimate=traffic(size * 4 * lay.blocks),
        name="gather_fill",
    )(tab, keys, values)

    def step(t, pool, got):
        call = dict(
            out_shape=(pool_shape, one, one, one),
            in_specs=[SMEM] + [ANY] * 4,
            out_specs=(ANY,) * 4,
            scratch_shapes=six,
            cost_estimate=traffic(size * 12),
            name="gather_step",
        )
        pool, *sends = numbered(step_kernel, t, call)(tab, pool, *got)
        return pool, send_all(sends, perms)

    for t in range(2, STATIC_SLOTS):
        pool, latest = step(t, pool, older)
        older, newer = newer, latest

    def close(t, pool, got):
        call = dict(
            out_shape=pool_shape,
            in_specs=[SMEM] + [ANY] * 4,
            out_specs=ANY,
            scratch_shapes=six,
            cost_estimate=traffic(size * 6),
            name="gather_close",
        )
        return numbered(close_kernel, t, call)(tab, pool, *got)

    pool = close(STATIC_SLOTS - 2, pool, older)
    pool = close(STATIC_SLOTS - 1, pool, newer)

    def body(state):
        t, end, pool = state
        got = send_all(take(t, tab, pool, 0), perms)
        return t + 1, end, close(t, pool, got)

    return lax.while_loop(
        lambda state: state[0] < state[1], body, (jnp.int32(STATIC_SLOTS), total, pool)
    )[2]


def add(target_ref, to, source_ref, at):
    target_ref[to] = (
        target_ref[to].astype(jnp.float32) + source_ref[at].astype(jnp.float32)
    ).astype(target_ref.dtype)


def back_kernel(*refs, slot):
    t, refs = slot_and_rest(slot, refs)
    tab_ref, _, in_up, in_down, in_over, pool_ref, up_ref, down_ref, over_ref = refs[:9]
    takes = [(entry(tab_ref, t, 3 + k), out) for k, out in enumerate((up_ref, down_ref, over_ref))]
    fold(tab_ref, t + 2, (in_up, in_down, in_over), takes, pool_ref, *refs[9:])


def add_kernel(*refs, slot):
    t, refs = slot_and_rest(slot, refs)
    tab_ref, _, in_up, in_down, in_over, pool_ref = refs[:6]
    fold(tab_ref, t, (in_up, in_down, in_over), [], pool_ref, *refs[6:])


def fold(tab_ref, t, arrived, takes, pool_ref, held_ref, got_ref, sems):
    codes = [entry(tab_ref, t, k) for k in range(3)]
    places = [place_of(c) for c in codes]
    valid = [c >= 0 for c in codes]
    fresh = [c >= FIRST for c in codes]
    same_10 = valid[1] & valid[0] & (places[1] == places[0])
    same_20 = valid[2] & valid[0] & (places[2] == places[0])
    same_21 = valid[2] & valid[1] & (places[2] == places[1]) & jnp.logical_not(same_20)
    alone = [
        valid[0],
        valid[1] & jnp.logical_not(same_10),
        valid[2] & jnp.logical_not(same_20 | same_21),
    ]
    loads = [(v, got, got_ref.at[k]) for k, (v, got) in enumerate(zip(valid, arrived))]
    loads += [
        (a & jnp.logical_not(f), pool_ref.at[p], held_ref.at[k])
        for k, (a, f, p) in enumerate(zip(alone, fresh, places))
    ]
    stores = []
    leaves = [False] * 3
    for k, (code, out) in enumerate(takes):
        leaving = code >= 0
        place = place_of(code)
        found, at = match(place, leaving, places, alone)
        loads.append((leaving & jnp.logical_not(found), pool_ref.at[place], held_ref.at[3 + k]))
        stores.append((leaving, held_ref.at[jnp.where(found, at, 3 + k)], out))
        leaves = [leave | (found & (at == n)) for n, leave in enumerate(leaves)]
    copies(loads, sems)
    for k in range(3):

        @pl.when(alone[k] & fresh[k])
        def _(k=k):
            held_ref[k] = got_ref[k]

        @pl.when(alone[k] & jnp.logical_not(fresh[k]))
        def _(k=k):
            add(held_ref, k, got_ref, k)

    for k, to, here in ((1, 0, same_10), (2, 0, same_20), (2, 1, same_21)):

        @pl.when(here)
        def _(k=k, to=to):
            add(held_ref, to, got_ref, k)

    stores += [
        (a & jnp.logical_not(leave), held_ref.at[k], pool_ref.at[p])
        for k, (a, leave, p) in enumerate(zip(alone, leaves, places))
    ]
    copies(stores, sems)


def home_kernel(tab_ref, pool_ref, *refs, lay):
    arrived, (key_ref, value_ref, own_ref, got_ref, sems) = refs[:6], refs[6:]
    blocks = lay.blocks
    level = tab_ref[lay.device] >> 1
    halves = (
        (pool_ref.at[pl.ds(level * blocks, blocks)], key_ref),
        (pool_ref.at[pl.ds(lay.value_own, blocks)], value_ref),
    )
    loads, stores = [], []
    for k, (source, target) in enumerate(halves):
        held = own_ref.at[pl.ds(k * blocks, blocks)]
        loads.append((level >= 0, source, held))
        stores.append((level >= 0, held, target))
    codes = [entry(tab_ref, 1 - n // 3, n % 3) for n in range(6)]
    for n, (code, got) in enumerate(zip(codes, arrived)):
        loads.append((code >= 0, got, got_ref.at[n]))
    copies(loads, sems)
    for n, code in enumerate(codes):
        place = place_of(code)
        at = jnp.where(
            place >= lay.value_own, place - lay.value_own + blocks, place - level * blocks
        )

        @pl.when(code >= 0)
        def _(n=n, at=at):
            add(own_ref, jnp.clip(at, 0, 2 * blocks - 1), got_ref, n)

    copies(stores, sems)


def return_blocks(pool, tab, total, lay):
    one = jax.ShapeDtypeStruct(pool.shape[1:], pool.dtype)
    pool_shape = jax.ShapeDtypeStruct(pool.shape, pool.dtype)
    own_shape = jax.ShapeDtypeStruct((lay.blocks,) + one.shape, one.dtype)
    size = 2 * math.prod(one.shape)
    up, down, over = routes(lay.ctx_size)
    perms = ([(b, a) for a, b in up], [(b, a) for a, b in down], over)

    scratch = [
        pltpu.VMEM((6,) + one.shape, one.dtype),
        pltpu.VMEM((3,) + one.shape, one.dtype),
        pltpu.SemaphoreType.DMA((9,)),
    ]

    def step(t, pool, got):
        call = dict(
            out_shape=(pool_shape, one, one, one),
            in_specs=[SMEM] + [ANY] * 4,
            out_specs=(ANY,) * 4,
            scratch_shapes=scratch,
            cost_estimate=traffic(size * 15),
            name="return_step",
        )
        pool, *sends = numbered(back_kernel, t, call)(tab, pool, *got)
        return pool, send_all(sends, perms)

    def body(state):
        t, pool = state
        got = send_all(take(t, tab, pool, 3), perms)
        call = dict(
            out_shape=pool_shape,
            in_specs=[SMEM] + [ANY] * 4,
            out_specs=ANY,
            scratch_shapes=scratch,
            cost_estimate=traffic(size * 9),
            name="return_add",
        )
        return t - 1, numbered(add_kernel, t, call)(tab, pool, *got)

    _, pool = lax.while_loop(lambda state: state[0] >= STATIC_SLOTS, body, (total - 1, pool))
    older = send_all(take(STATIC_SLOTS - 1, tab, pool, 3), perms)
    newer = send_all(take(STATIC_SLOTS - 2, tab, pool, 3), perms)
    for t in range(STATIC_SLOTS - 3, -1, -1):
        pool, latest = step(t, pool, older)
        older, newer = newer, latest
    return pl.pallas_call(
        functools.partial(home_kernel, lay=lay),
        out_shape=(own_shape, own_shape),
        in_specs=[SMEM] + [ANY] * 7,
        out_specs=(ANY, ANY),
        scratch_shapes=[
            pltpu.VMEM((2 * lay.blocks,) + one.shape, one.dtype),
            pltpu.VMEM((6,) + one.shape, one.dtype),
            pltpu.SemaphoreType.DMA((8,)),
        ],
        compiler_params=MOVE,
        cost_estimate=traffic(size * 30),
        name="return_home",
    )(tab, pool, *older, *newer)


QK = (((1,), (1,)), ((), ()))
AB = (((1,), (0,)), ((), ()))
TA = (((0,), (0,)), ((), ()))


def dot(a, b, dims):
    return lax.dot_general(a, b, dims, preferred_element_type=jnp.float32)


def rows_of(i):
    return slice(i * BLOCK, (i + 1) * BLOCK)


def parts_of(i, cols, own_ref, pick_refs):
    blocks = len(pick_refs) - 1
    before = pick_refs[blocks][0, :, cols] if i == 0 else own_ref[i - 1, :, cols]
    return own_ref[i, :, cols], before, pick_refs[i][0, :, cols]


def term_places(tab_ref, lay):
    level = tab_ref[lay.device] >> 1
    result = []
    for base, picks in ((level * lay.blocks, lay.key_picks), (lay.value_own, lay.value_picks)):
        places = [base + o for o in range(lay.blocks)]
        places += [tab_ref[picks + j] for j in range(lay.blocks + 1)]
        result.append(places)
    return result


def forward_kernel(tab_ref, *refs, lay, group):
    blocks = lay.blocks
    count = blocks + 2
    q_ref, key_refs, value_refs = refs[0], refs[1 : 1 + count], refs[1 + count : 1 + 2 * count]
    gain_ref, grad_ref, attended_ref, probs_ref, sums_ref, acc_ref = refs[1 + 2 * count :]
    h = pl.program_id(0)
    causal = lax.broadcasted_iota(jnp.int32, (BLOCK, BLOCK), 0) <= lax.broadcasted_iota(
        jnp.int32, (BLOCK, BLOCK), 1
    )
    hide = jnp.where(tab_ref[lay.device] > 0, 0.0, -jnp.inf).astype(jnp.float32)
    lane = lax.broadcasted_iota(jnp.int32, (BLOCK, LANES), 1)

    @pl.when(h == 0)
    def _():
        acc_ref[...] = jnp.zeros_like(acc_ref)

    def score(i, g):
        cols = slice(g * HDIM, (g + 1) * HDIM)
        q = q_ref[rows_of(i), cols]
        return [dot(k, q, QK) for k in parts_of(i, cols, key_refs[0], key_refs[1:])]

    tasks = [(i, g) for i in range(blocks) for g in range(group)]
    following = score(*tasks[0])
    for n, (i, g) in enumerate(tasks):
        scores = following
        if n + 1 < len(tasks):
            following = score(*tasks[n + 1])
        cols = slice(g * HDIM, (g + 1) * HDIM)
        scores[0] = jnp.where(causal, scores[0], -jnp.inf)
        if i == 0:
            scores[1] = scores[1] + hide
        top = jnp.max(
            jnp.maximum(jnp.maximum(scores[0], scores[1]), scores[2]), axis=0, keepdims=True
        )
        weights = [jnp.exp2((s - top) * SCALE_LOG2) for s in scores]
        scale = 1.0 / jnp.sum(weights[0] + weights[1] + weights[2], axis=0, keepdims=True)
        turned = 0.0
        values = parts_of(i, cols, value_refs[0], value_refs[1:])
        for j, (w, v) in enumerate(zip(weights, values)):
            low = (w * scale).astype(jnp.bfloat16)
            probs_ref[i, g, rows_of(j)] = low
            turned += dot(v, low, TA)
        attended = jnp.transpose(turned)
        attended_ref[rows_of(i), cols] = attended
        lifted = gain_ref[:, cols] * grad_ref[rows_of(i), cols].astype(jnp.float32)
        squares = jnp.sum(attended * attended, axis=1, keepdims=True)
        center = jnp.sum(lifted * attended, axis=1, keepdims=True)
        acc_ref[i] += jnp.where(lane == 0, squares, jnp.where(lane == 1, center, 0.0))

    @pl.when(h == pl.num_programs(0) - 1)
    def _():
        for i in range(blocks):
            sums_ref[:, rows_of(i)] = jnp.transpose(acc_ref[i])[:8]


def backward_kernel(
    tab_ref, q_ref, pool_in, gain_ref, grad_ref, attended_ref, probs_ref, *refs, lay, group
):
    del pool_in
    sums_refs, refs = refs[:-9], refs[-9:]
    normed_ref, gq_ref, pool_ref, rms_ref, acc_ref, out_ref, kv_ref, sems, load_sems = refs
    blocks = lay.blocks
    h = pl.program_id(0)
    steps = pl.num_programs(0)
    width = group * HDIM
    terms = 2 * blocks + 1
    places = term_places(tab_ref, lay)
    buffer = lax.rem(h, 2)

    def columns(at):
        return pl.ds(pl.multiple_of(at * width, width), width)

    def loads(at, buffer):
        return [
            pltpu.make_async_copy(
                pool_ref.at[places[kind][n], :, columns(at)],
                kv_ref.at[buffer, kind, n],
                load_sems.at[buffer, kind * terms + n],
            )
            for kind in range(2)
            for n in range(terms)
        ]

    @pl.when(h == 0)
    def _():
        for load in loads(0, 0):
            load.start()

    for load in loads(h, buffer):
        load.wait()

    @pl.when(h + 1 < steps)
    def _():
        for load in loads(h + 1, 1 - buffer):
            load.start()

    @pl.when(h == 0)
    def _():
        sums = sum(ref[...] for ref in sums_refs)
        squares = sums[0:1]
        center = sums[1:2]
        inv = lax.rsqrt(squares / WIDTH + 1e-05)
        factor = inv * inv * inv * center / WIDTH
        both = jnp.concatenate([inv, factor, jnp.zeros((6,) + inv.shape[1:], jnp.float32)], axis=0)
        for i in range(blocks):
            wide = jnp.concatenate([both[:, rows_of(i)]] * (LANES // 8), axis=0)
            rms_ref[i] = jnp.transpose(wide)

    def places_in(i):
        return (i, 2 * blocks if i == 0 else i - 1, blocks + i)

    def prepare(i, g):
        cols = slice(g * HDIM, (g + 1) * HDIM)
        inv_rms = rms_ref[i, :, 0:1]
        factor = rms_ref[i, :, 1:2]
        attended = attended_ref[rows_of(i), cols]
        gain = gain_ref[:, cols]
        normed_ref[rows_of(i), cols] = (attended * inv_rms * gain).astype(jnp.bfloat16)
        lifted = gain * grad_ref[rows_of(i), cols].astype(jnp.float32)
        grad = (inv_rms * lifted - attended * factor).astype(jnp.bfloat16)
        row = jnp.sum(jnp.transpose(grad.astype(jnp.float32) * attended), axis=0, keepdims=True)
        gps = [dot(kv_ref[buffer, 1, n, :, cols], grad, QK) for n in places_in(i)]
        return grad, row, gps

    tasks = [(i, g) for i in range(blocks) for g in range(group)]
    following = prepare(*tasks[0])
    for n, (i, g) in enumerate(tasks):
        grad, row, gps = following
        if n + 1 < len(tasks):
            following = prepare(*tasks[n + 1])
        cols = slice(g * HDIM, (g + 1) * HDIM)
        q = q_ref[rows_of(i), cols]
        gq = 0.0
        for j, at in enumerate(places_in(i)):
            low = probs_ref[i, g, rows_of(j)]
            gv = dot(low, grad, AB)
            gs = (low.astype(jnp.float32) * (gps[j] - row)).astype(jnp.bfloat16)
            gq += dot(kv_ref[buffer, 0, at, :, cols], gs, TA)
            gk = dot(gs, q, AB) * SCALE
            for kind, term in ((0, gk), (1, gv)):
                if j == 0 and i + 1 < blocks:
                    acc_ref[kind, i % 2, g] = term
                elif j == 1 and i > 0:
                    total = acc_ref[kind, at % 2, g] + term
                    out_ref[buffer, kind, at, :, cols] = total.astype(jnp.bfloat16)
                else:
                    out_ref[buffer, kind, at, :, cols] = term.astype(jnp.bfloat16)
        gq_ref[rows_of(i), cols] = (jnp.transpose(gq) * SCALE).astype(jnp.bfloat16)

    jobs = []
    for kind in range(2):
        writes = [steps > 0] * blocks
        for at in range(terms - 1, blocks - 1, -1):
            taken = False
            for to in list(range(blocks)) + list(range(at - 1, blocks - 1, -1)):
                here = (places[kind][at] == places[kind][to]) & jnp.logical_not(taken)
                taken = taken | here

                @pl.when(here)
                def _(kind=kind, at=at, to=to):
                    out_ref[buffer, kind, to] = (
                        out_ref[buffer, kind, to].astype(jnp.float32)
                        + out_ref[buffer, kind, at].astype(jnp.float32)
                    ).astype(jnp.bfloat16)

            writes.insert(blocks, jnp.logical_not(taken))
        for at in range(terms):
            jobs.append((kind, at, places[kind][at], writes[at]))

    def store(n, job, slot_h, buffer):
        kind, at, place, valid = job
        return valid, pltpu.make_async_copy(
            out_ref.at[buffer, kind, at],
            pool_ref.at[place, :, columns(slot_h)],
            sems.at[n],
        )

    for n, job in enumerate(jobs):
        valid, copy = store(n, job, jnp.maximum(h - 1, 0), 1 - buffer)
        pl.when(valid & (h > 0))(copy.wait)
    for n, job in enumerate(jobs):
        valid, copy = store(n, job, h, buffer)
        pl.when(valid)(copy.start)

    @pl.when(h == steps - 1)
    def _():
        for n, job in enumerate(jobs):
            valid, copy = store(n, job, h, buffer)
            pl.when(valid)(copy.wait)


def attention(queries, pool, gain, grad_normed, tab, lay):
    rows, columns = queries.shape
    blocks = lay.blocks
    heads = columns // HDIM
    group = 2 if heads % 2 == 0 else 1
    width = group * HDIM
    row_spec = pl.BlockSpec((rows, width), lambda h, tab: (0, h))
    gain_spec = pl.BlockSpec((1, width), lambda h, tab: (0, h))
    probs_spec = pl.BlockSpec((blocks, group, 3 * BLOCK, BLOCK), lambda h, tab: (0, h, 0, 0))
    sums_spec = pl.BlockSpec((8, rows), lambda h, tab: (0, 0))

    def pick_specs(own, picks):
        specs = [pl.BlockSpec((blocks, BLOCK, width), own)]
        for j in range(blocks + 1):
            specs.append(
                pl.BlockSpec((1, BLOCK, width), lambda h, tab, j=j: (tab[picks + j], 0, h))
            )
        return specs

    pool_specs = pick_specs(lambda h, tab: (tab[lay.device] >> 1, 0, h), lay.key_picks)
    pool_specs += pick_specs(lambda h, tab: (lay.value_own // blocks, 0, h), lay.value_picks)
    common = [row_spec] + pool_specs + [gain_spec, row_spec]
    operands = (queries,) + (pool,) * len(pool_specs) + (gain, grad_normed)

    attended, probs, sums = pl.pallas_call(
        functools.partial(forward_kernel, lay=lay, group=group),
        out_shape=(
            jax.ShapeDtypeStruct((rows, columns), jnp.float32),
            jax.ShapeDtypeStruct((blocks, heads, 3 * BLOCK, BLOCK), jnp.bfloat16),
            jax.ShapeDtypeStruct((8, rows), jnp.float32),
        ),
        grid_spec=pltpu.PrefetchScalarGridSpec(
            num_scalar_prefetch=1,
            grid=(heads // group,),
            in_specs=common,
            out_specs=(row_spec, probs_spec, sums_spec),
            scratch_shapes=[pltpu.VMEM((blocks, BLOCK, LANES), jnp.float32)],
        ),
        compiler_params=BIG,
        cost_estimate=pl.CostEstimate(
            flops=4 * rows * 3 * BLOCK * columns,
            bytes_accessed=50_000_000,
            transcendentals=rows * 3 * BLOCK * heads,
        ),
        name="attention_forward",
    )(tab, *operands)

    heads_size = lax.axis_size("head")
    sums = [sums] + [
        lax.ppermute(sums, "head", [(d, (d + k) % heads_size) for d in range(heads_size)])
        for k in range(1, heads_size)
    ]

    wide = jax.ShapeDtypeStruct((rows, columns), jnp.bfloat16)
    terms = (2, 2 * blocks + 1, BLOCK, width)
    normed, grad_q, pool = pl.pallas_call(
        functools.partial(backward_kernel, lay=lay, group=group),
        out_shape=(wide, wide, jax.ShapeDtypeStruct(pool.shape, pool.dtype)),
        grid_spec=pltpu.PrefetchScalarGridSpec(
            num_scalar_prefetch=1,
            grid=(heads // group,),
            in_specs=[row_spec, ANY, gain_spec, row_spec, row_spec, probs_spec]
            + [sums_spec] * len(sums),
            out_specs=(row_spec, row_spec, ANY),
            scratch_shapes=[
                pltpu.VMEM((blocks, BLOCK, LANES), jnp.float32),
                pltpu.VMEM((2, 2, group, BLOCK, HDIM), jnp.float32),
                pltpu.VMEM((2,) + terms, jnp.bfloat16),
                pltpu.VMEM((2,) + terms, jnp.bfloat16),
                pltpu.SemaphoreType.DMA((2 * terms[1],)),
                pltpu.SemaphoreType.DMA((2, 2 * terms[1])),
            ],
        ),
        input_output_aliases={2: 2},
        compiler_params=BIG,
        cost_estimate=pl.CostEstimate(
            flops=8 * rows * 3 * BLOCK * columns,
            bytes_accessed=70_000_000,
            transcendentals=0,
        ),
        name="attention_backward",
    )(tab, queries, pool, gain, grad_normed, attended, probs, *sums)
    return normed, grad_q, pool


def on_device(queries, key_rows, value_rows, norm_gain, sort_index, grad_normed):
    rows, columns = queries.shape
    blocks = rows // BLOCK
    lay = Layout(lax.axis_size("ctx"), blocks)
    tab, gain = routing_table(sort_index, norm_gain, lay)

    shape3 = (blocks, BLOCK, columns)
    own = (key_rows.reshape(shape3), value_rows.reshape(shape3))
    total = tab[lay.total]
    pool = gather_blocks(*own, tab, total, lay)

    normed, grad_q, pool = attention(queries, pool, gain, grad_normed, tab, lay)
    grad_k, grad_v = return_blocks(pool, tab, total, lay)
    return normed, grad_q, grad_k.reshape(rows, columns), grad_v.reshape(rows, columns)


def solution(mesh):
    in_specs = (
        P("ctx", "head"),
        P("ctx", "head"),
        P("ctx", "head"),
        P("head"),
        P(),
        P("ctx", "head"),
    )
    out_specs = (P("ctx", "head"), P("ctx", "head"), P("ctx", "head"), P("ctx", "head"))
    return jax.shard_map(
        on_device, mesh=mesh, in_specs=in_specs, out_specs=out_specs, check_vma=False
    )
```

```python
import functools
import math

import jax
import jax.numpy as jnp
import numpy as np
from jax import lax
from jax.experimental import pallas as pl
from jax.experimental.pallas import tpu as pltpu
from jax.sharding import PartitionSpec as P

HDIM = 128
BLOCK = 256
WIDTH = 5120
LANES = 128
ROW = 16
LEAD = 2
FIRST = 1024
STATIC_SLOTS = 9
SCALE = HDIM ** (-0.5)
SCALE_LOG2 = SCALE * math.log2(math.e)
ANY = pl.BlockSpec(memory_space=pl.ANY)
SMEM = pl.BlockSpec(memory_space=pltpu.SMEM)
VMEM = pl.BlockSpec(memory_space=pltpu.VMEM)
BIG = pltpu.CompilerParams(vmem_limit_bytes=56 * 1024 * 1024)
MOVE = pltpu.CompilerParams(vmem_limit_bytes=40 * 1024 * 1024)


class Layout:
    def __init__(self, ctx_size, blocks):
        self.ctx_size = ctx_size
        self.blocks = blocks
        self.levels = ctx_size // 2
        line = self.levels * blocks
        self.value_line = line
        self.value_own = 2 * line
        self.over = 2 * line + blocks
        self.places = self.over + 2 * (blocks + 1)
        self.slots = 2 * (2 * line + 2 * self.levels + 2 * blocks + 4)
        self.rows = self.slots + 2 * LEAD
        self.info = self.rows * ROW
        self.key_picks = self.info
        self.value_picks = self.info + blocks + 1
        self.total = self.info + 2 * blocks + 2
        self.device = self.info + 2 * blocks + 3


def shift_rows(array, count, rows):
    n = array.shape[0]
    if abs(count) >= n:
        return jnp.zeros_like(array)
    rolled = pltpu.roll(array, (-count) % n, 0)
    inside = (rows < n - count) if count > 0 else (rows >= -count)
    return jnp.where(inside, rolled, 0.0)


def table_kernel(picks_ref, gain_ref, out_ref, gain_row_ref, *, lay):
    n = lay.ctx_size
    blocks = lay.blocks
    count = n * blocks
    width = -(-2 * count // LANES) * LANES
    rows = lax.broadcasted_iota(jnp.int32, (n, width), 0)
    lanes = lax.broadcasted_iota(jnp.int32, (n, width), 1)
    out_lanes = lax.broadcasted_iota(jnp.int32, (n, LANES), 1)
    values = lanes >= count
    block = jnp.where(lanes >= 2 * count, -2, jnp.where(values, lanes - count, lanes))
    owner = jnp.floor((block.astype(jnp.float32) + 0.5) / blocks).astype(jnp.int32)
    within = block - owner * blocks
    line = (owner >> 1) * blocks + within
    place = jnp.where(values, jnp.where(owner == rows, lay.value_own + within, lay.value_line + line), line)
    place = jnp.where(block < 0, 0, place).astype(jnp.float32)
    picks = picks_ref[...]
    side = rows & 1
    level = rows >> 1
    same_side = side == (owner & 1)
    travels = jnp.logical_xor(same_side, values)
    owned = owner == rows

    def other(array):
        return jnp.where(side == 0, pltpu.roll(array, n - 1, 0), pltpu.roll(array, 1, 0))

    need = jnp.zeros((n, width), jnp.float32)
    for j in range(blocks + 1):
        need = jnp.where(picks[:, j : j + 1] == block, 1.0, need)
    need = jnp.where(owned, 0.0, need)
    across = other(need)
    wanted = jnp.maximum(need, across)
    final = jnp.where(travels, across, 0.0)
    hops = jnp.where(wanted > 0, 1.0 + final, 0.0)
    up_hops = jnp.zeros_like(need)
    down_hops = jnp.zeros_like(need)
    for k in range(1, lay.levels):
        above = shift_rows(hops, 2 * k, rows)
        below = shift_rows(hops, -2 * k, rows)
        up_hops = jnp.maximum(up_hops, jnp.where(above > 0, above + (k - 1), 0.0))
        down_hops = jnp.maximum(down_hops, jnp.where(below > 0, below + (k - 1), 0.0))
    up = jnp.where(travels & (level >= (owner >> 1)) & (up_hops > 0), 1.0, 0.0)
    down = jnp.where(travels & (level <= (owner >> 1)) & (down_hops > 0), 1.0, 0.0)
    source = owned & jnp.logical_not(travels)
    most = jnp.maximum(up_hops, down_hops)
    over = jnp.where(source & ((most > 0) | (across > 0)), 1.0, final)
    spread = jnp.minimum(jnp.sum(need, axis=0, keepdims=True), 3.0)
    low = (width - 1 - lanes).astype(jnp.float32)
    up_rank = (up_hops * 4.0 + spread) * width + low
    down_rank = (down_hops * 4.0 + spread) * width + low
    over_rank = jnp.where(source, most * 4.0 + spread, 2.0) * width + low
    first_over = float(lay.over)

    gain_row_ref[0, :] = gain_ref[:]
    out_ref[...] = jnp.full(out_ref.shape, -1, jnp.int32)

    def pick(pending, have, rank):
        score = jnp.where(pending * have > 0, rank, -1.0)
        best = jnp.max(score, axis=1, keepdims=True)
        return jnp.where((score == best) & (best >= 0), 1.0, 0.0)

    def where(chosen):
        return jnp.sum(chosen * (place + 1.0), axis=1, keepdims=True) - 1.0

    def pending(state):
        t, have, fresh, up, down, over, over_place, count = state
        return (t < lay.slots) & (jnp.sum(up + down + over) > 0)

    def step(state):
        t, have, fresh, up, down, over, over_place, count = state
        send_up = pick(up, have, up_rank)
        send_down = pick(down, have, down_rank)
        send_over = pick(over, have, over_rank)
        up = up - send_up
        down = down - send_down
        over = over - send_over
        got_up = shift_rows(send_up, -2, rows)
        got_down = shift_rows(send_down, 2, rows)
        got_over = other(send_over)
        got_final = jnp.where(travels, 0.0, got_over)
        any_final = jnp.max(got_final, axis=1, keepdims=True)
        over_at = jnp.where(any_final > 0, count + first_over, where(got_over))
        last = jnp.where((up + down + over + need > 0) | owned, 0.0, float(FIRST))

        def first_back(chosen):
            return jnp.max(chosen * last, axis=1, keepdims=True)

        columns = (
            where(send_up) + first_back(send_up),
            where(send_down) + first_back(send_down * (1.0 - send_up)),
            where(send_over) + first_back(send_over * (1.0 - send_up) * (1.0 - send_down)),
            where(got_up),
            where(got_down),
            over_at,
        )
        row = jnp.full((n, LANES), -1.0, jnp.float32)
        for k, column in enumerate(columns):
            row = jnp.where(out_lanes == k, column, row)
        out_ref[t + LEAD] = row.astype(jnp.int32)
        over_place = jnp.where(got_final > 0, count + first_over, over_place)
        have = jnp.maximum(have, fresh)
        fresh = jnp.maximum(got_up, jnp.maximum(got_down, got_over))
        return (t + 1, have, fresh, up, down, over, over_place, count + any_final)

    zeros = jnp.zeros_like(need)
    have = jnp.where(owned, 1.0, 0.0)
    state = (jnp.int32(0), have, zeros, up, down, over, zeros, jnp.zeros((n, 1), jnp.float32))
    state = lax.while_loop(pending, step, state)
    at = jnp.where(travels | owned, place, state[6])
    own_row = lax.broadcasted_iota(jnp.int32, (n, LANES), 0)
    row = jnp.zeros((n, LANES), jnp.float32)
    for kind in range(2):
        base = (own_row >> 1) * blocks if kind == 0 else jnp.full((n, LANES), lay.value_own)
        for j in range(blocks + 1):
            chosen = (picks[:, j : j + 1] == block) & (values if kind else jnp.logical_not(values))
            found = jnp.sum(jnp.where(chosen, at, 0.0), axis=1, keepdims=True)
            found = jnp.where(picks[:, j : j + 1] < 0, base[:, :1].astype(jnp.float32), found)
            row = jnp.where(out_lanes == kind * (blocks + 1) + j, found, row)
    row = jnp.where(out_lanes == 2 * blocks + 2, state[0].astype(jnp.float32), row)
    row = jnp.where(out_lanes == 2 * blocks + 3, own_row.astype(jnp.float32), row)
    out_ref[lay.rows] = row.astype(jnp.int32)


def routing_table(sort_index, norm_gain, lay):
    n, blocks = lay.ctx_size, lay.blocks
    before = (np.arange(n, dtype=np.int32) * blocks - 1)[:, None]
    picks = jnp.concatenate([sort_index.reshape(n, blocks), jnp.asarray(before)], axis=1)
    picks = jnp.pad(picks, ((0, 0), (0, LANES - blocks - 1)), constant_values=-1)
    table, gain = pl.pallas_call(
        functools.partial(table_kernel, lay=lay),
        out_shape=(
            jax.ShapeDtypeStruct((lay.rows + 1, n, LANES), jnp.int32),
            jax.ShapeDtypeStruct((1,) + norm_gain.shape, norm_gain.dtype),
        ),
        in_specs=[VMEM, VMEM],
        out_specs=(VMEM, VMEM),
        name="routing_table",
    )(picks, norm_gain)
    mine = lax.dynamic_slice(table, (0, lax.axis_index("ctx"), 0), (lay.rows + 1, 1, ROW))
    return mine.reshape((lay.rows + 1) * ROW), gain


def routes(ctx_size):
    up = [(d, d + 2) for d in range(ctx_size - 2)]
    down = [(d + 2, d) for d in range(ctx_size - 2)]
    over = [(d, d ^ 1) for d in range(ctx_size)]
    return up, down, over


def copies(jobs, sems):
    started = []
    for k, (valid, source, target) in enumerate(jobs):
        copy = pltpu.make_async_copy(source, target, sems.at[k])
        pl.when(valid)(copy.start)
        started.append((valid, copy))
    for valid, copy in started:
        pl.when(valid)(copy.wait)


def entry(tab_ref, t, k):
    return tab_ref[(t + LEAD) * ROW + k]


def place_of(code):
    return jnp.maximum(code, 0) & (FIRST - 1)


def fill_kernel(tab_ref, key_ref, value_ref, pool_ref, held_ref, sems, *, lay):
    blocks = lay.blocks
    level = tab_ref[lay.device] >> 1
    loads = [
        pltpu.make_async_copy(key_ref, held_ref.at[pl.ds(0, blocks)], sems.at[0]),
        pltpu.make_async_copy(value_ref, held_ref.at[pl.ds(blocks, blocks)], sems.at[1]),
    ]
    stores = [
        pltpu.make_async_copy(
            held_ref.at[pl.ds(0, blocks)], pool_ref.at[pl.ds(level * blocks, blocks)], sems.at[2]
        ),
        pltpu.make_async_copy(
            held_ref.at[pl.ds(blocks, blocks)],
            pool_ref.at[pl.ds(lay.value_own, blocks)],
            sems.at[3],
        ),
    ]
    for load in loads:
        load.start()
    for load, store in zip(loads, stores):
        load.wait()
        store.start()
    for store in stores:
        store.wait()


def first_kernel(
    tab_ref, key_ref, value_ref, up_ref, down_ref, over_ref, held_ref, sems, *, lay, slot
):
    blocks = lay.blocks
    level = tab_ref[lay.device] >> 1
    loads, stores = [], []
    for k, out in enumerate((up_ref, down_ref, over_ref)):
        code = entry(tab_ref, slot, k)
        at = place_of(code)
        is_value = at >= lay.value_own
        key_at = jnp.clip(at - level * blocks, 0, blocks - 1)
        value_at = jnp.clip(at - lay.value_own, 0, blocks - 1)
        valid = code >= 0
        loads.append((valid & jnp.logical_not(is_value), key_ref.at[key_at], held_ref.at[k]))
        loads.append((valid & is_value, value_ref.at[value_at], held_ref.at[k]))
        stores.append((valid, held_ref.at[k], out))
    copies(loads, sems)
    copies(stores, sems)


def slot_and_rest(slot, refs):
    return (refs[0][0], refs[1:]) if slot is None else (slot, refs)


def match(place, valid, places, valids):
    hits = [valid & v & (place == p) for p, v in zip(places, valids)]
    found = hits[0] | hits[1] | hits[2]
    return found, jnp.where(hits[0], 0, jnp.where(hits[1], 1, 2))


def step_kernel(*refs, slot):
    t, refs = slot_and_rest(slot, refs)
    (
        tab_ref, _, in_up, in_down, in_over, pool_ref, up_ref, down_ref, over_ref, held_ref, sems,
    ) = refs
    got_codes = [entry(tab_ref, t - 2, 3 + k) for k in range(3)]
    got_valid = [c >= 0 for c in got_codes]
    got_places = [place_of(c) for c in got_codes]
    loads = [
        (v, got, held_ref.at[k])
        for k, (v, got) in enumerate(zip(got_valid, (in_up, in_down, in_over)))
    ]
    stores = [
        (v, held_ref.at[k], pool_ref.at[p])
        for k, (v, p) in enumerate(zip(got_valid, got_places))
    ]
    for k, out in enumerate((up_ref, down_ref, over_ref)):
        code = entry(tab_ref, t, k)
        valid = code >= 0
        place = place_of(code)
        found, at = match(place, valid, got_places, got_valid)
        loads.append((valid & jnp.logical_not(found), pool_ref.at[place], held_ref.at[3 + k]))
        stores.append((valid, held_ref.at[jnp.where(found, at, 3 + k)], out))
    copies(loads, sems)
    copies(stores, sems)


def close_kernel(*refs, slot):
    t, refs = slot_and_rest(slot, refs)
    tab_ref, _, in_up, in_down, in_over, pool_ref, held_ref, sems = refs
    loads, stores = [], []
    for k, got in enumerate((in_up, in_down, in_over)):
        code = entry(tab_ref, t, 3 + k)
        loads.append((code >= 0, got, held_ref.at[k]))
        stores.append((code >= 0, held_ref.at[k], pool_ref.at[place_of(code)]))
    copies(loads, sems)
    copies(stores, sems)


def take_kernel(*refs, slot, first):
    t, refs = slot_and_rest(slot, refs)
    tab_ref, pool_ref, up_ref, down_ref, over_ref, held_ref, sems = refs
    loads, stores = [], []
    for k, out in enumerate((up_ref, down_ref, over_ref)):
        code = entry(tab_ref, t, first + k)
        loads.append((code >= 0, pool_ref.at[place_of(code)], held_ref.at[k]))
        stores.append((code >= 0, held_ref.at[k], out))
    copies(loads, sems)
    copies(stores, sems)


def traffic(byte_count):
    return pl.CostEstimate(flops=0, bytes_accessed=byte_count, transcendentals=0)


def take(t, tab, pool, first):
    one = jax.ShapeDtypeStruct(pool.shape[1:], pool.dtype)
    call = dict(
        out_shape=(one,) * 3,
        in_specs=[SMEM, ANY],
        out_specs=(ANY,) * 3,
        scratch_shapes=[pltpu.VMEM((3,) + one.shape, one.dtype), pltpu.SemaphoreType.DMA((3,))],
        cost_estimate=traffic(12 * math.prod(one.shape)),
        name="take_step",
        in_place=False,
    )
    return numbered(functools.partial(take_kernel, first=first), t, call)(tab, pool)


def send_all(sends, perms):
    return tuple(lax.ppermute(s, "ctx", p) for s, p in zip(sends, perms))


def numbered(kernel, t, call):
    known = isinstance(t, int)
    extra = [] if known else [t.reshape(1)]
    specs = [] if known else [SMEM]
    return functools.partial(
        pl.pallas_call(
            functools.partial(kernel, slot=t if known else None),
            in_specs=specs + call.pop("in_specs"),
            input_output_aliases={1 + len(extra): 0} if call.pop("in_place", True) else {},
            compiler_params=MOVE,
            **call,
        ),
        *extra,
    )


def gather_blocks(keys, values, tab, total, lay):
    one = jax.ShapeDtypeStruct(keys.shape[1:], keys.dtype)
    pool_shape = jax.ShapeDtypeStruct((lay.places,) + one.shape, one.dtype)
    size = 2 * math.prod(one.shape)
    perms = routes(lay.ctx_size)
    six = [pltpu.VMEM((6,) + one.shape, one.dtype), pltpu.SemaphoreType.DMA((6,))]

    def first(slot):
        sends = pl.pallas_call(
            functools.partial(first_kernel, lay=lay, slot=slot),
            out_shape=(one,) * 3,
            in_specs=[SMEM, ANY, ANY],
            out_specs=(ANY,) * 3,
            scratch_shapes=six,
            compiler_params=MOVE,
            cost_estimate=traffic(size * 6),
            name="gather_first",
        )(tab, keys, values)
        return send_all(sends, perms)

    older = first(0)
    newer = first(1)
    pool = pl.pallas_call(
        functools.partial(fill_kernel, lay=lay),
        out_shape=pool_shape,
        in_specs=[SMEM, ANY, ANY],
        out_specs=ANY,
        scratch_shapes=[
            pltpu.VMEM((2 * lay.blocks,) + one.shape, one.dtype),
            pltpu.SemaphoreType.DMA((4,)),
        ],
        compiler_params=MOVE,
        cost_estimate=traffic(size * 4 * lay.blocks),
        name="gather_fill",
    )(tab, keys, values)

    def step(t, pool, got):
        call = dict(
            out_shape=(pool_shape, one, one, one),
            in_specs=[SMEM] + [ANY] * 4,
            out_specs=(ANY,) * 4,
            scratch_shapes=six,
            cost_estimate=traffic(size * 12),
            name="gather_step",
        )
        pool, *sends = numbered(step_kernel, t, call)(tab, pool, *got)
        return pool, send_all(sends, perms)

    for t in range(2, STATIC_SLOTS):
        pool, latest = step(t, pool, older)
        older, newer = newer, latest

    def close(t, pool, got):
        call = dict(
            out_shape=pool_shape,
            in_specs=[SMEM] + [ANY] * 4,
            out_specs=ANY,
            scratch_shapes=six,
            cost_estimate=traffic(size * 6),
            name="gather_close",
        )
        return numbered(close_kernel, t, call)(tab, pool, *got)

    pool = close(STATIC_SLOTS - 2, pool, older)
    pool = close(STATIC_SLOTS - 1, pool, newer)

    def body(state):
        t, end, pool = state
        got = send_all(take(t, tab, pool, 0), perms)
        return t + 1, end, close(t, pool, got)

    return lax.while_loop(
        lambda state: state[0] < state[1], body, (jnp.int32(STATIC_SLOTS), total, pool)
    )[2]


def add(target_ref, to, source_ref, at):
    target_ref[to] = (
        target_ref[to].astype(jnp.float32) + source_ref[at].astype(jnp.float32)
    ).astype(target_ref.dtype)


def same_blocks(places, valid):
    same_10 = valid[1] & valid[0] & (places[1] == places[0])
    same_20 = valid[2] & valid[0] & (places[2] == places[0])
    same_21 = valid[2] & valid[1] & (places[2] == places[1]) & jnp.logical_not(same_20)
    alone = [
        valid[0],
        valid[1] & jnp.logical_not(same_10),
        valid[2] & jnp.logical_not(same_20 | same_21),
    ]
    return alone, ((1, 0, same_10), (2, 0, same_20), (2, 1, same_21))


def add_doubles(doubles, held_ref, got_ref):
    for k, to, here in doubles:

        @pl.when(here)
        def _(k=k, to=to):
            add(held_ref, to, got_ref, k)


def back_kernel(*refs, slot):
    t, refs = slot_and_rest(slot, refs)
    tab_ref, _, in_up, in_down, in_over, pool_ref, up_ref, down_ref, over_ref = refs[:9]
    takes = [(entry(tab_ref, t, 3 + k), out) for k, out in enumerate((up_ref, down_ref, over_ref))]
    fold(tab_ref, t + 2, (in_up, in_down, in_over), takes, pool_ref, *refs[9:])


def add_kernel(*refs, slot):
    t, refs = slot_and_rest(slot, refs)
    tab_ref, _, in_up, in_down, in_over, pool_ref = refs[:6]
    fold(tab_ref, t, (in_up, in_down, in_over), [], pool_ref, *refs[6:])


def fold(tab_ref, t, arrived, takes, pool_ref, held_ref, got_ref, sems):
    codes = [entry(tab_ref, t, k) for k in range(3)]
    places = [place_of(c) for c in codes]
    valid = [c >= 0 for c in codes]
    fresh = [c >= FIRST for c in codes]
    alone, doubles = same_blocks(places, valid)
    loads = [(v, got, got_ref.at[k]) for k, (v, got) in enumerate(zip(valid, arrived))]
    loads += [
        (a & jnp.logical_not(f), pool_ref.at[p], held_ref.at[k])
        for k, (a, f, p) in enumerate(zip(alone, fresh, places))
    ]
    stores = []
    leaves = [False] * 3
    for k, (code, out) in enumerate(takes):
        leaving = code >= 0
        place = place_of(code)
        found, at = match(place, leaving, places, alone)
        loads.append((leaving & jnp.logical_not(found), pool_ref.at[place], held_ref.at[3 + k]))
        stores.append((leaving, held_ref.at[jnp.where(found, at, 3 + k)], out))
        leaves = [leave | (found & (at == n)) for n, leave in enumerate(leaves)]
    copies(loads, sems)
    for k in range(3):

        @pl.when(alone[k] & fresh[k])
        def _(k=k):
            held_ref[k] = got_ref[k]

        @pl.when(alone[k] & jnp.logical_not(fresh[k]))
        def _(k=k):
            add(held_ref, k, got_ref, k)

    add_doubles(doubles, held_ref, got_ref)
    stores += [
        (a & jnp.logical_not(leave), held_ref.at[k], pool_ref.at[p])
        for k, (a, leave, p) in enumerate(zip(alone, leaves, places))
    ]
    copies(stores, sems)


def own_index(place, tab_ref, lay):
    is_value = place >= lay.value_own
    base = jnp.where(is_value, lay.value_own, (tab_ref[lay.device] >> 1) * lay.blocks)
    return is_value, jnp.clip(place - base, 0, lay.blocks - 1)


def home_kernel(
    tab_ref, pool_ref, in_up, in_down, in_over, key_ref, value_ref, own_ref, got_ref, sems, *, lay
):
    blocks = lay.blocks
    level = tab_ref[lay.device] >> 1
    halves = (
        (pool_ref.at[pl.ds(level * blocks, blocks)], key_ref),
        (pool_ref.at[pl.ds(lay.value_own, blocks)], value_ref),
    )
    loads, stores = [], []
    for k, (source, target) in enumerate(halves):
        held = own_ref.at[pl.ds(k * blocks, blocks)]
        loads.append((level >= 0, source, held))
        stores.append((level >= 0, held, target))
    codes = [entry(tab_ref, 1, k) for k in range(3)]
    for k, (code, got) in enumerate(zip(codes, (in_up, in_down, in_over))):
        loads.append((code >= 0, got, got_ref.at[k]))
    copies(loads, sems)
    for k, code in enumerate(codes):
        is_value, at = own_index(place_of(code), tab_ref, lay)

        @pl.when(code >= 0)
        def _(k=k, at=jnp.where(is_value, blocks + at, at)):
            add(own_ref, at, got_ref, k)

    copies(stores, sems)


def last_kernel(
    tab_ref, key_in, value_in, in_up, in_down, in_over, key_ref, value_ref, held_ref, got_ref, sems,
    *, lay,
):
    del key_in, value_in
    codes = [entry(tab_ref, 0, k) for k in range(3)]
    places = [place_of(c) for c in codes]
    valid = [c >= 0 for c in codes]
    alone, doubles = same_blocks(places, valid)
    loads, stores = [], []
    for k, got in enumerate((in_up, in_down, in_over)):
        loads.append((valid[k], got, got_ref.at[k]))
        is_value, at = own_index(places[k], tab_ref, lay)
        for out, here in ((key_ref, jnp.logical_not(is_value)), (value_ref, is_value)):
            loads.append((alone[k] & here, out.at[at], held_ref.at[k]))
            stores.append((alone[k] & here, held_ref.at[k], out.at[at]))
    copies(loads, sems)
    for k in range(3):

        @pl.when(alone[k])
        def _(k=k):
            add(held_ref, k, got_ref, k)

    add_doubles(doubles, held_ref, got_ref)
    copies(stores, sems)


def return_blocks(pool, tab, total, lay):
    one = jax.ShapeDtypeStruct(pool.shape[1:], pool.dtype)
    pool_shape = jax.ShapeDtypeStruct(pool.shape, pool.dtype)
    own_shape = jax.ShapeDtypeStruct((lay.blocks,) + one.shape, one.dtype)
    size = 2 * math.prod(one.shape)
    up, down, over = routes(lay.ctx_size)
    perms = ([(b, a) for a, b in up], [(b, a) for a, b in down], over)

    scratch = [
        pltpu.VMEM((6,) + one.shape, one.dtype),
        pltpu.VMEM((3,) + one.shape, one.dtype),
        pltpu.SemaphoreType.DMA((9,)),
    ]

    def step(t, pool, got):
        call = dict(
            out_shape=(pool_shape, one, one, one),
            in_specs=[SMEM] + [ANY] * 4,
            out_specs=(ANY,) * 4,
            scratch_shapes=scratch,
            cost_estimate=traffic(size * 15),
            name="return_step",
        )
        pool, *sends = numbered(back_kernel, t, call)(tab, pool, *got)
        return pool, send_all(sends, perms)

    def body(state):
        t, pool = state
        got = send_all(take(t, tab, pool, 3), perms)
        call = dict(
            out_shape=pool_shape,
            in_specs=[SMEM] + [ANY] * 4,
            out_specs=ANY,
            scratch_shapes=scratch,
            cost_estimate=traffic(size * 9),
            name="return_add",
        )
        return t - 1, numbered(add_kernel, t, call)(tab, pool, *got)

    _, pool = lax.while_loop(lambda state: state[0] >= STATIC_SLOTS, body, (total - 1, pool))
    older = send_all(take(STATIC_SLOTS - 1, tab, pool, 3), perms)
    newer = send_all(take(STATIC_SLOTS - 2, tab, pool, 3), perms)
    for t in range(STATIC_SLOTS - 3, -1, -1):
        pool, latest = step(t, pool, older)
        older, newer = newer, latest
    three = [pltpu.VMEM((3,) + one.shape, one.dtype)]
    sums = pl.pallas_call(
        functools.partial(home_kernel, lay=lay),
        out_shape=(own_shape, own_shape),
        in_specs=[SMEM] + [ANY] * 4,
        out_specs=(ANY, ANY),
        scratch_shapes=[pltpu.VMEM((2 * lay.blocks,) + one.shape, one.dtype)]
        + three
        + [pltpu.SemaphoreType.DMA((5,))],
        compiler_params=MOVE,
        cost_estimate=traffic(size * 24),
        name="return_home",
    )(tab, pool, *older)
    return pl.pallas_call(
        functools.partial(last_kernel, lay=lay),
        out_shape=(own_shape, own_shape),
        in_specs=[SMEM] + [ANY] * 5,
        out_specs=(ANY, ANY),
        scratch_shapes=three * 2 + [pltpu.SemaphoreType.DMA((9,))],
        input_output_aliases={1: 0, 2: 1},
        compiler_params=MOVE,
        cost_estimate=traffic(size * 9),
        name="return_last",
    )(tab, *sums, *newer)


QK = (((1,), (1,)), ((), ()))
AB = (((1,), (0,)), ((), ()))
TA = (((0,), (0,)), ((), ()))


def dot(a, b, dims):
    return lax.dot_general(a, b, dims, preferred_element_type=jnp.float32)


def rows_of(i):
    return slice(i * BLOCK, (i + 1) * BLOCK)


def parts_of(i, cols, own_ref, pick_refs):
    blocks = len(pick_refs) - 1
    before = pick_refs[blocks][0, :, cols] if i == 0 else own_ref[i - 1, :, cols]
    return own_ref[i, :, cols], before, pick_refs[i][0, :, cols]


def term_places(tab_ref, lay):
    level = tab_ref[lay.device] >> 1
    result = []
    for base, picks in ((level * lay.blocks, lay.key_picks), (lay.value_own, lay.value_picks)):
        places = [base + o for o in range(lay.blocks)]
        places += [tab_ref[picks + j] for j in range(lay.blocks + 1)]
        result.append(places)
    return result


def forward_kernel(tab_ref, *refs, lay, group):
    blocks = lay.blocks
    count = blocks + 2
    q_ref, key_refs, value_refs = refs[0], refs[1 : 1 + count], refs[1 + count : 1 + 2 * count]
    gain_ref, grad_ref, attended_ref, probs_ref, sums_ref, acc_ref = refs[1 + 2 * count :]
    h = pl.program_id(0)
    causal = lax.broadcasted_iota(jnp.int32, (BLOCK, BLOCK), 0) <= lax.broadcasted_iota(
        jnp.int32, (BLOCK, BLOCK), 1
    )
    hide = jnp.where(tab_ref[lay.device] > 0, 0.0, -jnp.inf).astype(jnp.float32)
    lane = lax.broadcasted_iota(jnp.int32, (BLOCK, LANES), 1)

    @pl.when(h == 0)
    def _():
        acc_ref[...] = jnp.zeros_like(acc_ref)

    def score(i, g):
        cols = slice(g * HDIM, (g + 1) * HDIM)
        q = q_ref[rows_of(i), cols]
        return [dot(k, q, QK) for k in parts_of(i, cols, key_refs[0], key_refs[1:])]

    tasks = [(i, g) for i in range(blocks) for g in range(group)]
    following = score(*tasks[0])
    for n, (i, g) in enumerate(tasks):
        scores = following
        if n + 1 < len(tasks):
            following = score(*tasks[n + 1])
        cols = slice(g * HDIM, (g + 1) * HDIM)
        scores[0] = jnp.where(causal, scores[0], -jnp.inf)
        if i == 0:
            scores[1] = scores[1] + hide
        top = jnp.max(
            jnp.maximum(jnp.maximum(scores[0], scores[1]), scores[2]), axis=0, keepdims=True
        )
        weights = [jnp.exp2((s - top) * SCALE_LOG2) for s in scores]
        scale = 1.0 / jnp.sum(weights[0] + weights[1] + weights[2], axis=0, keepdims=True)
        turned = 0.0
        values = parts_of(i, cols, value_refs[0], value_refs[1:])
        for j, (w, v) in enumerate(zip(weights, values)):
            low = (w * scale).astype(jnp.bfloat16)
            probs_ref[i, g, rows_of(j)] = low
            turned += dot(v, low, TA)
        attended = jnp.transpose(turned)
        attended_ref[rows_of(i), cols] = attended
        lifted = gain_ref[:, cols] * grad_ref[rows_of(i), cols].astype(jnp.float32)
        squares = jnp.sum(attended * attended, axis=1, keepdims=True)
        center = jnp.sum(lifted * attended, axis=1, keepdims=True)
        acc_ref[i] += jnp.where(lane == 0, squares, jnp.where(lane == 1, center, 0.0))

    @pl.when(h == pl.num_programs(0) - 1)
    def _():
        for i in range(blocks):
            sums_ref[:, rows_of(i)] = jnp.transpose(acc_ref[i])[:8]


def backward_kernel(
    tab_ref, q_ref, pool_in, gain_ref, grad_ref, attended_ref, probs_ref, *refs, lay, group
):
    del pool_in
    sums_refs, refs = refs[:-9], refs[-9:]
    normed_ref, gq_ref, pool_ref, rms_ref, acc_ref, out_ref, kv_ref, sems, load_sems = refs
    blocks = lay.blocks
    h = pl.program_id(0)
    steps = pl.num_programs(0)
    width = group * HDIM
    terms = 2 * blocks + 1
    places = term_places(tab_ref, lay)
    buffer = lax.rem(h, 2)

    def columns(at):
        return pl.ds(pl.multiple_of(at * width, width), width)

    def loads(at, buffer):
        return [
            pltpu.make_async_copy(
                pool_ref.at[places[kind][n], :, columns(at)],
                kv_ref.at[buffer, kind, n],
                load_sems.at[buffer, kind * terms + n],
            )
            for kind in range(2)
            for n in range(terms)
        ]

    @pl.when(h == 0)
    def _():
        for load in loads(0, 0):
            load.start()

    for load in loads(h, buffer):
        load.wait()

    @pl.when(h + 1 < steps)
    def _():
        for load in loads(h + 1, 1 - buffer):
            load.start()

    @pl.when(h == 0)
    def _():
        sums = sum(ref[...] for ref in sums_refs)
        squares = sums[0:1]
        center = sums[1:2]
        inv = lax.rsqrt(squares / WIDTH + 1e-05)
        factor = inv * inv * inv * center / WIDTH
        both = jnp.concatenate([inv, factor, jnp.zeros((6,) + inv.shape[1:], jnp.float32)], axis=0)
        for i in range(blocks):
            wide = jnp.concatenate([both[:, rows_of(i)]] * (LANES // 8), axis=0)
            rms_ref[i] = jnp.transpose(wide)

    def places_in(i):
        return (i, 2 * blocks if i == 0 else i - 1, blocks + i)

    def prepare(i, g):
        cols = slice(g * HDIM, (g + 1) * HDIM)
        inv_rms = rms_ref[i, :, 0:1]
        factor = rms_ref[i, :, 1:2]
        attended = attended_ref[rows_of(i), cols]
        gain = gain_ref[:, cols]
        normed_ref[rows_of(i), cols] = (attended * inv_rms * gain).astype(jnp.bfloat16)
        lifted = gain * grad_ref[rows_of(i), cols].astype(jnp.float32)
        grad = (inv_rms * lifted - attended * factor).astype(jnp.bfloat16)
        row = jnp.sum(jnp.transpose(grad.astype(jnp.float32) * attended), axis=0, keepdims=True)
        gps = [dot(kv_ref[buffer, 1, n, :, cols], grad, QK) for n in places_in(i)]
        return grad, row, gps

    tasks = [(i, g) for i in range(blocks) for g in range(group)]
    following = prepare(*tasks[0])
    for n, (i, g) in enumerate(tasks):
        grad, row, gps = following
        if n + 1 < len(tasks):
            following = prepare(*tasks[n + 1])
        cols = slice(g * HDIM, (g + 1) * HDIM)
        q = q_ref[rows_of(i), cols]
        gq = 0.0
        for j, at in enumerate(places_in(i)):
            low = probs_ref[i, g, rows_of(j)]
            gv = dot(low, grad, AB)
            gs = (low.astype(jnp.float32) * (gps[j] - row)).astype(jnp.bfloat16)
            gq += dot(kv_ref[buffer, 0, at, :, cols], gs, TA)
            gk = dot(gs, q, AB) * SCALE
            for kind, term in ((0, gk), (1, gv)):
                if j == 0 and i + 1 < blocks:
                    acc_ref[kind, i % 2, g] = term
                elif j == 1 and i > 0:
                    total = acc_ref[kind, at % 2, g] + term
                    out_ref[buffer, kind, at, :, cols] = total.astype(jnp.bfloat16)
                else:
                    out_ref[buffer, kind, at, :, cols] = term.astype(jnp.bfloat16)
        gq_ref[rows_of(i), cols] = (jnp.transpose(gq) * SCALE).astype(jnp.bfloat16)

    jobs = []
    for kind in range(2):
        writes = [steps > 0] * blocks
        for at in range(terms - 1, blocks - 1, -1):
            taken = False
            for to in list(range(blocks)) + list(range(at - 1, blocks - 1, -1)):
                here = (places[kind][at] == places[kind][to]) & jnp.logical_not(taken)
                taken = taken | here

                @pl.when(here)
                def _(kind=kind, at=at, to=to):
                    out_ref[buffer, kind, to] = (
                        out_ref[buffer, kind, to].astype(jnp.float32)
                        + out_ref[buffer, kind, at].astype(jnp.float32)
                    ).astype(jnp.bfloat16)

            writes.insert(blocks, jnp.logical_not(taken))
        for at in range(terms):
            jobs.append((kind, at, places[kind][at], writes[at]))

    def store(n, job, slot_h, buffer):
        kind, at, place, valid = job
        return valid, pltpu.make_async_copy(
            out_ref.at[buffer, kind, at],
            pool_ref.at[place, :, columns(slot_h)],
            sems.at[n],
        )

    for n, job in enumerate(jobs):
        valid, copy = store(n, job, jnp.maximum(h - 1, 0), 1 - buffer)
        pl.when(valid & (h > 0))(copy.wait)
    for n, job in enumerate(jobs):
        valid, copy = store(n, job, h, buffer)
        pl.when(valid)(copy.start)

    @pl.when(h == steps - 1)
    def _():
        for n, job in enumerate(jobs):
            valid, copy = store(n, job, h, buffer)
            pl.when(valid)(copy.wait)


def attention(queries, pool, gain, grad_normed, tab, lay):
    rows, columns = queries.shape
    blocks = lay.blocks
    heads = columns // HDIM
    group = 2 if heads % 2 == 0 else 1
    width = group * HDIM
    row_spec = pl.BlockSpec((rows, width), lambda h, tab: (0, h))
    gain_spec = pl.BlockSpec((1, width), lambda h, tab: (0, h))
    probs_spec = pl.BlockSpec((blocks, group, 3 * BLOCK, BLOCK), lambda h, tab: (0, h, 0, 0))
    sums_spec = pl.BlockSpec((8, rows), lambda h, tab: (0, 0))

    def pick_specs(own, picks):
        specs = [pl.BlockSpec((blocks, BLOCK, width), own)]
        for j in range(blocks + 1):
            specs.append(
                pl.BlockSpec((1, BLOCK, width), lambda h, tab, j=j: (tab[picks + j], 0, h))
            )
        return specs

    pool_specs = pick_specs(lambda h, tab: (tab[lay.device] >> 1, 0, h), lay.key_picks)
    pool_specs += pick_specs(lambda h, tab: (lay.value_own // blocks, 0, h), lay.value_picks)
    common = [row_spec] + pool_specs + [gain_spec, row_spec]
    operands = (queries,) + (pool,) * len(pool_specs) + (gain, grad_normed)

    attended, probs, sums = pl.pallas_call(
        functools.partial(forward_kernel, lay=lay, group=group),
        out_shape=(
            jax.ShapeDtypeStruct((rows, columns), jnp.float32),
            jax.ShapeDtypeStruct((blocks, heads, 3 * BLOCK, BLOCK), jnp.bfloat16),
            jax.ShapeDtypeStruct((8, rows), jnp.float32),
        ),
        grid_spec=pltpu.PrefetchScalarGridSpec(
            num_scalar_prefetch=1,
            grid=(heads // group,),
            in_specs=common,
            out_specs=(row_spec, probs_spec, sums_spec),
            scratch_shapes=[pltpu.VMEM((blocks, BLOCK, LANES), jnp.float32)],
        ),
        compiler_params=BIG,
        cost_estimate=pl.CostEstimate(
            flops=4 * rows * 3 * BLOCK * columns,
            bytes_accessed=50_000_000,
            transcendentals=rows * 3 * BLOCK * heads,
        ),
        name="attention_forward",
    )(tab, *operands)

    heads_size = lax.axis_size("head")
    sums = [sums] + [
        lax.ppermute(sums, "head", [(d, (d + k) % heads_size) for d in range(heads_size)])
        for k in range(1, heads_size)
    ]

    wide = jax.ShapeDtypeStruct((rows, columns), jnp.bfloat16)
    terms = (2, 2 * blocks + 1, BLOCK, width)
    normed, grad_q, pool = pl.pallas_call(
        functools.partial(backward_kernel, lay=lay, group=group),
        out_shape=(wide, wide, jax.ShapeDtypeStruct(pool.shape, pool.dtype)),
        grid_spec=pltpu.PrefetchScalarGridSpec(
            num_scalar_prefetch=1,
            grid=(heads // group,),
            in_specs=[row_spec, ANY, gain_spec, row_spec, row_spec, probs_spec]
            + [sums_spec] * len(sums),
            out_specs=(row_spec, row_spec, ANY),
            scratch_shapes=[
                pltpu.VMEM((blocks, BLOCK, LANES), jnp.float32),
                pltpu.VMEM((2, 2, group, BLOCK, HDIM), jnp.float32),
                pltpu.VMEM((2,) + terms, jnp.bfloat16),
                pltpu.VMEM((2,) + terms, jnp.bfloat16),
                pltpu.SemaphoreType.DMA((2 * terms[1],)),
                pltpu.SemaphoreType.DMA((2, 2 * terms[1])),
            ],
        ),
        input_output_aliases={2: 2},
        compiler_params=BIG,
        cost_estimate=pl.CostEstimate(
            flops=8 * rows * 3 * BLOCK * columns,
            bytes_accessed=70_000_000,
            transcendentals=0,
        ),
        name="attention_backward",
    )(tab, queries, pool, gain, grad_normed, attended, probs, *sums)
    return normed, grad_q, pool


def on_device(queries, key_rows, value_rows, norm_gain, sort_index, grad_normed):
    rows, columns = queries.shape
    blocks = rows // BLOCK
    lay = Layout(lax.axis_size("ctx"), blocks)
    tab, gain = routing_table(sort_index, norm_gain, lay)

    shape3 = (blocks, BLOCK, columns)
    own = (key_rows.reshape(shape3), value_rows.reshape(shape3))
    total = tab[lay.total]
    pool = gather_blocks(*own, tab, total, lay)

    normed, grad_q, pool = attention(queries, pool, gain, grad_normed, tab, lay)
    grad_k, grad_v = return_blocks(pool, tab, total, lay)
    return normed, grad_q, grad_k.reshape(rows, columns), grad_v.reshape(rows, columns)


def solution(mesh):
    in_specs = (
        P("ctx", "head"),
        P("ctx", "head"),
        P("ctx", "head"),
        P("head"),
        P(),
        P("ctx", "head"),
    )
    out_specs = (P("ctx", "head"), P("ctx", "head"), P("ctx", "head"), P("ctx", "head"))
    return jax.shard_map(
        on_device, mesh=mesh, in_specs=in_specs, out_specs=out_specs, check_vma=False
    )
```

```python
import functools
import math

import jax
import jax.numpy as jnp
import numpy as np
from jax import lax
from jax.experimental import pallas as pl
from jax.experimental.pallas import tpu as pltpu
from jax.sharding import PartitionSpec as P

HDIM = 128
BLOCK = 256
WIDTH = 5120
LANES = 128
ROW = 16
LEAD = 2
FIRST = 1024
STATIC_SLOTS = 9
SCALE = HDIM ** (-0.5)
SCALE_LOG2 = SCALE * math.log2(math.e)
ANY = pl.BlockSpec(memory_space=pl.ANY)
SMEM = pl.BlockSpec(memory_space=pltpu.SMEM)
VMEM = pl.BlockSpec(memory_space=pltpu.VMEM)
BIG = pltpu.CompilerParams(vmem_limit_bytes=56 * 1024 * 1024)
MOVE = pltpu.CompilerParams(vmem_limit_bytes=40 * 1024 * 1024)


class Layout:
    def __init__(self, ctx_size, blocks):
        self.ctx_size = ctx_size
        self.blocks = blocks
        self.levels = ctx_size // 2
        line = self.levels * blocks
        self.value_line = line
        self.value_own = 2 * line
        self.over = 2 * line + blocks
        self.places = self.over + 2 * (blocks + 1)
        self.slots = 2 * (2 * line + 2 * self.levels + 2 * blocks + 4)
        self.rows = self.slots + 2 * LEAD
        self.info = self.rows * ROW
        self.key_picks = self.info
        self.value_picks = self.info + blocks + 1
        self.total = self.info + 2 * blocks + 2
        self.device = self.info + 2 * blocks + 3


def shift_rows(array, count, rows):
    n = array.shape[0]
    if abs(count) >= n:
        return jnp.zeros_like(array)
    rolled = pltpu.roll(array, (-count) % n, 0)
    inside = (rows < n - count) if count > 0 else (rows >= -count)
    return jnp.where(inside, rolled, 0.0)


def table_kernel(picks_ref, gain_ref, out_ref, gain_row_ref, *, lay):
    n = lay.ctx_size
    blocks = lay.blocks
    count = n * blocks
    width = -(-2 * count // LANES) * LANES
    rows = lax.broadcasted_iota(jnp.int32, (n, width), 0)
    lanes = lax.broadcasted_iota(jnp.int32, (n, width), 1)
    out_lanes = lax.broadcasted_iota(jnp.int32, (n, LANES), 1)
    values = lanes >= count
    block = jnp.where(lanes >= 2 * count, -2, jnp.where(values, lanes - count, lanes))
    owner = jnp.floor((block.astype(jnp.float32) + 0.5) / blocks).astype(jnp.int32)
    within = block - owner * blocks
    line = (owner >> 1) * blocks + within
    place = jnp.where(values, jnp.where(owner == rows, lay.value_own + within, lay.value_line + line), line)
    place = jnp.where(block < 0, 0, place).astype(jnp.float32)
    picks = picks_ref[...]
    side = rows & 1
    level = rows >> 1
    same_side = side == (owner & 1)
    travels = jnp.logical_xor(same_side, values)
    owned = owner == rows

    def other(array):
        return jnp.where(side == 0, pltpu.roll(array, n - 1, 0), pltpu.roll(array, 1, 0))

    need = jnp.zeros((n, width), jnp.float32)
    for j in range(blocks + 1):
        need = jnp.where(picks[:, j : j + 1] == block, 1.0, need)
    need = jnp.where(owned, 0.0, need)
    across = other(need)
    wanted = jnp.maximum(need, across)
    final = jnp.where(travels, across, 0.0)
    hops = jnp.where(wanted > 0, 1.0 + final, 0.0)
    up_hops = jnp.zeros_like(need)
    down_hops = jnp.zeros_like(need)
    for k in range(1, lay.levels):
        above = shift_rows(hops, 2 * k, rows)
        below = shift_rows(hops, -2 * k, rows)
        up_hops = jnp.maximum(up_hops, jnp.where(above > 0, above + (k - 1), 0.0))
        down_hops = jnp.maximum(down_hops, jnp.where(below > 0, below + (k - 1), 0.0))
    up = jnp.where(travels & (level >= (owner >> 1)) & (up_hops > 0), 1.0, 0.0)
    down = jnp.where(travels & (level <= (owner >> 1)) & (down_hops > 0), 1.0, 0.0)
    source = owned & jnp.logical_not(travels)
    most = jnp.maximum(up_hops, down_hops)
    over = jnp.where(source & ((most > 0) | (across > 0)), 1.0, final)
    spread = jnp.minimum(jnp.sum(need, axis=0, keepdims=True), 3.0)
    low = (width - 1 - lanes).astype(jnp.float32)
    up_rank = (up_hops * 4.0 + spread) * width + low
    down_rank = (down_hops * 4.0 + spread) * width + low
    over_rank = jnp.where(source, most * 4.0 + spread, 2.0) * width + low
    first_over = float(lay.over)

    gain_row_ref[0, :] = gain_ref[:]
    out_ref[...] = jnp.full(out_ref.shape, -1, jnp.int32)

    def pick(pending, have, rank):
        score = jnp.where(pending * have > 0, rank, -1.0)
        best = jnp.max(score, axis=1, keepdims=True)
        return jnp.where((score == best) & (best >= 0), 1.0, 0.0)

    def where(chosen):
        return jnp.sum(chosen * (place + 1.0), axis=1, keepdims=True) - 1.0

    def pending(state):
        t, have, fresh, up, down, over, over_place, count = state
        return (t < lay.slots) & (jnp.sum(up + down + over) > 0)

    def step(state):
        t, have, fresh, up, down, over, over_place, count = state
        send_up = pick(up, have, up_rank)
        send_down = pick(down, have, down_rank)
        send_over = pick(over, have, over_rank)
        up = up - send_up
        down = down - send_down
        over = over - send_over
        got_up = shift_rows(send_up, -2, rows)
        got_down = shift_rows(send_down, 2, rows)
        got_over = other(send_over)
        got_final = jnp.where(travels, 0.0, got_over)
        any_final = jnp.max(got_final, axis=1, keepdims=True)
        over_at = jnp.where(any_final > 0, count + first_over, where(got_over))
        last = jnp.where((up + down + over + need > 0) | owned, 0.0, float(FIRST))

        def first_back(chosen):
            return jnp.max(chosen * last, axis=1, keepdims=True)

        columns = (
            where(send_up) + first_back(send_up),
            where(send_down) + first_back(send_down * (1.0 - send_up)),
            where(send_over) + first_back(send_over * (1.0 - send_up) * (1.0 - send_down)),
            where(got_up),
            where(got_down),
            over_at,
        )
        row = jnp.full((n, LANES), -1.0, jnp.float32)
        for k, column in enumerate(columns):
            row = jnp.where(out_lanes == k, column, row)
        out_ref[t + LEAD] = row.astype(jnp.int32)
        over_place = jnp.where(got_final > 0, count + first_over, over_place)
        have = jnp.maximum(have, fresh)
        fresh = jnp.maximum(got_up, jnp.maximum(got_down, got_over))
        return (t + 1, have, fresh, up, down, over, over_place, count + any_final)

    zeros = jnp.zeros_like(need)
    have = jnp.where(owned, 1.0, 0.0)
    state = (jnp.int32(0), have, zeros, up, down, over, zeros, jnp.zeros((n, 1), jnp.float32))
    state = lax.while_loop(pending, step, state)
    at = jnp.where(travels | owned, place, state[6])
    own_row = lax.broadcasted_iota(jnp.int32, (n, LANES), 0)
    row = jnp.zeros((n, LANES), jnp.float32)
    for kind in range(2):
        base = (own_row >> 1) * blocks if kind == 0 else jnp.full((n, LANES), lay.value_own)
        for j in range(blocks + 1):
            chosen = (picks[:, j : j + 1] == block) & (values if kind else jnp.logical_not(values))
            found = jnp.sum(jnp.where(chosen, at, 0.0), axis=1, keepdims=True)
            found = jnp.where(picks[:, j : j + 1] < 0, base[:, :1].astype(jnp.float32), found)
            row = jnp.where(out_lanes == kind * (blocks + 1) + j, found, row)
    row = jnp.where(out_lanes == 2 * blocks + 2, state[0].astype(jnp.float32), row)
    row = jnp.where(out_lanes == 2 * blocks + 3, own_row.astype(jnp.float32), row)
    out_ref[lay.rows] = row.astype(jnp.int32)


def routing_table(sort_index, norm_gain, lay):
    n, blocks = lay.ctx_size, lay.blocks
    before = (np.arange(n, dtype=np.int32) * blocks - 1)[:, None]
    picks = jnp.concatenate([sort_index.reshape(n, blocks), jnp.asarray(before)], axis=1)
    picks = jnp.pad(picks, ((0, 0), (0, LANES - blocks - 1)), constant_values=-1)
    table, gain = pl.pallas_call(
        functools.partial(table_kernel, lay=lay),
        out_shape=(
            jax.ShapeDtypeStruct((lay.rows + 1, n, LANES), jnp.int32),
            jax.ShapeDtypeStruct((1,) + norm_gain.shape, norm_gain.dtype),
        ),
        in_specs=[VMEM, VMEM],
        out_specs=(VMEM, VMEM),
        name="routing_table",
    )(picks, norm_gain)
    mine = lax.dynamic_slice(table, (0, lax.axis_index("ctx"), 0), (lay.rows + 1, 1, ROW))
    return mine.reshape((lay.rows + 1) * ROW), gain


def routes(ctx_size):
    up = [(d, d + 2) for d in range(ctx_size - 2)]
    down = [(d + 2, d) for d in range(ctx_size - 2)]
    over = [(d, d ^ 1) for d in range(ctx_size)]
    return up, down, over


def copies(jobs, sems):
    started = []
    for k, (valid, source, target) in enumerate(jobs):
        copy = pltpu.make_async_copy(source, target, sems.at[k])
        pl.when(valid)(copy.start)
        started.append((valid, copy))
    for valid, copy in started:
        pl.when(valid)(copy.wait)


def entry(tab_ref, t, k):
    return tab_ref[(t + LEAD) * ROW + k]


def place_of(code):
    return jnp.maximum(code, 0) & (FIRST - 1)


def fill_kernel(tab_ref, key_ref, value_ref, pool_ref, mark_ref, held_ref, sems, *, lay):
    mark_ref[...] = jnp.zeros_like(mark_ref)
    blocks = lay.blocks
    level = tab_ref[lay.device] >> 1
    loads = [
        pltpu.make_async_copy(key_ref, held_ref.at[pl.ds(0, blocks)], sems.at[0]),
        pltpu.make_async_copy(value_ref, held_ref.at[pl.ds(blocks, blocks)], sems.at[1]),
    ]
    stores = [
        pltpu.make_async_copy(
            held_ref.at[pl.ds(0, blocks)], pool_ref.at[pl.ds(level * blocks, blocks)], sems.at[2]
        ),
        pltpu.make_async_copy(
            held_ref.at[pl.ds(blocks, blocks)],
            pool_ref.at[pl.ds(lay.value_own, blocks)],
            sems.at[3],
        ),
    ]
    for load in loads:
        load.start()
    for load, store in zip(loads, stores):
        load.wait()
        store.start()
    for store in stores:
        store.wait()


def first_kernel(tab_ref, key_ref, value_ref, *refs, lay, slot):
    up_ref, down_ref, over_ref, held_ref, sems = refs[-5:]
    blocks = lay.blocks
    level = tab_ref[lay.device] >> 1
    loads, stores = [], []
    for k, out in enumerate((up_ref, down_ref, over_ref)):
        code = entry(tab_ref, slot, k)
        at = place_of(code)
        is_value = at >= lay.value_own
        key_at = jnp.clip(at - level * blocks, 0, blocks - 1)
        value_at = jnp.clip(at - lay.value_own, 0, blocks - 1)
        valid = code >= 0
        loads.append((valid & jnp.logical_not(is_value), key_ref.at[key_at], held_ref.at[k]))
        loads.append((valid & is_value, value_ref.at[value_at], held_ref.at[k]))
        stores.append((valid, held_ref.at[k], out))
    copies(loads, sems)
    copies(stores, sems)


def slot_and_rest(slot, refs):
    return (refs[0][0], refs[1:]) if slot is None else (slot, refs)


def match(place, valid, places, valids):
    hits = [valid & v & (place == p) for p, v in zip(places, valids)]
    found = hits[0] | hits[1] | hits[2]
    return found, jnp.where(hits[0], 0, jnp.where(hits[1], 1, 2))


def step_kernel(*refs, slot):
    t, refs = slot_and_rest(slot, refs)
    (
        tab_ref, _, in_up, in_down, in_over, pool_ref, up_ref, down_ref, over_ref, held_ref, sems,
    ) = refs
    got_codes = [entry(tab_ref, t - 2, 3 + k) for k in range(3)]
    got_valid = [c >= 0 for c in got_codes]
    got_places = [place_of(c) for c in got_codes]
    loads = [
        (v, got, held_ref.at[k])
        for k, (v, got) in enumerate(zip(got_valid, (in_up, in_down, in_over)))
    ]
    stores = [
        (v, held_ref.at[k], pool_ref.at[p])
        for k, (v, p) in enumerate(zip(got_valid, got_places))
    ]
    for k, out in enumerate((up_ref, down_ref, over_ref)):
        code = entry(tab_ref, t, k)
        valid = code >= 0
        place = place_of(code)
        found, at = match(place, valid, got_places, got_valid)
        loads.append((valid & jnp.logical_not(found), pool_ref.at[place], held_ref.at[3 + k]))
        stores.append((valid, held_ref.at[jnp.where(found, at, 3 + k)], out))
    copies(loads, sems)
    copies(stores, sems)


def close_kernel(*refs, slot):
    t, refs = slot_and_rest(slot, refs)
    tab_ref, _, in_up, in_down, in_over, pool_ref, held_ref, sems = refs
    loads, stores = [], []
    for k, got in enumerate((in_up, in_down, in_over)):
        code = entry(tab_ref, t, 3 + k)
        loads.append((code >= 0, got, held_ref.at[k]))
        stores.append((code >= 0, held_ref.at[k], pool_ref.at[place_of(code)]))
    copies(loads, sems)
    copies(stores, sems)


def take_kernel(*refs, slot, first):
    t, refs = slot_and_rest(slot, refs)
    tab_ref, pool_ref, up_ref, down_ref, over_ref, held_ref, sems = refs
    loads, stores = [], []
    for k, out in enumerate((up_ref, down_ref, over_ref)):
        code = entry(tab_ref, t, first + k)
        loads.append((code >= 0, pool_ref.at[place_of(code)], held_ref.at[k]))
        stores.append((code >= 0, held_ref.at[k], out))
    copies(loads, sems)
    copies(stores, sems)


def traffic(byte_count):
    return pl.CostEstimate(flops=0, bytes_accessed=byte_count, transcendentals=0)


def take(t, tab, pool, first):
    one = jax.ShapeDtypeStruct(pool.shape[1:], pool.dtype)
    call = dict(
        out_shape=(one,) * 3,
        in_specs=[SMEM, ANY],
        out_specs=(ANY,) * 3,
        scratch_shapes=[pltpu.VMEM((3,) + one.shape, one.dtype), pltpu.SemaphoreType.DMA((3,))],
        cost_estimate=traffic(12 * math.prod(one.shape)),
        name="take_step",
        in_place=False,
    )
    return numbered(functools.partial(take_kernel, first=first), t, call)(tab, pool)


def send_all(sends, perms):
    return tuple(lax.ppermute(s, "ctx", p) for s, p in zip(sends, perms))


def numbered(kernel, t, call):
    known = isinstance(t, int)
    extra = [] if known else [t.reshape(1)]
    specs = [] if known else [SMEM]
    return functools.partial(
        pl.pallas_call(
            functools.partial(kernel, slot=t if known else None),
            in_specs=specs + call.pop("in_specs"),
            input_output_aliases={1 + len(extra): 0} if call.pop("in_place", True) else {},
            compiler_params=MOVE,
            **call,
        ),
        *extra,
    )


def gather_blocks(keys, values, tab, total, lay):
    one = jax.ShapeDtypeStruct(keys.shape[1:], keys.dtype)
    pool_shape = jax.ShapeDtypeStruct((lay.places,) + one.shape, one.dtype)
    size = 2 * math.prod(one.shape)
    perms = routes(lay.ctx_size)
    six = [pltpu.VMEM((6,) + one.shape, one.dtype), pltpu.SemaphoreType.DMA((6,))]

    def first(slot, behind):
        sends = pl.pallas_call(
            functools.partial(first_kernel, lay=lay, slot=slot),
            out_shape=(one,) * 3,
            in_specs=[SMEM, ANY, ANY] + [ANY] * len(behind),
            out_specs=(ANY,) * 3,
            scratch_shapes=six,
            compiler_params=MOVE,
            cost_estimate=traffic(size * 6),
            name="gather_first",
        )(tab, keys, values, *behind)
        return send_all(sends, perms)

    older = first(0, [])
    pool, mark = pl.pallas_call(
        functools.partial(fill_kernel, lay=lay),
        out_shape=(pool_shape, jax.ShapeDtypeStruct((8, LANES), jnp.float32)),
        in_specs=[SMEM, ANY, ANY],
        out_specs=(ANY, VMEM),
        scratch_shapes=[
            pltpu.VMEM((2 * lay.blocks,) + one.shape, one.dtype),
            pltpu.SemaphoreType.DMA((4,)),
        ],
        compiler_params=MOVE,
        cost_estimate=traffic(size * 4 * lay.blocks),
        name="gather_fill",
    )(tab, keys, values)
    newer = first(1, [mark])

    def step(t, pool, got):
        call = dict(
            out_shape=(pool_shape, one, one, one),
            in_specs=[SMEM] + [ANY] * 4,
            out_specs=(ANY,) * 4,
            scratch_shapes=six,
            cost_estimate=traffic(size * 12),
            name="gather_step",
        )
        pool, *sends = numbered(step_kernel, t, call)(tab, pool, *got)
        return pool, send_all(sends, perms)

    for t in range(2, STATIC_SLOTS):
        pool, latest = step(t, pool, older)
        older, newer = newer, latest

    def close(t, pool, got):
        call = dict(
            out_shape=pool_shape,
            in_specs=[SMEM] + [ANY] * 4,
            out_specs=ANY,
            scratch_shapes=six,
            cost_estimate=traffic(size * 6),
            name="gather_close",
        )
        return numbered(close_kernel, t, call)(tab, pool, *got)

    pool = close(STATIC_SLOTS - 2, pool, older)
    pool = close(STATIC_SLOTS - 1, pool, newer)

    def body(state):
        t, end, pool = state
        got = send_all(take(t, tab, pool, 0), perms)
        return t + 1, end, close(t, pool, got)

    return lax.while_loop(
        lambda state: state[0] < state[1], body, (jnp.int32(STATIC_SLOTS), total, pool)
    )[2]


def add(target_ref, to, source_ref, at):
    target_ref[to] = (
        target_ref[to].astype(jnp.float32) + source_ref[at].astype(jnp.float32)
    ).astype(target_ref.dtype)


def same_blocks(places, valid):
    same_10 = valid[1] & valid[0] & (places[1] == places[0])
    same_20 = valid[2] & valid[0] & (places[2] == places[0])
    same_21 = valid[2] & valid[1] & (places[2] == places[1]) & jnp.logical_not(same_20)
    alone = [
        valid[0],
        valid[1] & jnp.logical_not(same_10),
        valid[2] & jnp.logical_not(same_20 | same_21),
    ]
    return alone, ((1, 0, same_10), (2, 0, same_20), (2, 1, same_21))


def add_doubles(doubles, held_ref, got_ref):
    for k, to, here in doubles:

        @pl.when(here)
        def _(k=k, to=to):
            add(held_ref, to, got_ref, k)


def back_kernel(*refs, slot):
    t, refs = slot_and_rest(slot, refs)
    tab_ref, _, in_up, in_down, in_over, pool_ref, up_ref, down_ref, over_ref = refs[:9]
    takes = [(entry(tab_ref, t, 3 + k), out) for k, out in enumerate((up_ref, down_ref, over_ref))]
    fold(tab_ref, t + 2, (in_up, in_down, in_over), takes, pool_ref, *refs[9:])


def add_kernel(*refs, slot):
    t, refs = slot_and_rest(slot, refs)
    tab_ref, _, in_up, in_down, in_over, pool_ref = refs[:6]
    fold(tab_ref, t, (in_up, in_down, in_over), [], pool_ref, *refs[6:])


def fold(tab_ref, t, arrived, takes, pool_ref, held_ref, got_ref, sems):
    codes = [entry(tab_ref, t, k) for k in range(3)]
    places = [place_of(c) for c in codes]
    valid = [c >= 0 for c in codes]
    fresh = [c >= FIRST for c in codes]
    alone, doubles = same_blocks(places, valid)
    loads = [(v, got, got_ref.at[k]) for k, (v, got) in enumerate(zip(valid, arrived))]
    loads += [
        (a & jnp.logical_not(f), pool_ref.at[p], held_ref.at[k])
        for k, (a, f, p) in enumerate(zip(alone, fresh, places))
    ]
    stores = []
    leaves = [False] * 3
    for k, (code, out) in enumerate(takes):
        leaving = code >= 0
        place = place_of(code)
        found, at = match(place, leaving, places, alone)
        loads.append((leaving & jnp.logical_not(found), pool_ref.at[place], held_ref.at[3 + k]))
        stores.append((leaving, held_ref.at[jnp.where(found, at, 3 + k)], out))
        leaves = [leave | (found & (at == n)) for n, leave in enumerate(leaves)]
    copies(loads, sems)
    for k in range(3):

        @pl.when(alone[k] & fresh[k])
        def _(k=k):
            held_ref[k] = got_ref[k]

        @pl.when(alone[k] & jnp.logical_not(fresh[k]))
        def _(k=k):
            add(held_ref, k, got_ref, k)

    add_doubles(doubles, held_ref, got_ref)
    stores += [
        (a & jnp.logical_not(leave), held_ref.at[k], pool_ref.at[p])
        for k, (a, leave, p) in enumerate(zip(alone, leaves, places))
    ]
    copies(stores, sems)


def own_index(place, tab_ref, lay):
    is_value = place >= lay.value_own
    base = jnp.where(is_value, lay.value_own, (tab_ref[lay.device] >> 1) * lay.blocks)
    return is_value, jnp.clip(place - base, 0, lay.blocks - 1)


def home_kernel(
    tab_ref, pool_ref, in_up, in_down, in_over, key_ref, value_ref, own_ref, got_ref, sems, *, lay
):
    blocks = lay.blocks
    level = tab_ref[lay.device] >> 1
    halves = (
        (pool_ref.at[pl.ds(level * blocks, blocks)], key_ref),
        (pool_ref.at[pl.ds(lay.value_own, blocks)], value_ref),
    )
    loads, stores = [], []
    for k, (source, target) in enumerate(halves):
        held = own_ref.at[pl.ds(k * blocks, blocks)]
        loads.append((level >= 0, source, held))
        stores.append((level >= 0, held, target))
    codes = [entry(tab_ref, 1, k) for k in range(3)]
    for k, (code, got) in enumerate(zip(codes, (in_up, in_down, in_over))):
        loads.append((code >= 0, got, got_ref.at[k]))
    copies(loads, sems)
    for k, code in enumerate(codes):
        is_value, at = own_index(place_of(code), tab_ref, lay)

        @pl.when(code >= 0)
        def _(k=k, at=jnp.where(is_value, blocks + at, at)):
            add(own_ref, at, got_ref, k)

    copies(stores, sems)


def last_kernel(
    tab_ref, key_in, value_in, in_up, in_down, in_over, key_ref, value_ref, held_ref, got_ref, sems,
    *, lay,
):
    del key_in, value_in
    codes = [entry(tab_ref, 0, k) for k in range(3)]
    places = [place_of(c) for c in codes]
    valid = [c >= 0 for c in codes]
    alone, doubles = same_blocks(places, valid)
    loads, stores = [], []
    for k, got in enumerate((in_up, in_down, in_over)):
        loads.append((valid[k], got, got_ref.at[k]))
        is_value, at = own_index(places[k], tab_ref, lay)
        for out, here in ((key_ref, jnp.logical_not(is_value)), (value_ref, is_value)):
            loads.append((alone[k] & here, out.at[at], held_ref.at[k]))
            stores.append((alone[k] & here, held_ref.at[k], out.at[at]))
    copies(loads, sems)
    for k in range(3):

        @pl.when(alone[k])
        def _(k=k):
            add(held_ref, k, got_ref, k)

    add_doubles(doubles, held_ref, got_ref)
    copies(stores, sems)


def return_blocks(pool, tab, total, lay):
    one = jax.ShapeDtypeStruct(pool.shape[1:], pool.dtype)
    pool_shape = jax.ShapeDtypeStruct(pool.shape, pool.dtype)
    own_shape = jax.ShapeDtypeStruct((lay.blocks,) + one.shape, one.dtype)
    size = 2 * math.prod(one.shape)
    up, down, over = routes(lay.ctx_size)
    perms = ([(b, a) for a, b in up], [(b, a) for a, b in down], over)

    scratch = [
        pltpu.VMEM((6,) + one.shape, one.dtype),
        pltpu.VMEM((3,) + one.shape, one.dtype),
        pltpu.SemaphoreType.DMA((9,)),
    ]

    def step(t, pool, got):
        call = dict(
            out_shape=(pool_shape, one, one, one),
            in_specs=[SMEM] + [ANY] * 4,
            out_specs=(ANY,) * 4,
            scratch_shapes=scratch,
            cost_estimate=traffic(size * 15),
            name="return_step",
        )
        pool, *sends = numbered(back_kernel, t, call)(tab, pool, *got)
        return pool, send_all(sends, perms)

    def body(state):
        t, pool = state
        got = send_all(take(t, tab, pool, 3), perms)
        call = dict(
            out_shape=pool_shape,
            in_specs=[SMEM] + [ANY] * 4,
            out_specs=ANY,
            scratch_shapes=scratch,
            cost_estimate=traffic(size * 9),
            name="return_add",
        )
        return t - 1, numbered(add_kernel, t, call)(tab, pool, *got)

    _, pool = lax.while_loop(lambda state: state[0] >= STATIC_SLOTS, body, (total - 1, pool))
    older = send_all(take(STATIC_SLOTS - 1, tab, pool, 3), perms)
    newer = send_all(take(STATIC_SLOTS - 2, tab, pool, 3), perms)
    for t in range(STATIC_SLOTS - 3, -1, -1):
        pool, latest = step(t, pool, older)
        older, newer = newer, latest
    three = [pltpu.VMEM((3,) + one.shape, one.dtype)]
    sums = pl.pallas_call(
        functools.partial(home_kernel, lay=lay),
        out_shape=(own_shape, own_shape),
        in_specs=[SMEM] + [ANY] * 4,
        out_specs=(ANY, ANY),
        scratch_shapes=[pltpu.VMEM((2 * lay.blocks,) + one.shape, one.dtype)]
        + three
        + [pltpu.SemaphoreType.DMA((5,))],
        compiler_params=MOVE,
        cost_estimate=traffic(size * 24),
        name="return_home",
    )(tab, pool, *older)
    return pl.pallas_call(
        functools.partial(last_kernel, lay=lay),
        out_shape=(own_shape, own_shape),
        in_specs=[SMEM] + [ANY] * 5,
        out_specs=(ANY, ANY),
        scratch_shapes=three * 2 + [pltpu.SemaphoreType.DMA((9,))],
        input_output_aliases={1: 0, 2: 1},
        compiler_params=MOVE,
        cost_estimate=traffic(size * 9),
        name="return_last",
    )(tab, *sums, *newer)


QK = (((1,), (1,)), ((), ()))
AB = (((1,), (0,)), ((), ()))
TA = (((0,), (0,)), ((), ()))


def dot(a, b, dims):
    return lax.dot_general(a, b, dims, preferred_element_type=jnp.float32)


def rows_of(i):
    return slice(i * BLOCK, (i + 1) * BLOCK)


def parts_of(i, cols, own_ref, pick_refs):
    blocks = len(pick_refs) - 1
    before = pick_refs[blocks][0, :, cols] if i == 0 else own_ref[i - 1, :, cols]
    return own_ref[i, :, cols], before, pick_refs[i][0, :, cols]


def term_places(tab_ref, lay):
    level = tab_ref[lay.device] >> 1
    result = []
    for base, picks in ((level * lay.blocks, lay.key_picks), (lay.value_own, lay.value_picks)):
        places = [base + o for o in range(lay.blocks)]
        places += [tab_ref[picks + j] for j in range(lay.blocks + 1)]
        result.append(places)
    return result


def forward_kernel(tab_ref, *refs, lay, group):
    blocks = lay.blocks
    count = blocks + 2
    q_ref, key_refs, value_refs = refs[0], refs[1 : 1 + count], refs[1 + count : 1 + 2 * count]
    gain_ref, grad_ref, attended_ref, probs_ref, sums_ref, acc_ref = refs[1 + 2 * count :]
    h = pl.program_id(0)
    causal = lax.broadcasted_iota(jnp.int32, (BLOCK, BLOCK), 0) <= lax.broadcasted_iota(
        jnp.int32, (BLOCK, BLOCK), 1
    )
    hide = jnp.where(tab_ref[lay.device] > 0, 0.0, -jnp.inf).astype(jnp.float32)
    lane = lax.broadcasted_iota(jnp.int32, (BLOCK, LANES), 1)

    @pl.when(h == 0)
    def _():
        acc_ref[...] = jnp.zeros_like(acc_ref)

    def score(i, g):
        cols = slice(g * HDIM, (g + 1) * HDIM)
        q = q_ref[rows_of(i), cols]
        return [dot(k, q, QK) for k in parts_of(i, cols, key_refs[0], key_refs[1:])]

    tasks = [(i, g) for i in range(blocks) for g in range(group)]
    following = score(*tasks[0])
    for n, (i, g) in enumerate(tasks):
        scores = following
        if n + 1 < len(tasks):
            following = score(*tasks[n + 1])
        cols = slice(g * HDIM, (g + 1) * HDIM)
        scores[0] = jnp.where(causal, scores[0], -jnp.inf)
        if i == 0:
            scores[1] = scores[1] + hide
        top = jnp.max(
            jnp.maximum(jnp.maximum(scores[0], scores[1]), scores[2]), axis=0, keepdims=True
        )
        weights = [jnp.exp2((s - top) * SCALE_LOG2) for s in scores]
        scale = 1.0 / jnp.sum(weights[0] + weights[1] + weights[2], axis=0, keepdims=True)
        turned = 0.0
        values = parts_of(i, cols, value_refs[0], value_refs[1:])
        for j, (w, v) in enumerate(zip(weights, values)):
            low = (w * scale).astype(jnp.bfloat16)
            probs_ref[i, g, rows_of(j)] = low
            turned += dot(v, low, TA)
        attended = jnp.transpose(turned)
        attended_ref[rows_of(i), cols] = attended
        lifted = gain_ref[:, cols] * grad_ref[rows_of(i), cols].astype(jnp.float32)
        squares = jnp.sum(attended * attended, axis=1, keepdims=True)
        center = jnp.sum(lifted * attended, axis=1, keepdims=True)
        acc_ref[i] += jnp.where(lane == 0, squares, jnp.where(lane == 1, center, 0.0))

    @pl.when(h == pl.num_programs(0) - 1)
    def _():
        for i in range(blocks):
            sums_ref[:, rows_of(i)] = jnp.transpose(acc_ref[i])[:8]


def backward_kernel(
    tab_ref, q_ref, pool_in, gain_ref, grad_ref, attended_ref, probs_ref, *refs, lay, group
):
    del pool_in
    sums_refs, refs = refs[:-9], refs[-9:]
    normed_ref, gq_ref, pool_ref, rms_ref, acc_ref, out_ref, kv_ref, sems, load_sems = refs
    blocks = lay.blocks
    h = pl.program_id(0)
    steps = pl.num_programs(0)
    width = group * HDIM
    terms = 2 * blocks + 1
    places = term_places(tab_ref, lay)
    buffer = lax.rem(h, 2)

    def columns(at):
        return pl.ds(pl.multiple_of(at * width, width), width)

    def loads(at, buffer):
        return [
            pltpu.make_async_copy(
                pool_ref.at[places[kind][n], :, columns(at)],
                kv_ref.at[buffer, kind, n],
                load_sems.at[buffer, kind * terms + n],
            )
            for kind in range(2)
            for n in range(terms)
        ]

    @pl.when(h == 0)
    def _():
        for load in loads(0, 0):
            load.start()

    for load in loads(h, buffer):
        load.wait()

    @pl.when(h + 1 < steps)
    def _():
        for load in loads(h + 1, 1 - buffer):
            load.start()

    @pl.when(h == 0)
    def _():
        sums = sum(ref[...] for ref in sums_refs)
        squares = sums[0:1]
        center = sums[1:2]
        inv = lax.rsqrt(squares / WIDTH + 1e-05)
        factor = inv * inv * inv * center / WIDTH
        both = jnp.concatenate([inv, factor, jnp.zeros((6,) + inv.shape[1:], jnp.float32)], axis=0)
        for i in range(blocks):
            wide = jnp.concatenate([both[:, rows_of(i)]] * (LANES // 8), axis=0)
            rms_ref[i] = jnp.transpose(wide)

    def places_in(i):
        return (i, 2 * blocks if i == 0 else i - 1, blocks + i)

    def prepare(i, g):
        cols = slice(g * HDIM, (g + 1) * HDIM)
        inv_rms = rms_ref[i, :, 0:1]
        factor = rms_ref[i, :, 1:2]
        attended = attended_ref[rows_of(i), cols]
        gain = gain_ref[:, cols]
        normed_ref[rows_of(i), cols] = (attended * inv_rms * gain).astype(jnp.bfloat16)
        lifted = gain * grad_ref[rows_of(i), cols].astype(jnp.float32)
        grad = (inv_rms * lifted - attended * factor).astype(jnp.bfloat16)
        row = jnp.sum(jnp.transpose(grad.astype(jnp.float32) * attended), axis=0, keepdims=True)
        gps = [dot(kv_ref[buffer, 1, n, :, cols], grad, QK) for n in places_in(i)]
        return grad, row, gps

    tasks = [(i, g) for i in range(blocks) for g in range(group)]
    following = prepare(*tasks[0])
    for n, (i, g) in enumerate(tasks):
        grad, row, gps = following
        if n + 1 < len(tasks):
            following = prepare(*tasks[n + 1])
        cols = slice(g * HDIM, (g + 1) * HDIM)
        q = q_ref[rows_of(i), cols]
        gq = 0.0
        for j, at in enumerate(places_in(i)):
            low = probs_ref[i, g, rows_of(j)]
            gv = dot(low, grad, AB)
            gs = (low.astype(jnp.float32) * (gps[j] - row)).astype(jnp.bfloat16)
            gq += dot(kv_ref[buffer, 0, at, :, cols], gs, TA)
            gk = dot(gs, q, AB) * SCALE
            for kind, term in ((0, gk), (1, gv)):
                if j == 0 and i + 1 < blocks:
                    acc_ref[kind, i % 2, g] = term
                elif j == 1 and i > 0:
                    total = acc_ref[kind, at % 2, g] + term
                    out_ref[buffer, kind, at, :, cols] = total.astype(jnp.bfloat16)
                else:
                    out_ref[buffer, kind, at, :, cols] = term.astype(jnp.bfloat16)
        gq_ref[rows_of(i), cols] = (jnp.transpose(gq) * SCALE).astype(jnp.bfloat16)

    jobs = []
    for kind in range(2):
        writes = [steps > 0] * blocks
        for at in range(terms - 1, blocks - 1, -1):
            taken = False
            for to in list(range(blocks)) + list(range(at - 1, blocks - 1, -1)):
                here = (places[kind][at] == places[kind][to]) & jnp.logical_not(taken)
                taken = taken | here

                @pl.when(here)
                def _(kind=kind, at=at, to=to):
                    out_ref[buffer, kind, to] = (
                        out_ref[buffer, kind, to].astype(jnp.float32)
                        + out_ref[buffer, kind, at].astype(jnp.float32)
                    ).astype(jnp.bfloat16)

            writes.insert(blocks, jnp.logical_not(taken))
        for at in range(terms):
            jobs.append((kind, at, places[kind][at], writes[at]))

    def store(n, job, slot_h, buffer):
        kind, at, place, valid = job
        return valid, pltpu.make_async_copy(
            out_ref.at[buffer, kind, at],
            pool_ref.at[place, :, columns(slot_h)],
            sems.at[n],
        )

    for n, job in enumerate(jobs):
        valid, copy = store(n, job, jnp.maximum(h - 1, 0), 1 - buffer)
        pl.when(valid & (h > 0))(copy.wait)
    for n, job in enumerate(jobs):
        valid, copy = store(n, job, h, buffer)
        pl.when(valid)(copy.start)

    @pl.when(h == steps - 1)
    def _():
        for n, job in enumerate(jobs):
            valid, copy = store(n, job, h, buffer)
            pl.when(valid)(copy.wait)


def attention(queries, pool, gain, grad_normed, tab, lay):
    rows, columns = queries.shape
    blocks = lay.blocks
    heads = columns // HDIM
    group = 2 if heads % 2 == 0 else 1
    width = group * HDIM
    row_spec = pl.BlockSpec((rows, width), lambda h, tab: (0, h))
    gain_spec = pl.BlockSpec((1, width), lambda h, tab: (0, h))
    probs_spec = pl.BlockSpec((blocks, group, 3 * BLOCK, BLOCK), lambda h, tab: (0, h, 0, 0))
    sums_spec = pl.BlockSpec((8, rows), lambda h, tab: (0, 0))

    def pick_specs(own, picks):
        specs = [pl.BlockSpec((blocks, BLOCK, width), own)]
        for j in range(blocks + 1):
            specs.append(
                pl.BlockSpec((1, BLOCK, width), lambda h, tab, j=j: (tab[picks + j], 0, h))
            )
        return specs

    pool_specs = pick_specs(lambda h, tab: (tab[lay.device] >> 1, 0, h), lay.key_picks)
    pool_specs += pick_specs(lambda h, tab: (lay.value_own // blocks, 0, h), lay.value_picks)
    common = [row_spec] + pool_specs + [gain_spec, row_spec]
    operands = (queries,) + (pool,) * len(pool_specs) + (gain, grad_normed)

    attended, probs, sums = pl.pallas_call(
        functools.partial(forward_kernel, lay=lay, group=group),
        out_shape=(
            jax.ShapeDtypeStruct((rows, columns), jnp.float32),
            jax.ShapeDtypeStruct((blocks, heads, 3 * BLOCK, BLOCK), jnp.bfloat16),
            jax.ShapeDtypeStruct((8, rows), jnp.float32),
        ),
        grid_spec=pltpu.PrefetchScalarGridSpec(
            num_scalar_prefetch=1,
            grid=(heads // group,),
            in_specs=common,
            out_specs=(row_spec, probs_spec, sums_spec),
            scratch_shapes=[pltpu.VMEM((blocks, BLOCK, LANES), jnp.float32)],
        ),
        compiler_params=BIG,
        cost_estimate=pl.CostEstimate(
            flops=4 * rows * 3 * BLOCK * columns,
            bytes_accessed=50_000_000,
            transcendentals=rows * 3 * BLOCK * heads,
        ),
        name="attention_forward",
    )(tab, *operands)

    heads_size = lax.axis_size("head")
    sums = [sums] + [
        lax.ppermute(sums, "head", [(d, (d + k) % heads_size) for d in range(heads_size)])
        for k in range(1, heads_size)
    ]

    wide = jax.ShapeDtypeStruct((rows, columns), jnp.bfloat16)
    terms = (2, 2 * blocks + 1, BLOCK, width)
    normed, grad_q, pool = pl.pallas_call(
        functools.partial(backward_kernel, lay=lay, group=group),
        out_shape=(wide, wide, jax.ShapeDtypeStruct(pool.shape, pool.dtype)),
        grid_spec=pltpu.PrefetchScalarGridSpec(
            num_scalar_prefetch=1,
            grid=(heads // group,),
            in_specs=[row_spec, ANY, gain_spec, row_spec, row_spec, probs_spec]
            + [sums_spec] * len(sums),
            out_specs=(row_spec, row_spec, ANY),
            scratch_shapes=[
                pltpu.VMEM((blocks, BLOCK, LANES), jnp.float32),
                pltpu.VMEM((2, 2, group, BLOCK, HDIM), jnp.float32),
                pltpu.VMEM((2,) + terms, jnp.bfloat16),
                pltpu.VMEM((2,) + terms, jnp.bfloat16),
                pltpu.SemaphoreType.DMA((2 * terms[1],)),
                pltpu.SemaphoreType.DMA((2, 2 * terms[1])),
            ],
        ),
        input_output_aliases={2: 2},
        compiler_params=BIG,
        cost_estimate=pl.CostEstimate(
            flops=8 * rows * 3 * BLOCK * columns,
            bytes_accessed=70_000_000,
            transcendentals=0,
        ),
        name="attention_backward",
    )(tab, queries, pool, gain, grad_normed, attended, probs, *sums)
    return normed, grad_q, pool


def on_device(queries, key_rows, value_rows, norm_gain, sort_index, grad_normed):
    rows, columns = queries.shape
    blocks = rows // BLOCK
    lay = Layout(lax.axis_size("ctx"), blocks)
    tab, gain = routing_table(sort_index, norm_gain, lay)

    shape3 = (blocks, BLOCK, columns)
    own = (key_rows.reshape(shape3), value_rows.reshape(shape3))
    total = tab[lay.total]
    pool = gather_blocks(*own, tab, total, lay)

    normed, grad_q, pool = attention(queries, pool, gain, grad_normed, tab, lay)
    grad_k, grad_v = return_blocks(pool, tab, total, lay)
    return normed, grad_q, grad_k.reshape(rows, columns), grad_v.reshape(rows, columns)


def solution(mesh):
    in_specs = (
        P("ctx", "head"),
        P("ctx", "head"),
        P("ctx", "head"),
        P("head"),
        P(),
        P("ctx", "head"),
    )
    out_specs = (P("ctx", "head"), P("ctx", "head"), P("ctx", "head"), P("ctx", "head"))
    return jax.shard_map(
        on_device, mesh=mesh, in_specs=in_specs, out_specs=out_specs, check_vma=False
    )
```
